128 devices in a mesh: shard: 8 (over x_hi, z), replica: 16 (over x_lo, y, core).
Axes of the slice: x: 4 (x_hi: 2, x_lo: 2; x = x_hi * 2 + x_lo), y: 4, z: 4, core: 2. Of those that a mesh axis runs over, the one named last changes fastest.
Arguments:
- tokens: bfloat16 [16384, 1024], P(('replica', 'shard')), may hold values from -6 to 6
- cotangent: bfloat16 [16384, 1024], P(('replica', 'shard')), may hold values from -6 to 6
- lengths: int32 [16, 6], P('replica'), may hold values from 1 to 896, as said below
- gains: float32 [2304], replicated, may hold values from 0.5 to 1.5
- gain_first: float32 [2304], replicated, may hold values from -48 to 48
- gain_second: float32 [2304], replicated, may hold values from 16.384 to 65.536
- query_weight: float32 [1024, 2048], P(None, 'shard'), may hold values from -0.1875 to 0.1875
- key_weight: float32 [1024, 1024], P(None, 'shard'), may hold values from -0.1875 to 0.1875
- value_weight: float32 [1024, 1024], P(None, 'shard'), may hold values from -0.1875 to 0.1875
- output_weight: float32 [2048, 1024], P('shard'), may hold values from -2 to 2
- gate_weight: float32 [1024, 3072], P(None, 'shard'), may hold values from -0.1875 to 0.1875
- up_weight: float32 [1024, 3072], P(None, 'shard'), may hold values from -0.1875 to 0.1875
- down_weight: float32 [3072, 1024], P('shard'), may hold values from -0.109375 to 0.109375
- query_momentum: float32 [1024, 2048], P(None, 'shard'), may hold values from -224 to 224
- key_momentum: float32 [1024, 1024], P(None, 'shard'), may hold values from -224 to 224
- value_momentum: float32 [1024, 1024], P(None, 'shard'), may hold values from -224 to 224
- output_momentum: float32 [2048, 1024], P('shard'), may hold values from -224 to 224
- gate_momentum: float32 [1024, 3072], P(None, 'shard'), may hold values from -224 to 224
- up_momentum: float32 [1024, 3072], P(None, 'shard'), may hold values from -224 to 224
- down_momentum: float32 [3072, 1024], P('shard'), may hold values from -224 to 224
Outputs:
- output: bfloat16 [16384, 1024], P(('replica', 'shard'))
- input_grad: float32 [16384, 1024], P(('replica', 'shard'))
- new_gain_first: float32 [2304], replicated
- new_gain_second: float32 [2304], replicated
- new_gains: float32 [2304], replicated
- new_query_momentum: float32 [1024, 2048], P(None, 'shard')
- new_key_momentum: float32 [1024, 1024], P(None, 'shard')
- new_value_momentum: float32 [1024, 1024], P(None, 'shard')
- new_output_momentum: float32 [2048, 1024], P('shard')
- new_gate_momentum: float32 [1024, 3072], P(None, 'shard')
- new_up_momentum: float32 [1024, 3072], P(None, 'shard')
- new_down_momentum: float32 [3072, 1024], P('shard')
- new_query_weight: float32 [1024, 2048], P(None, ('shard', 'replica'))
- new_key_weight: float32 [1024, 1024], P(None, ('shard', 'replica'))
- new_value_weight: float32 [1024, 1024], P(None, ('shard', 'replica'))
- new_output_weight: float32 [2048, 1024], P(('shard', 'replica'))
- new_gate_weight: float32 [1024, 3072], P(None, ('shard', 'replica'))
- new_up_weight: float32 [1024, 3072], P(None, ('shard', 'replica'))
- new_down_weight: float32 [3072, 1024], P(('shard', 'replica'))
The draws below stay inside these ranges and needn't reach their ends.
Inputs may be any that keep to these rules, and one draw needn't show every extreme that they name: In every group the lengths sum to 1024; the first sequence has 1 to 64 tokens and the second, the longest, exactly 896.
All inputs are finite; a program needn't handle non-finite values.
Results may differ from the reference program's by a relative error of at most 0.028.
Values may be sent and summed in bfloat16 or wider, within the bound.
No kernel may reach another device: no remote copies, remote signals or barrier semaphores. Data moves between devices by JAX's collectives and lax.ppermute only.
A program may use at most 192 MiB of HBM per device.

```python
import math
from functools import partial
import jax
import jax.numpy as jnp
from jax import lax

D = 1024
H = 16
KV = 8
HD = 128
FF = 3072
TOK_DEV = 128
DOCS = 6
NS_ITERS = 5
STEP = 10
GROUP = 1024
GROUPS = 16
TOKENS = 16384


def draw_lengths(key, part):
    key = jax.random.fold_in(key, 11)
    first_key, weight_key = jax.random.split(key)
    leading = jax.random.randint(first_key, (GROUPS, 1), 1, TOK_DEV // 2 + 1).astype(jnp.int32)
    remain = TOK_DEV - leading
    spare = remain - (DOCS - 2)
    shares_raw = jax.random.randint(weight_key, (GROUPS, DOCS - 2), 1, 6).astype(jnp.int32)
    shares = spare * shares_raw // jnp.sum(shares_raw, axis=1, keepdims=True)
    tails = 1 + shares
    closing = remain - jnp.sum(tails[:, :-1], axis=1, keepdims=True)
    longest = jnp.full((GROUPS, 1), GROUP - TOK_DEV, jnp.int32)
    return jnp.concatenate([leading, longest, tails[:, :-1], closing], axis=1).astype(jnp.int32)


def block_scale(rng, dims, cuts, low, largest):
    factor_of, own = 1.0, jax.random.fold_in(rng, 6)
    for axis_at, blocks in cuts:
        draws = jnp.exp(jax.random.uniform(jax.random.fold_in(own, axis_at), (blocks,), jnp.float32, low / len(cuts), largest / len(cuts)))
        factor_of = factor_of * jnp.repeat(draws, dims[axis_at] // blocks).reshape([-1 if axis == axis_at else 1 for axis in range(len(dims))])
    return factor_of


def noise(rng, shape, deviation, bound, cuts=(), kind=jnp.bfloat16):
    values = deviation * jax.random.normal(rng, shape, jnp.float32)
    if cuts:
        values = values * block_scale(rng, shape, cuts, -0.22, 0.18)
    return jnp.clip(values, -bound, bound).astype(kind)


def setup_inputs(seed: int = 0) -> dict:
    streams_of = jax.random.split(jax.random.key(seed), 21)
    return {
        "tokens": noise(streams_of[0], (TOKENS, D), 1.0, 6.0, ((0, 128),)),
        "cotangent": noise(streams_of[1], (TOKENS, D), 1.0, 6.0, ((0, 128),)),
        "lengths": draw_lengths(jax.random.fold_in(streams_of[20], 71), 0),
        "gains": jnp.clip(1.0 + 0.1 * jax.random.normal(streams_of[3], (2 * D + 2 * HD,), jnp.float32), 0.5, 1.5),
        "gain_first": noise(streams_of[4], (2 * D + 2 * HD,), (0.06 * TOKENS ** 0.5), 48.0, (), jnp.float32),
        "gain_second": jnp.clip(jnp.exp(jax.random.uniform(streams_of[5], (2 * D + 2 * HD,), jnp.float32, math.log(16.384), math.log(65.536))), 16.384, 65.536),
        "query_weight": noise(streams_of[6], (D, H * HD), D ** -0.5, 0.1875, ((1, 8),), jnp.float32),
        "key_weight": noise(streams_of[7], (D, KV * HD), D ** -0.5, 0.1875, ((1, 8),), jnp.float32),
        "value_weight": noise(streams_of[8], (D, KV * HD), D ** -0.5, 0.1875, ((1, 8),), jnp.float32),
        "output_weight": noise(streams_of[9], (H * HD, D), (max(H * HD // 256, 4)) ** -0.5, 2.0, ((0, 8),), jnp.float32),
        "gate_weight": noise(streams_of[10], (D, FF), D ** -0.5, 0.1875, ((1, 8),), jnp.float32),
        "up_weight": noise(streams_of[11], (D, FF), D ** -0.5, 0.1875, ((1, 8),), jnp.float32),
        "down_weight": noise(streams_of[12], (FF, D), FF ** -0.5, 0.109375, ((0, 8),), jnp.float32),
        "query_momentum": noise(streams_of[13], (D, H * HD), (0.3 * TOKENS ** 0.5), 224.0, ((1, 8),), jnp.float32),
        "key_momentum": noise(streams_of[14], (D, KV * HD), (0.3 * TOKENS ** 0.5), 224.0, ((1, 8),), jnp.float32),
        "value_momentum": noise(streams_of[15], (D, KV * HD), (0.3 * TOKENS ** 0.5), 224.0, ((1, 8),), jnp.float32),
        "output_momentum": noise(streams_of[16], (H * HD, D), (0.3 * TOKENS ** 0.5), 224.0, ((0, 8),), jnp.float32),
        "gate_momentum": noise(streams_of[17], (D, FF), (0.3 * TOKENS ** 0.5), 224.0, ((1, 8),), jnp.float32),
        "up_momentum": noise(streams_of[18], (D, FF), (0.3 * TOKENS ** 0.5), 224.0, ((1, 8),), jnp.float32),
        "down_momentum": noise(streams_of[19], (FF, D), (0.3 * TOKENS ** 0.5), 224.0, ((0, 8),), jnp.float32),
    }


@jax.custom_vjp
def low(v):
    return lax.optimization_barrier(v.astype(jnp.bfloat16)).astype(jnp.float32)

@jax.custom_vjp
def low_back(v):
    return v

def low_keep(v):
    return (low(v), None)

def low_pass(kept, grad):
    return (grad,)

def back_keep(v):
    return (v, None)

def back_low(kept, grad):
    return (low(grad),)
low.defvjp(low_keep, low_pass)
low_back.defvjp(back_keep, back_low)
norm_epsilon = 1e-06
rotary_base = 1000000.0
momentum_decay = 0.95
poly_first = 3.4445
poly_second = -4.775
poly_third = 2.0315
orth_epsilon = 1e-07
update_rate = 0.5
weight_shrink = 0.002
adam_first = 0.9
adam_second = 0.999
adam_epsilon = 1e-08
gain_rate = 0.8
highest = lax.Precision.HIGHEST

def rms_scale(values):
    return lax.rsqrt(lax.optimization_barrier(jnp.mean(values * values, axis=-1, keepdims=True)) + norm_epsilon)

def rotary_tables(position, head_width):
    half_width = head_width // 2
    freq_steps = jnp.arange(half_width, dtype=jnp.float32)
    inverse = rotary_base ** (-2.0 * freq_steps / head_width)
    angles = position.astype(jnp.float32)[:, None] * inverse[None, :]
    return (jnp.cos(angles)[:, None, :], jnp.sin(angles)[:, None, :])

def rotate(values, cosine, sine_table):
    half_width = values.shape[-1] // 2
    front_half = values[..., :half_width]
    back_half = values[..., half_width:]
    return jnp.concatenate([front_half * cosine - back_half * sine_table, back_half * cosine + front_half * sine_table], axis=-1)

def stream_layout(lengths_row, stream_rows):
    ends_at = jnp.cumsum(lengths_row).astype(jnp.int32)
    places = jnp.arange(stream_rows, dtype=jnp.int32)
    passed = (places[:, None] >= ends_at[None, :]).astype(jnp.int32)
    segment = lax.optimization_barrier(jnp.sum(passed, axis=1)).astype(jnp.int32)
    position = places - lax.optimization_barrier(jnp.sum(passed * lengths_row[None, :], axis=1)).astype(jnp.int32)
    return (segment, position)

def weight_spreads():
    narrow = max(H * HD // 256, 4) ** (-0.5)
    wide = D ** (-0.5)
    return (wide, wide, wide, narrow, wide, wide, FF ** (-0.5))

def group_attention(items):
    queries, key_rows, value_rows, segment = items
    stream_rows = queries.shape[0]
    block_rows = min(512, stream_rows)
    order_all = jnp.arange(stream_rows, dtype=jnp.int32)

    def one_block(block_index):
        begin_row = block_index * block_rows
        query_block = lax.dynamic_slice_in_dim(queries, begin_row, block_rows)
        query_segment = lax.dynamic_slice_in_dim(segment, begin_row, block_rows)
        query_order = begin_row + jnp.arange(block_rows, dtype=jnp.int32)
        scores = low_back(jnp.einsum('qkgd,pkd->kgqp', query_block, key_rows, precision=highest) * HD ** (-0.5))
        allowed = (query_segment[:, None] == segment[None, :]) & (query_order[:, None] >= order_all[None, :])
        masked = jnp.where(allowed, scores, -1e+30)
        row_peak = lax.optimization_barrier(jnp.max(masked, axis=-1, keepdims=True))
        weights = jnp.where(allowed, jnp.exp(masked - row_peak), 0.0)
        probabilities = weights / lax.optimization_barrier(jnp.sum(weights, axis=-1, keepdims=True))
        return jnp.einsum('kgqp,pkd->qkgd', low(probabilities), value_rows, precision=highest)
    pieces = lax.map(jax.checkpoint(one_block), jnp.arange(stream_rows // block_rows, dtype=jnp.int32))
    return pieces.reshape(queries.shape)

def block_forward(inputs, gain_values, query_weight, key_weight, value_weight, output_weight, gate_weight, up_weight, down_weight, segment, position):
    row_count = inputs.shape[0]
    gain_attn = gain_values[:D]
    gain_mlp = gain_values[D:2 * D]
    gain_query = gain_values[2 * D:2 * D + HD]
    gain_key = gain_values[2 * D + HD:]
    normed = low(inputs * rms_scale(inputs) * gain_attn)
    query_pre = low_back(jnp.dot(normed, low(query_weight), precision=highest))
    key_pre = low_back(jnp.dot(normed, low(key_weight), precision=highest))
    value_use = low(low_back(jnp.dot(normed, low(value_weight), precision=highest)))
    cosine, sine_table = rotary_tables(position, HD)
    query_heads = query_pre.reshape(row_count, H, HD)
    query_use = low(rotate(query_heads * rms_scale(query_heads) * gain_query, cosine, sine_table))
    key_heads = key_pre.reshape(row_count, KV, HD)
    key_use = low(rotate(key_heads * rms_scale(key_heads) * gain_key, cosine, sine_table))
    group_count = row_count // GROUP
    attended = lax.map(jax.checkpoint(group_attention), (query_use.reshape(group_count, GROUP, KV, H // KV, HD), key_use.reshape(group_count, GROUP, KV, HD), value_use.reshape(group_count, GROUP, KV, HD), segment.reshape(group_count, GROUP)))
    attn_use = low_back(low(attended.reshape(row_count, H * HD)))
    middle = inputs + low_back(jnp.dot(attn_use, low(output_weight), precision=highest))
    normed_two = low(middle * rms_scale(middle) * gain_mlp)
    gate = low_back(jnp.dot(normed_two, low(gate_weight), precision=highest))
    upward = low_back(jnp.dot(normed_two, low(up_weight), precision=highest))
    hidden = low(gate * jax.nn.sigmoid(gate) * upward)
    return middle + low_back(jnp.dot(hidden, low(down_weight), precision=highest))

def orthogonalize(matrix):
    current = matrix * lax.rsqrt(jnp.sum(matrix * matrix) + orth_epsilon)
    for iteration in range(NS_ITERS):
        gram_matrix = jnp.dot(current, current.T, precision=highest)
        poly_matrix = poly_second * gram_matrix + poly_third * jnp.dot(gram_matrix, gram_matrix, precision=highest)
        current = poly_first * current + jnp.dot(poly_matrix, current, precision=highest)
    return current

def reference(tokens, cotangent, lengths, gains, gain_first, gain_second, query_weight, key_weight, value_weight, output_weight, gate_weight, up_weight, down_weight, query_momentum, key_momentum, value_momentum, output_momentum, gate_momentum, up_momentum, down_momentum):
    segment, position = jax.vmap(partial(stream_layout, stream_rows=GROUP))(lengths)
    segment = segment.reshape(-1)
    position = position.reshape(-1)
    weights = (query_weight, key_weight, value_weight, output_weight, gate_weight, up_weight, down_weight)
    moments = (query_momentum, key_momentum, value_momentum, output_momentum, gate_momentum, up_momentum, down_momentum)

    def forward(inputs, gain_values, first_w, second_w, third_w, fourth_w, fifth_w, sixth_w, seventh_w):
        return block_forward(inputs, gain_values, first_w, second_w, third_w, fourth_w, fifth_w, sixth_w, seventh_w, segment, position)
    result, pullback = jax.vjp(forward, tokens.astype(jnp.float32), gains, query_weight, key_weight, value_weight, output_weight, gate_weight, up_weight, down_weight)
    gradients = pullback(cotangent.astype(jnp.float32))
    input_grad = gradients[0]
    gain_grad = gradients[1]
    new_first = adam_first * gain_first + (1.0 - adam_first) * gain_grad
    new_second = adam_second * gain_second + (1.0 - adam_second) * gain_grad * gain_grad
    step_first = new_first / (1.0 - adam_first ** STEP)
    step_second = new_second / (1.0 - adam_second ** STEP)
    new_gains = gains - gain_rate * step_first / (jnp.sqrt(step_second) + adam_epsilon)
    spreads = weight_spreads()
    new_moments = []
    new_weights = []
    for matrix_index in range(7):
        moment = momentum_decay * moments[matrix_index] + gradients[2 + matrix_index]
        tall = matrix_index in (3, 6)
        oriented = moment.T if tall else moment
        update = orthogonalize(oriented)
        if tall:
            update = update.T
        step_rate = update_rate * spreads[matrix_index] * math.sqrt(max(moment.shape))
        new_moments.append(moment)
        new_weights.append(weights[matrix_index] * (1.0 - weight_shrink) - step_rate * update)
    mom_q, mom_k, mom_v, mom_o, mom_g, mom_u, mom_d = new_moments
    wei_q, wei_k, wei_v, wei_o, wei_g, wei_u, wei_d = new_weights
    return (result.astype(jnp.bfloat16), input_grad, new_first, new_second, new_gains, mom_q, mom_k, mom_v, mom_o, mom_g, mom_u, mom_d, wei_q, wei_k, wei_v, wei_o, wei_g, wei_u, wei_d)
```

```python
import math

import jax
import jax.numpy as jnp
from jax import lax
from jax.sharding import Mesh, PartitionSpec as P

D = 1024
H = 16
KV = 8
HD = 128
FF = 3072
NS_ITERS = 5
STEP = 10

norm_epsilon = 1e-06
rotary_base = 1000000.0
momentum_decay = 0.95
poly_first = 3.4445
poly_second = -4.775
poly_third = 2.0315
orth_epsilon = 1e-07
update_rate = 0.5
weight_shrink = 0.002
adam_first = 0.9
adam_second = 0.999
adam_epsilon = 1e-08
gain_rate = 0.8

f32 = jnp.float32
bf16 = jnp.bfloat16

PLANE = ("xl", "y", "xh")
TP = 8
REPLICAS = 16

SHARD_ROWS = (256, 128, 128, 256, 384, 384, 384)
PIECE_ROWS = tuple(n // REPLICAS for n in SHARD_ROWS)
WIDEST = 384
FULL_SHAPES = ((D, H * HD), (D, KV * HD), (D, KV * HD), (H * HD, D), (D, FF), (D, FF), (FF, D))
SPREADS = (
    D ** (-0.5),
    D ** (-0.5),
    D ** (-0.5),
    max(H * HD // 256, 4) ** (-0.5),
    D ** (-0.5),
    D ** (-0.5),
    FF ** (-0.5),
)
SPLIT_FIRST = (3, 6)


def trade(x, home):
    other = lax.ppermute(x, ("xh", "c"), [(1, 2), (2, 1)])
    return jnp.where(home, x, other)


def over_z(x, k):
    return lax.ppermute(x, "z", [(i, i ^ k) for i in range(4)])


def over_core(x):
    return lax.ppermute(x, "c", [(0, 1), (1, 0)])


def gather_rows(block, z, c):
    rows = block.shape[0]
    parts = [(z, block)] + [(z ^ k, over_z(block, k)) for k in (1, 3, 2)]
    whole = jnp.zeros((TP * rows,) + block.shape[1:], block.dtype)
    for place, part in parts:
        whole = lax.dynamic_update_slice_in_dim(whole, part, (c * 4 + place) * rows, 0)
        whole = lax.dynamic_update_slice_in_dim(whole, over_core(part), ((1 - c) * 4 + place) * rows, 0)
    return whole


def scatter_rows(product, z, c):
    away = product((1 - c) * 512, 512).astype(bf16)
    kept = product(c * 512, 512)
    half = kept + over_core(away).astype(f32)
    total = lax.dynamic_slice_in_dim(half, z * 128, 128, 0)
    sent = half.astype(bf16)
    for k in (1, 3, 2):
        total = total + over_z(lax.dynamic_slice_in_dim(sent, (z ^ k) * 128, 128, 0), k).astype(f32)
    return total


def rms_scale(values):
    return lax.rsqrt(jnp.mean(values * values, axis=-1, keepdims=True) + norm_epsilon)


def rotary_tables(position, head_width):
    half_width = head_width // 2
    freq_steps = jnp.arange(half_width, dtype=f32)
    inverse = rotary_base ** (-2.0 * freq_steps / head_width)
    angles = position.astype(f32)[:, None] * inverse[None, :]
    return (jnp.cos(angles)[:, None, :], jnp.sin(angles)[:, None, :])


def rotate(values, cosine, sine_table):
    half_width = values.shape[-1] // 2
    front_half = values[..., :half_width]
    back_half = values[..., half_width:]
    return jnp.concatenate(
        [
            front_half * cosine - back_half * sine_table,
            back_half * cosine + front_half * sine_table,
        ],
        axis=-1,
    )


def stream_layout(lengths_row, stream_rows):
    ends_at = jnp.cumsum(lengths_row)
    places = jnp.arange(stream_rows, dtype=jnp.int32)
    passed = (places[:, None] >= ends_at[None, :]).astype(jnp.int32)
    segment = jnp.sum(passed, axis=1)
    position = places - jnp.sum(passed * lengths_row[None, :], axis=1)
    return (segment, position)


def norm_back(upstream, values, scale, gain):
    weighted = upstream * gain
    inner = jnp.mean(weighted * values, axis=-1, keepdims=True)
    grad_values = scale * (weighted - values * scale * scale * inner)
    return (grad_values, upstream * values * scale)


def dot(a, b):
    return jnp.dot(a, b, preferred_element_type=f32)


def dot_t(a, b):
    return lax.dot_general(a, b, (((1,), (1,)), ((), ())), preferred_element_type=f32)


def t_dot(a, b):
    return lax.dot_general(a, b, (((0,), (0,)), ((), ())), preferred_element_type=f32)


def to_slot(rows, index):
    per = PIECE_ROWS[index]
    return jnp.pad(rows.reshape(REPLICAS, per, D), ((0, 0), (0, WIDEST // REPLICAS - per), (0, 0)))


def newton_schulz(gram, rows):
    total = jnp.trace(gram) + orth_epsilon
    inverse = lax.rsqrt(total)
    gram = gram * (inverse * inverse)
    rows = rows * inverse
    for iteration in range(NS_ITERS):
        gram_low = gram.astype(bf16)
        rest = poly_second * gram + poly_third * dot(gram_low, gram_low)
        rest_low = rest.astype(bf16)
        rows = poly_first * rows + dot(rows.astype(bf16), rest_low)
        if iteration + 1 < NS_ITERS:
            once = poly_first * gram + dot(rest_low, gram_low)
            gram = poly_first * once + dot(rest_low, once.astype(bf16))
    return rows


def shards(tokens, cotangent, lengths, gains, gain_first, gain_second, *matrices):
    weights, moments = matrices[:7], matrices[7:]
    xh, z, xl, y, c = (lax.axis_index(a) for a in ("xh", "z", "xl", "y", "c"))
    home = xh == c
    gain_attn = gains[:D]
    gain_mlp = gains[D : 2 * D]
    gain_query = gains[2 * D : 2 * D + HD]
    gain_key = gains[2 * D + HD :]

    inputs = trade(tokens, home).astype(f32)
    w_qkv = trade(jnp.concatenate([w.astype(bf16) for w in weights[:3]], axis=1), home)
    w_out = trade(weights[3].astype(bf16), home)
    w_gate = trade(weights[4].astype(bf16), home)
    w_up = trade(weights[5].astype(bf16), home)
    w_down = trade(weights[6].astype(bf16), home)
    cot_own = trade(cotangent, home)
    segment, position = stream_layout(trade(lengths, home)[0], TP * 128)

    scale_one = rms_scale(inputs)
    normed = gather_rows((inputs * scale_one * gain_attn).astype(bf16), z, c)
    cot = gather_rows(cot_own, z, c)
    pre = dot(normed, w_qkv)
    rows = pre.shape[0]
    cosine, sine_table = rotary_tables(position, HD)
    query_heads = pre[:, :256].reshape(rows, 2, HD)
    key_heads = pre[:, 256:384].reshape(rows, 1, HD)
    value_use = pre[:, 384:].astype(bf16)
    query_scale = rms_scale(query_heads)
    key_scale = rms_scale(key_heads)
    query_use = rotate(query_heads * query_scale * gain_query, cosine, sine_table).astype(bf16)
    key_use = rotate(key_heads * key_scale * gain_key, cosine, sine_table).astype(bf16)[:, 0]
    order = jnp.arange(rows, dtype=jnp.int32)
    allowed = (segment[:, None] == segment[None, :]) & (order[:, None] >= order[None, :])
    scores = jnp.einsum("qhd,pd->hqp", query_use, key_use, preferred_element_type=f32) * HD ** (-0.5)
    masked = jnp.where(allowed, scores, -1e30)
    peak = jnp.max(masked, axis=-1, keepdims=True)
    raised = jnp.where(allowed, jnp.exp(masked - peak), 0.0)
    probs = raised / jnp.sum(raised, axis=-1, keepdims=True)
    probs_use = probs.astype(bf16)
    attended = jnp.einsum("hqp,pd->qhd", probs_use, value_use, preferred_element_type=f32)
    attn_use = attended.reshape(rows, 2 * HD).astype(bf16)

    middle = inputs + scatter_rows(
        lambda at, n: dot(lax.dynamic_slice_in_dim(attn_use, at, n, 0), w_out), z, c
    )
    scale_two = rms_scale(middle)
    normed_two = gather_rows((middle * scale_two * gain_mlp).astype(bf16), z, c)
    gate = dot(normed_two, w_gate)
    upward = dot(normed_two, w_up)
    dhidden = dot_t(cot, w_down)
    sigmoid_gate = jax.nn.sigmoid(gate)
    activated = gate * sigmoid_gate
    hidden = (activated * upward).astype(bf16)
    dgate = (dhidden * upward * sigmoid_gate * (1.0 + gate * (1.0 - sigmoid_gate))).astype(bf16)
    dupward = (dhidden * activated).astype(bf16)
    dnormed_two = scatter_rows(
        lambda at, n: dot_t(lax.dynamic_slice_in_dim(dgate, at, n, 0), w_gate)
        + dot_t(lax.dynamic_slice_in_dim(dupward, at, n, 0), w_up),
        z,
        c,
    )
    dmiddle_norm, mlp_gain_rows = norm_back(dnormed_two, middle, scale_two, gain_mlp)
    dmiddle = cot_own.astype(f32) + dmiddle_norm
    dbranch = gather_rows(dmiddle.astype(bf16), z, c)
    output = (
        middle
        + scatter_rows(lambda at, n: dot(lax.dynamic_slice_in_dim(hidden, at, n, 0), w_down), z, c)
    ).astype(bf16)

    early = jnp.concatenate(
        [
            t_dot(attn_use, dbranch).astype(bf16),
            t_dot(dgate, normed_two).astype(bf16),
            t_dot(dupward, normed_two).astype(bf16),
            t_dot(hidden, cot).astype(bf16),
        ],
        axis=0,
    )
    early = lax.psum(early, PLANE)

    dattn = dot_t(dbranch, w_out).astype(bf16).reshape(rows, 2, HD)
    row_dot = jnp.sum(dattn.astype(f32) * attended, axis=-1).T[..., None]
    dprobs = jnp.einsum("qhd,pd->hqp", dattn, value_use, preferred_element_type=f32)
    dscores = (probs * (dprobs - row_dot)).astype(bf16)
    dquery_rot = jnp.einsum("hqp,pd->qhd", dscores, key_use, preferred_element_type=f32) * HD ** (-0.5)
    dkey_rot = jnp.einsum("hqp,qhd->pd", dscores, query_use, preferred_element_type=f32) * HD ** (-0.5)
    dvalue_use = jnp.einsum("hqp,qhd->pd", probs_use, dattn, preferred_element_type=f32).astype(bf16)
    dquery_heads, query_gain_rows = norm_back(
        rotate(dquery_rot, cosine, -sine_table), query_heads, query_scale, gain_query
    )
    dkey_heads, key_gain_rows = norm_back(
        rotate(dkey_rot[:, None], cosine, -sine_table), key_heads, key_scale, gain_key
    )
    dpre = jnp.concatenate(
        [
            dquery_heads.reshape(rows, 2 * HD).astype(bf16),
            dkey_heads.reshape(rows, HD).astype(bf16),
            dvalue_use,
        ],
        axis=1,
    )
    dnormed = scatter_rows(
        lambda at, n: dot_t(lax.dynamic_slice_in_dim(dpre, at, n, 0), w_qkv), z, c
    )
    dinput_norm, attn_gain_rows = norm_back(dnormed, inputs, scale_one, gain_attn)
    input_grad = dmiddle + dinput_norm

    gain_part = jnp.concatenate(
        [
            jnp.sum(attn_gain_rows, axis=0),
            jnp.sum(mlp_gain_rows, axis=0),
            jnp.sum(query_gain_rows, axis=(0, 1)),
            jnp.sum(key_gain_rows, axis=(0, 1)),
            jnp.zeros((3 * D - 2 * D - 2 * HD,), f32),
        ]
    ).reshape(3, D)
    gain_high = gain_part.astype(bf16)
    gain_low = (gain_part - gain_high.astype(f32)).astype(bf16)
    late = jnp.concatenate(
        [t_dot(dpre, normed).astype(bf16), gain_high, gain_low, jnp.zeros((2, D), bf16)], axis=0
    )
    late = lax.psum(late, PLANE)

    gain_sum = (late[512:515].astype(f32) + late[515:518].astype(f32)).reshape(3 * D)
    gain_sum = gain_sum + over_z(gain_sum, 1)
    gain_sum = gain_sum + over_z(gain_sum, 2)
    gain_sum = gain_sum + over_core(gain_sum)
    gain_grad = gain_sum[: 2 * D + 2 * HD]
    new_first = adam_first * gain_first + (1.0 - adam_first) * gain_grad
    new_second = adam_second * gain_second + (1.0 - adam_second) * gain_grad * gain_grad
    step_first = new_first / (1.0 - adam_first**STEP)
    step_second = new_second / (1.0 - adam_second**STEP)
    new_gains = gains - gain_rate * step_first / (jnp.sqrt(step_second) + adam_epsilon)

    def seven(late_rows, early_rows):
        return (
            late_rows[:256],
            late_rows[256:384],
            late_rows[384:512],
            early_rows[:256],
            early_rows[256:640],
            early_rows[640:1024],
            early_rows[1024:],
        )

    sums = seven(late, early)
    home_sums = seven(trade(late, home), trade(early, home))
    new_moments = [
        momentum_decay * moments[i] + (home_sums[i] if i in SPLIT_FIRST else home_sums[i].T).astype(f32)
        for i in range(7)
    ]

    own_slot = jnp.minimum(xl * 8 + y * 2 + c, 6)
    plane_slot = jnp.minimum(xl * 8 + y * 2 + xh, 6)
    old = lax.switch(
        own_slot,
        [lambda i=i: to_slot(moments[i] if i in SPLIT_FIRST else moments[i].T, i) for i in range(7)],
    )
    old = trade(old.reshape(WIDEST, D), home)
    added = lax.switch(plane_slot, [lambda i=i: to_slot(sums[i], i) for i in range(7)])
    rows_own = momentum_decay * old + added.reshape(WIDEST, D).astype(f32)
    rows_all = lax.all_gather(rows_own.astype(bf16), ("c", "z"), axis=0, tiled=True)
    gram = t_dot(rows_all, rows_all)
    orth = newton_schulz(gram, rows_own).astype(bf16)
    orth = trade(orth, home).reshape(REPLICAS, WIDEST // REPLICAS, D)
    pieces = lax.all_to_all(orth, ("xl", "y", "c"), 0, 0)
    place = xl * 8 + y * 2 + c
    new_weights = []
    for i in range(7):
        per = PIECE_ROWS[i]
        update = pieces[i, :per].astype(f32)
        axis = 0 if i in SPLIT_FIRST else 1
        if axis:
            update = update.T
        kept = lax.dynamic_slice_in_dim(weights[i], place * per, per, axis)
        rate = update_rate * SPREADS[i] * math.sqrt(max(FULL_SHAPES[i]))
        new_weights.append(kept * (1.0 - weight_shrink) - rate * update)

    return (
        trade(output, home),
        trade(input_grad, home),
        new_first,
        new_second,
        new_gains,
        *new_moments,
        *new_weights,
    )


def solution(mesh):
    fine = Mesh(mesh.devices.reshape(2, 4, 2, 4, 2), ("xh", "z", "xl", "y", "c"))
    shard = ("xh", "z")
    replica = ("xl", "y", "c")
    rows = P(replica + shard, None)
    split = tuple(P(shard, None) if i in SPLIT_FIRST else P(None, shard) for i in range(7))
    pieces = tuple(
        P(shard + replica, None) if i in SPLIT_FIRST else P(None, shard + replica) for i in range(7)
    )
    in_specs = (rows, rows, P(replica, None), P(), P(), P()) + split + split
    out_specs = (rows, rows, P(), P(), P()) + split + pieces
    return jax.shard_map(shards, mesh=fine, in_specs=in_specs, out_specs=out_specs, check_vma=False)
```

```python
import math

import jax
import jax.numpy as jnp
from jax import lax
from jax.experimental import pallas as pl
from jax.experimental.pallas import tpu as pltpu
from jax.sharding import Mesh, PartitionSpec as P

D = 1024
H = 16
KV = 8
HD = 128
FF = 3072
NS_ITERS = 5
STEP = 10

norm_epsilon = 1e-06
rotary_base = 1000000.0
momentum_decay = 0.95
poly_first = 3.4445
poly_second = -4.775
poly_third = 2.0315
orth_epsilon = 1e-07
update_rate = 0.5
weight_shrink = 0.002
adam_first = 0.9
adam_second = 0.999
adam_epsilon = 1e-08
gain_rate = 0.8

f32 = jnp.float32
bf16 = jnp.bfloat16

PLANE = ("xh", "xl", "y")
TP = 8
REPLICAS = 16

EARLY = 96
LATE = 64
PIECE = 16
FULL_SHAPES = ((D, H * HD), (D, KV * HD), (D, KV * HD), (H * HD, D), (D, FF), (D, FF), (FF, D))
SPREADS = (
    D ** (-0.5),
    D ** (-0.5),
    D ** (-0.5),
    max(H * HD // 256, 4) ** (-0.5),
    D ** (-0.5),
    D ** (-0.5),
    FF ** (-0.5),
)
SPLIT_FIRST = (3, 6)


def trade(x, home):
    other = lax.ppermute(x, ("xh", "c"), [(1, 2), (2, 1)])
    return jnp.where(home, x, other)


def over_z(x, k):
    return lax.ppermute(x, "z", [(i, i ^ k) for i in range(4)])


def over_core(x):
    return lax.ppermute(x, "c", [(0, 1), (1, 0)])


def gather_rows(block, z, c):
    rows = block.shape[0]
    parts = [(z, block)] + [(z ^ k, over_z(block, k)) for k in (1, 3, 2)]
    whole = jnp.zeros((TP * rows,) + block.shape[1:], block.dtype)
    for place, part in parts:
        whole = lax.dynamic_update_slice_in_dim(whole, part, (c * 4 + place) * rows, 0)
        whole = lax.dynamic_update_slice_in_dim(whole, over_core(part), ((1 - c) * 4 + place) * rows, 0)
    return whole


def scatter_rows(product, z, c):
    away = product((1 - c) * 512, 512).astype(bf16)
    kept = product(c * 512, 512)
    half = kept + over_core(away).astype(f32)
    total = lax.dynamic_slice_in_dim(half, z * 128, 128, 0)
    sent = half.astype(bf16)
    for k in (1, 3, 2):
        total = total + over_z(lax.dynamic_slice_in_dim(sent, (z ^ k) * 128, 128, 0), k).astype(f32)
    return total


def rms_scale(values):
    return lax.rsqrt(jnp.mean(values * values, axis=-1, keepdims=True) + norm_epsilon)


def rotary_tables(position, head_width):
    half_width = head_width // 2
    freq_steps = jnp.arange(half_width, dtype=f32)
    inverse = rotary_base ** (-2.0 * freq_steps / head_width)
    angles = position.astype(f32)[:, None] * inverse[None, :]
    return (jnp.cos(angles)[:, None, :], jnp.sin(angles)[:, None, :])


def rotate(values, cosine, sine_table):
    half_width = values.shape[-1] // 2
    front_half = values[..., :half_width]
    back_half = values[..., half_width:]
    return jnp.concatenate(
        [
            front_half * cosine - back_half * sine_table,
            back_half * cosine + front_half * sine_table,
        ],
        axis=-1,
    )


def stream_layout(lengths_row, stream_rows):
    ends_at = jnp.cumsum(lengths_row)
    places = jnp.arange(stream_rows, dtype=jnp.int32)
    passed = (places[:, None] >= ends_at[None, :]).astype(jnp.int32)
    segment = jnp.sum(passed, axis=1)
    position = places - jnp.sum(passed * lengths_row[None, :], axis=1)
    return (segment, position)


def norm_back(upstream, values, scale, gain):
    weighted = upstream * gain
    inner = jnp.mean(weighted * values, axis=-1, keepdims=True)
    grad_values = scale * (weighted - values * scale * scale * inner)
    return (grad_values, upstream * values * scale)


def dot(a, b):
    return jnp.dot(a, b, preferred_element_type=f32)


def dot_t(a, b):
    return lax.dot_general(a, b, (((1,), (1,)), ((), ())), preferred_element_type=f32)


def t_dot(a, b):
    return lax.dot_general(a, b, (((0,), (0,)), ((), ())), preferred_element_type=f32)


def turned(rows):
    return t_dot(rows, jnp.eye(rows.shape[0], dtype=bf16))


def newton_schulz_kernel(gram_ref, rows_ref, out_ref, full, low, rest, once, rows):
    eye = lax.broadcasted_iota(jnp.int32, (128, 128), 0) == lax.broadcasted_iota(jnp.int32, (128, 128), 1)
    diagonal = jnp.zeros((128, 128), f32)
    for i in range(D // 128):
        span = slice(i * 128, (i + 1) * 128)
        diagonal = diagonal + jnp.where(eye, gram_ref[span, span], 0.0)
    total = jnp.sum(diagonal, axis=(0, 1), keepdims=True) + orth_epsilon
    inverse = lax.rsqrt(total)
    scaled = gram_ref[...] * (inverse * inverse)
    full[...] = scaled
    low[...] = scaled.astype(bf16)
    rows[...] = rows_ref[...].astype(f32) * inverse
    for iteration in range(NS_ITERS):
        rest[...] = (poly_second * full[...] + poly_third * dot(low[...], low[...])).astype(bf16)
        rows[...] = poly_first * rows[...] + dot(rows[...].astype(bf16), rest[...])
        if iteration + 1 < NS_ITERS:
            value = poly_first * full[...] + dot(rest[...], low[...])
            full[...] = value
            once[...] = value.astype(bf16)
            value = poly_first * full[...] + dot(rest[...], once[...])
            full[...] = value
            low[...] = value.astype(bf16)
    out_ref[...] = rows[...].astype(bf16)


def newton_schulz(gram, rows):
    count = rows.shape[0]
    return pl.pallas_call(
        newton_schulz_kernel,
        out_shape=jax.ShapeDtypeStruct((count, D), bf16),
        in_specs=[pl.BlockSpec(memory_space=pltpu.VMEM)] * 2,
        out_specs=pl.BlockSpec(memory_space=pltpu.VMEM),
        scratch_shapes=[pltpu.VMEM((D, D), f32)]
        + [pltpu.VMEM((D, D), bf16)] * 3
        + [pltpu.VMEM((count, D), f32)],
        compiler_params=pltpu.CompilerParams(vmem_limit_bytes=40 * 2**20),
        cost_estimate=pl.CostEstimate(
            flops=13 * 2 * D**3 + 10 * count * D * D, bytes_accessed=5 * D * D, transcendentals=0
        ),
    )(gram, rows)


def sum_groups(rows):
    parts = lax.all_to_all(rows, PLANE, 0, 0)
    return jnp.sum(parts.astype(f32), axis=0)


def pad_rows(rows, count):
    return jnp.pad(rows, ((0, 0), (0, count - rows.shape[1]), (0, 0)))


def shards(tokens, cotangent, lengths, gains, gain_first, gain_second, *matrices):
    weights, moments = matrices[:7], matrices[7:]
    xh, z, xl, y, c = (lax.axis_index(a) for a in ("xh", "z", "xl", "y", "c"))
    home = xh == c
    gain_attn = gains[:D]
    gain_mlp = gains[D : 2 * D]
    gain_query = gains[2 * D : 2 * D + HD]
    gain_key = gains[2 * D + HD :]

    inputs = trade(tokens, home).astype(f32)
    segment, position = stream_layout(trade(lengths, home)[0], TP * 128)

    scale_one = rms_scale(inputs)
    normed = gather_rows((inputs * scale_one * gain_attn).astype(bf16), z, c)
    w_qkv = trade(jnp.concatenate([w.astype(bf16) for w in weights[:3]], axis=1), home)
    pre = dot(normed, w_qkv)

    pre, cotangent, moments, *others = lax.optimization_barrier((pre, cotangent, moments, *weights[3:]))
    cot_own = trade(cotangent, home)
    w_out, w_gate, w_up, w_down = (trade(w.astype(bf16), home) for w in others)
    cot = gather_rows(cot_own, z, c)

    x_own, x_plane = c * 2 + xl, xh * 2 + xl

    def old_rows(columns, count, first=False):
        def take():
            rows = lax.dynamic_slice_in_dim(columns, y * count, count, 0 if first else 1)
            return rows if first else rows.T

        return take

    def padded(take, count):
        return lambda: pad_rows(take()[None], count)[0]

    old_early = lax.switch(
        x_own,
        [
            old_rows(moments[4], EARLY),
            old_rows(moments[5], EARLY),
            old_rows(moments[6], EARLY, True),
            lambda: jnp.zeros((EARLY, D), f32),
        ],
    )
    old_late = lax.switch(
        x_own,
        [
            old_rows(moments[0], LATE),
            padded(old_rows(moments[1], LATE // 2), LATE),
            padded(old_rows(moments[2], LATE // 2), LATE),
            old_rows(moments[3], LATE, True),
        ],
    )
    old = trade(jnp.concatenate([old_early, old_late], axis=0), home)
    old_early, old_late = old[:EARLY], old[EARLY:]

    rows = pre.shape[0]
    cosine, sine_table = rotary_tables(position, HD)
    query_heads = pre[:, :256].reshape(rows, 2, HD)
    key_heads = pre[:, 256:384].reshape(rows, 1, HD)
    value_use = pre[:, 384:].astype(bf16)
    query_scale = rms_scale(query_heads)
    key_scale = rms_scale(key_heads)
    query_use = rotate(query_heads * query_scale * gain_query, cosine, sine_table).astype(bf16)
    key_use = rotate(key_heads * key_scale * gain_key, cosine, sine_table).astype(bf16)[:, 0]
    order = jnp.arange(rows, dtype=jnp.int32)
    allowed = (segment[:, None] == segment[None, :]) & (order[:, None] >= order[None, :])
    scores = jnp.einsum("qhd,pd->hqp", query_use, key_use, preferred_element_type=f32) * HD ** (-0.5)
    masked = jnp.where(allowed, scores, -1e30)
    peak = jnp.max(masked, axis=-1, keepdims=True)
    raised = jnp.where(allowed, jnp.exp(masked - peak), 0.0)
    probs = raised / jnp.sum(raised, axis=-1, keepdims=True)
    probs_use = probs.astype(bf16)
    attended = jnp.einsum("hqp,pd->qhd", probs_use, value_use, preferred_element_type=f32)
    attn_use = attended.reshape(rows, 2 * HD).astype(bf16)

    middle = inputs + scatter_rows(
        lambda at, n: dot(lax.dynamic_slice_in_dim(attn_use, at, n, 0), w_out), z, c
    )
    scale_two = rms_scale(middle)
    normed_two = gather_rows((middle * scale_two * gain_mlp).astype(bf16), z, c)
    gate = dot(normed_two, w_gate)
    upward = dot(normed_two, w_up)
    dhidden = dot_t(cot, w_down)
    sigmoid_gate = jax.nn.sigmoid(gate)
    activated = gate * sigmoid_gate
    hidden = (activated * upward).astype(bf16)
    dgate = (dhidden * upward * sigmoid_gate * (1.0 + gate * (1.0 - sigmoid_gate))).astype(bf16)
    dupward = (dhidden * activated).astype(bf16)
    dnormed_two = scatter_rows(
        lambda at, n: dot_t(lax.dynamic_slice_in_dim(dgate, at, n, 0), w_gate)
        + dot_t(lax.dynamic_slice_in_dim(dupward, at, n, 0), w_up),
        z,
        c,
    )
    dmiddle_norm, mlp_gain_rows = norm_back(dnormed_two, middle, scale_two, gain_mlp)
    dmiddle = cot_own.astype(f32) + dmiddle_norm
    dbranch = gather_rows(dmiddle.astype(bf16), z, c)
    early = jnp.concatenate(
        [
            t_dot(dgate, normed_two).astype(bf16),
            t_dot(dupward, normed_two).astype(bf16),
            t_dot(hidden, cot).astype(bf16),
            jnp.zeros((4 * EARLY, D), bf16),
        ],
        axis=0,
    )
    early_sum = sum_groups(early.reshape(REPLICAS, EARLY, D))
    early_own = (momentum_decay * old_early + early_sum).astype(bf16)
    early_all = lax.all_gather(early_own, ("y", "c", "z"), axis=0, tiled=True)

    dattn = dot_t(dbranch, w_out).astype(bf16).reshape(rows, 2, HD)
    row_dot = jnp.sum(dattn.astype(f32) * attended, axis=-1).T[..., None]
    dprobs = jnp.einsum("qhd,pd->hqp", dattn, value_use, preferred_element_type=f32)
    dscores = (probs * (dprobs - row_dot)).astype(bf16)
    dquery_rot = jnp.einsum("hqp,pd->qhd", dscores, key_use, preferred_element_type=f32) * HD ** (-0.5)
    dkey_rot = jnp.einsum("hqp,qhd->pd", dscores, query_use, preferred_element_type=f32) * HD ** (-0.5)
    dvalue_use = jnp.einsum("hqp,qhd->pd", probs_use, dattn, preferred_element_type=f32).astype(bf16)
    dquery_heads, query_gain_rows = norm_back(
        rotate(dquery_rot, cosine, -sine_table), query_heads, query_scale, gain_query
    )
    dkey_heads, key_gain_rows = norm_back(
        rotate(dkey_rot[:, None], cosine, -sine_table), key_heads, key_scale, gain_key
    )
    dpre = jnp.concatenate(
        [
            dquery_heads.reshape(rows, 2 * HD).astype(bf16),
            dkey_heads.reshape(rows, HD).astype(bf16),
            dvalue_use,
        ],
        axis=1,
    )
    late_grad = t_dot(dpre, normed).astype(bf16)
    late = jnp.concatenate(
        [
            late_grad[:256].reshape(4, 64, D),
            pad_rows(late_grad[256:384].reshape(4, 32, D), LATE),
            pad_rows(late_grad[384:].reshape(4, 32, D), LATE),
            t_dot(attn_use, dbranch).astype(bf16).reshape(4, 64, D),
        ],
        axis=0,
    )
    late, hidden, dpre, dmiddle = lax.optimization_barrier((late, hidden, dpre, dmiddle))
    late_sum = sum_groups(late)
    late_own = (momentum_decay * old_late + late_sum).astype(bf16)

    by_y = [late_own] + [lax.ppermute(late_own, "y", [(i, i ^ k) for i in range(4)]) for k in (3, 2, 1)]
    late_line = jnp.concatenate(by_y, axis=0)
    late_four = [late_line] + [over_z(late_line, k) for k in (1, 3, 2)]
    late_gram = 0.0
    for part in late_four:
        both = jnp.concatenate([part, over_core(part)], axis=0)
        late_gram = late_gram + t_dot(both, both)
    early_gram = t_dot(early_all, early_all)

    early_rows = lax.dynamic_index_in_dim(early_all.reshape(4, 8, EARLY, D), c * 4 + z, 1, False)
    early_rows = early_rows.reshape(REPLICAS, 3, 8, D)
    early_rows = pad_rows(lax.dynamic_index_in_dim(early_rows, jnp.minimum(y, 2), 1, False), PIECE)
    late_rows = jnp.stack([by_y[1], by_y[2], by_y[3], by_y[0]], axis=0)
    late_rows = jnp.where(
        (x_plane == 0) | (x_plane == 3),
        late_rows.reshape(REPLICAS, PIECE, D),
        pad_rows(late_rows[:, :32].reshape(REPLICAS, 8, D), PIECE),
    )
    is_late = y == 3
    gram = jnp.where(is_late, late_gram, early_gram)
    home_sum = trade(jnp.concatenate([early_sum, late_sum], axis=0).astype(bf16), home)
    gram, home_sum = lax.optimization_barrier((gram, home_sum))
    home_all = lax.all_gather(home_sum, ("xl", "y", "c"), axis=0)
    orth = newton_schulz(
        gram,
        jnp.where(is_late, late_rows, early_rows).reshape(REPLICAS * PIECE, D),
    )
    orth = trade(orth, home).reshape(REPLICAS, PIECE, D)
    pieces = lax.all_to_all(orth, ("xl", "y", "c"), 0, 0)

    dnormed = scatter_rows(
        lambda at, n: dot_t(lax.dynamic_slice_in_dim(dpre, at, n, 0), w_qkv), z, c
    )
    output = (
        middle
        + scatter_rows(lambda at, n: dot(lax.dynamic_slice_in_dim(hidden, at, n, 0), w_down), z, c)
    ).astype(bf16)
    dinput_norm, attn_gain_rows = norm_back(dnormed, inputs, scale_one, gain_attn)
    input_grad = dmiddle + dinput_norm

    gain_sum = jnp.concatenate(
        [
            jnp.sum(attn_gain_rows, axis=0),
            jnp.sum(mlp_gain_rows, axis=0),
            jnp.sum(query_gain_rows, axis=(0, 1)),
            jnp.sum(key_gain_rows, axis=(0, 1)),
        ]
    )
    for axis, step in (("c", 1), ("z", 1), ("z", 2), ("y", 1), ("y", 2), ("xl", 1), ("xh", 1)):
        size = 4 if axis in ("z", "y") else 2
        gain_sum = gain_sum + lax.ppermute(gain_sum, axis, [(i, i ^ step) for i in range(size)])
    gain_grad = gain_sum
    new_first = adam_first * gain_first + (1.0 - adam_first) * gain_grad
    new_second = adam_second * gain_second + (1.0 - adam_second) * gain_grad * gain_grad
    step_first = new_first / (1.0 - adam_first**STEP)
    step_second = new_second / (1.0 - adam_second**STEP)
    new_gains = gains - gain_rate * step_first / (jnp.sqrt(step_second) + adam_epsilon)

    home_all = home_all.reshape(2, 4, 2, EARLY + LATE, D)
    home_early, home_late = home_all[..., :EARLY, :], home_all[..., EARLY:, :]
    home_sums = (
        home_late[0, :, 0].reshape(256, D),
        home_late[1, :, 0, :32].reshape(128, D),
        home_late[0, :, 1, :32].reshape(128, D),
        home_late[1, :, 1].reshape(256, D),
        home_early[0, :, 0].reshape(384, D),
        home_early[1, :, 0].reshape(384, D),
        home_early[0, :, 1].reshape(384, D),
    )
    new_moments = [
        momentum_decay * moments[i]
        + (home_sums[i].astype(f32) if i in SPLIT_FIRST else turned(home_sums[i]))
        for i in range(7)
    ]

    pieces = pieces.reshape(2, 4, 2, PIECE, D)
    updates = (
        pieces[0, 3, 0],
        pieces[1, 3, 0, :8],
        pieces[0, 3, 1, :8],
        pieces[1, 3, 1],
        pieces[0, :3, 0, :8].reshape(24, D),
        pieces[1, :3, 0, :8].reshape(24, D),
        pieces[0, :3, 1, :8].reshape(24, D),
    )
    place = xl * 8 + y * 2 + c
    new_weights = []
    for i in range(7):
        update = updates[i].astype(f32)
        axis = 0 if i in SPLIT_FIRST else 1
        kept = lax.dynamic_slice_in_dim(weights[i], place * update.shape[0], update.shape[0], axis)
        rate = update_rate * SPREADS[i] * math.sqrt(max(FULL_SHAPES[i]))
        new_weights.append(kept * (1.0 - weight_shrink) - rate * (update.T if axis else update))

    return (
        trade(output, home),
        trade(input_grad, home),
        new_first,
        new_second,
        new_gains,
        *new_moments,
        *new_weights,
    )


def solution(mesh):
    fine = Mesh(mesh.devices.reshape(2, 4, 2, 4, 2), ("xh", "z", "xl", "y", "c"))
    shard = ("xh", "z")
    replica = ("xl", "y", "c")
    rows = P(replica + shard, None)
    split = tuple(P(shard, None) if i in SPLIT_FIRST else P(None, shard) for i in range(7))
    pieces = tuple(
        P(shard + replica, None) if i in SPLIT_FIRST else P(None, shard + replica) for i in range(7)
    )
    in_specs = (rows, rows, P(replica, None), P(), P(), P()) + split + split
    out_specs = (rows, rows, P(), P(), P()) + split + pieces
    return jax.shard_map(shards, mesh=fine, in_specs=in_specs, out_specs=out_specs, check_vma=False)
```

```python
import math

import jax
import jax.numpy as jnp
from jax import lax
from jax.experimental import pallas as pl
from jax.experimental.pallas import tpu as pltpu
from jax.sharding import Mesh, PartitionSpec as P

D = 1024
H = 16
KV = 8
HD = 128
FF = 3072
NS_ITERS = 5
STEP = 10

norm_epsilon = 1e-06
rotary_base = 1000000.0
momentum_decay = 0.95
poly_first = 3.4445
poly_second = -4.775
poly_third = 2.0315
orth_epsilon = 1e-07
update_rate = 0.5
weight_shrink = 0.002
adam_first = 0.9
adam_second = 0.999
adam_epsilon = 1e-08
gain_rate = 0.8

f32 = jnp.float32
bf16 = jnp.bfloat16

PLANE = ("xh", "xl", "y")
TP = 8
REPLICAS = 16

EARLY = 96
LATE = 64
PIECE = 16
FULL_SHAPES = ((D, H * HD), (D, KV * HD), (D, KV * HD), (H * HD, D), (D, FF), (D, FF), (FF, D))
SPREADS = (
    D ** (-0.5),
    D ** (-0.5),
    D ** (-0.5),
    max(H * HD // 256, 4) ** (-0.5),
    D ** (-0.5),
    D ** (-0.5),
    FF ** (-0.5),
)
SPLIT_FIRST = (3, 6)


def trade(x, home):
    other = lax.ppermute(x, ("xh", "c"), [(1, 2), (2, 1)])
    return jnp.where(home, x, other)


def trade_copied(x, home):
    half = x.shape[0] // 2
    first = lax.ppermute(x[:half], ("xh", "c"), [(2, 1), (0, 2)])
    second = lax.ppermute(x[half:], ("xh", "c"), [(3, 1), (1, 2)])
    return jnp.where(home, x, jnp.concatenate([first, second], axis=0))


def over_z(x, k):
    return lax.ppermute(x, "z", [(i, i ^ k) for i in range(4)])


def over_core(x):
    return lax.ppermute(x, "c", [(0, 1), (1, 0)])


def gather_rows(block, z, c):
    rows = block.shape[0]
    parts = [(z, block)] + [(z ^ k, over_z(block, k)) for k in (1, 3, 2)]
    whole = jnp.zeros((TP * rows,) + block.shape[1:], block.dtype)
    for place, part in parts:
        whole = lax.dynamic_update_slice_in_dim(whole, part, (c * 4 + place) * rows, 0)
        whole = lax.dynamic_update_slice_in_dim(whole, over_core(part), ((1 - c) * 4 + place) * rows, 0)
    return whole


def halves(x, c, axis):
    middle = x.shape[axis] // 2
    low, high = lax.slice_in_dim(x, 0, middle, axis=axis), lax.slice_in_dim(x, middle, 2 * middle, axis=axis)
    return jnp.where(c == 0, low, high), jnp.where(c == 0, high, low)


def scatter_over_z(half, z):
    total = lax.dynamic_slice_in_dim(half, z * 128, 128, 0)
    sent = half.astype(bf16)
    for k in (1, 3, 2):
        total = total + over_z(lax.dynamic_slice_in_dim(sent, (z ^ k) * 128, 128, 0), k).astype(f32)
    return total


def scatter_over_core(product, factors, axis, c):
    pairs = [halves(factor, c, axis) for factor in factors]
    away = product(*(pair[1] for pair in pairs)).astype(bf16)
    return product(*(pair[0] for pair in pairs)) + over_core(away).astype(f32)


def rms_scale(values):
    return lax.rsqrt(jnp.mean(values * values, axis=-1, keepdims=True) + norm_epsilon)


def rotary_tables(position, head_width):
    half_width = head_width // 2
    freq_steps = jnp.arange(half_width, dtype=f32)
    inverse = rotary_base ** (-2.0 * freq_steps / head_width)
    angles = inverse[:, None] * position.astype(f32)[None, :]
    return (jnp.cos(angles), jnp.sin(angles))


def stream_layout(lengths_row, stream_rows):
    ends_at = jnp.cumsum(lengths_row)
    places = jnp.arange(stream_rows, dtype=jnp.int32)
    passed = (places[:, None] >= ends_at[None, :]).astype(jnp.int32)
    start = jnp.sum(passed * lengths_row[None, :], axis=1)
    return (start, places - start)


def norm_back(upstream, values, scale, gain):
    weighted = upstream * gain
    inner = jnp.mean(weighted * values, axis=-1, keepdims=True)
    grad_values = scale * (weighted - values * scale * scale * inner)
    return (grad_values, upstream * values * scale)


def dot(a, b):
    return jnp.dot(a, b, preferred_element_type=f32)


def dot_t(a, b):
    return lax.dot_general(a, b, (((1,), (1,)), ((), ())), preferred_element_type=f32)


def t_dot(a, b):
    return lax.dot_general(a, b, (((0,), (0,)), ((), ())), preferred_element_type=f32)


def turn(values, cosine, sine):
    front, back = values[: HD // 2], values[HD // 2 :]
    return jnp.concatenate([front * cosine - back * sine, back * cosine + front * sine], axis=0)


def column_scale(values):
    return lax.rsqrt(jnp.mean(values * values, axis=0, keepdims=True) + norm_epsilon)


def block_mask(start_ref, at, count, keys):
    key = lax.broadcasted_iota(jnp.int32, (keys, count), 0)
    token = at + lax.broadcasted_iota(jnp.int32, (keys, count), 1)
    allowed = (key >= start_ref[:, at : at + count]) & (key <= token)
    return jnp.concatenate([allowed, allowed], axis=1)


def both_heads(ref, at, count):
    return jnp.concatenate([ref[:HD, at : at + count], ref[HD : 2 * HD, at : at + count]], axis=1)


def attention_kernel(pre_ref, cosine_ref, sine_ref, start_ref, gain_query_ref, gain_key_ref,
                     query_ref, key_t_ref, key_ref, value_ref, attended_ref, attn_ref, log_ref, value_t):
    cosine, sine = cosine_ref[...], sine_ref[...]
    for head in range(3):
        values = pre_ref[head * HD : (head + 1) * HD, :]
        gain = gain_query_ref[...] if head < 2 else gain_key_ref[...]
        turned_low = turn(values * column_scale(values) * gain, cosine, sine).astype(bf16)
        if head < 2:
            query_ref[head * HD : (head + 1) * HD, :] = turned_low
        else:
            key_t_ref[...] = turned_low
            key_ref[...] = turned_low.T
    low = pre_ref[3 * HD :, :].astype(bf16)
    value_t[...] = low
    value_ref[...] = low.T
    tokens, block = pre_ref.shape[1], 256
    for at in range(0, tokens, block):
        keys = at + block
        scores = dot(key_ref[:keys, :], both_heads(query_ref, at, block)) * HD ** (-0.5)
        masked = jnp.where(block_mask(start_ref, at, block, keys), scores, -1e30)
        peak = jnp.max(masked, axis=0, keepdims=True)
        raised = jnp.exp(masked - peak)
        total = jnp.sum(raised, axis=0, keepdims=True)
        probs = (raised * (1.0 / total)).astype(bf16)
        attended = dot(value_t[:, :keys], probs)
        log_total = peak + jnp.log(total)
        for head in range(2):
            span = slice(head * block, (head + 1) * block)
            attended_ref[head * HD : (head + 1) * HD, at:keys] = attended[:, span]
            attn_ref[head * HD : (head + 1) * HD, at:keys] = attended[:, span].astype(bf16)
            log_ref[head : head + 1, at:keys] = log_total[:, span]


def attention(pre, cosine, sine, start, gain_query, gain_key):
    tokens = pre.shape[1]
    shape = jax.ShapeDtypeStruct
    return pl.pallas_call(
        attention_kernel,
        out_shape=(
            shape((2 * HD, tokens), bf16),
            shape((HD, tokens), bf16),
            shape((tokens, HD), bf16),
            shape((tokens, HD), bf16),
            shape((2 * HD, tokens), f32),
            shape((2 * HD, tokens), bf16),
            shape((2, tokens), f32),
        ),
        in_specs=[pl.BlockSpec(memory_space=pltpu.VMEM)] * 6,
        out_specs=[pl.BlockSpec(memory_space=pltpu.VMEM)] * 7,
        scratch_shapes=[pltpu.VMEM((HD, tokens), bf16)],
        compiler_params=pltpu.CompilerParams(vmem_limit_bytes=40 * 2**20),
        cost_estimate=pl.CostEstimate(flops=10**9, bytes_accessed=8 * 2**20, transcendentals=2**21),
    )(pre, cosine, sine, start, gain_query, gain_key)


def norm_back_columns(upstream, values, gain):
    scale = column_scale(values)
    weighted = upstream * gain
    inner = jnp.mean(weighted * values, axis=0, keepdims=True)
    grad = scale * (weighted - values * (scale * scale * inner))
    return grad, jnp.sum(upstream * values * scale, axis=1, keepdims=True)


def attention_back_kernel(pre_ref, cosine_ref, sine_ref, start_ref, gain_query_ref, gain_key_ref,
                          query_ref, key_t_ref, key_ref, value_ref, attended_ref, log_ref, dattn_ref,
                          dpre_ref, query_gain_ref, key_gain_ref, dquery, dkey, dvalue):
    tokens, block = pre_ref.shape[1], 256
    dkey[...] = jnp.zeros_like(dkey)
    dvalue[...] = jnp.zeros_like(dvalue)
    for at in range(0, tokens, block):
        keys = at + block
        query = both_heads(query_ref, at, block)
        dattn = both_heads(dattn_ref, at, block)
        row_dot = jnp.sum(dattn.astype(f32) * both_heads(attended_ref, at, block), axis=0, keepdims=True)
        log_total = jnp.concatenate([log_ref[:1, at:keys], log_ref[1:, at:keys]], axis=1)
        scores = dot(key_ref[:keys, :], query) * HD ** (-0.5)
        allowed = block_mask(start_ref, at, block, keys)
        probs = jnp.where(allowed, jnp.exp(scores - log_total), 0.0)
        dprobs = dot(value_ref[:keys, :], dattn)
        dscores = (probs * (dprobs - row_dot)).astype(bf16)
        grad = dot(key_t_ref[:, :keys], dscores)
        for head in range(2):
            dquery[head * HD : (head + 1) * HD, at:keys] = grad[:, head * block : (head + 1) * block]
        dkey[:, :keys] += dot_t(query, dscores)
        dvalue[:, :keys] += dot_t(dattn, probs.astype(bf16))
    cosine, sine = cosine_ref[...], sine_ref[...]
    query_gain = jnp.zeros_like(query_gain_ref)
    for head in range(3):
        span = slice(head * HD, (head + 1) * HD)
        upstream = (dquery[span, :] if head < 2 else dkey[...]) * HD ** (-0.5)
        gain = gain_query_ref[...] if head < 2 else gain_key_ref[...]
        grad, gain_part = norm_back_columns(turn(upstream, cosine, -sine), pre_ref[span, :], gain)
        dpre_ref[span, :] = grad.astype(bf16)
        if head < 2:
            query_gain = query_gain + gain_part
        else:
            key_gain_ref[...] = gain_part
    query_gain_ref[...] = query_gain
    dpre_ref[3 * HD :, :] = dvalue[...].astype(bf16)


def attention_back(pre, cosine, sine, start, gain_query, gain_key, query, key_t, key, value, attended, log_total, dattn):
    tokens = pre.shape[1]
    shape = jax.ShapeDtypeStruct
    return pl.pallas_call(
        attention_back_kernel,
        out_shape=(shape((4 * HD, tokens), bf16), shape((HD, 1), f32), shape((HD, 1), f32)),
        in_specs=[pl.BlockSpec(memory_space=pltpu.VMEM)] * 13,
        out_specs=[pl.BlockSpec(memory_space=pltpu.VMEM)] * 3,
        scratch_shapes=[
            pltpu.VMEM((2 * HD, tokens), f32),
            pltpu.VMEM((HD, tokens), f32),
            pltpu.VMEM((HD, tokens), f32),
        ],
        compiler_params=pltpu.CompilerParams(vmem_limit_bytes=40 * 2**20),
        cost_estimate=pl.CostEstimate(flops=2 * 10**9, bytes_accessed=8 * 2**20, transcendentals=2**21),
    )(pre, cosine, sine, start, gain_query, gain_key, query, key_t, key, value, attended, log_total, dattn)


def turned(rows):
    return t_dot(rows, jnp.eye(rows.shape[0], dtype=bf16))


def newton_schulz_kernel(late_ref, early_ref, rows_ref, *refs):
    parts, (out_ref, full, low, rest, once, rows, stacked) = refs[:8], refs[8:]

    @pl.when(late_ref[0] == 0)
    def _():
        full[...] = early_ref[...]

    @pl.when(late_ref[0] == 1)
    def _():
        count = parts[0].shape[0]
        for i, part in enumerate(parts):
            stacked[i * count : (i + 1) * count, :] = part[...]
        full[...] = t_dot(stacked[...], stacked[...])

    eye = lax.broadcasted_iota(jnp.int32, (128, 128), 0) == lax.broadcasted_iota(jnp.int32, (128, 128), 1)
    diagonal = jnp.zeros((128, 128), f32)
    for i in range(D // 128):
        span = slice(i * 128, (i + 1) * 128)
        diagonal = diagonal + jnp.where(eye, full[span, span], 0.0)
    total = jnp.sum(diagonal, axis=(0, 1), keepdims=True) + orth_epsilon
    inverse = lax.rsqrt(total)
    scaled = full[...] * (inverse * inverse)
    full[...] = scaled
    low[...] = scaled.astype(bf16)
    rows[...] = rows_ref[...].astype(f32) * inverse
    for iteration in range(NS_ITERS):
        rest[...] = (poly_second * full[...] + poly_third * dot(low[...], low[...])).astype(bf16)
        rows[...] = poly_first * rows[...] + dot(rows[...].astype(bf16), rest[...])
        if iteration + 1 < NS_ITERS:
            value = poly_first * full[...] + dot(rest[...], low[...])
            full[...] = value
            once[...] = value.astype(bf16)
            value = poly_first * full[...] + dot(rest[...], once[...])
            full[...] = value
            low[...] = value.astype(bf16)
    out_ref[...] = rows[...].astype(bf16)


def newton_schulz(is_late, early_gram, rows, late_parts):
    count = rows.shape[0]
    vmem = pl.BlockSpec(memory_space=pltpu.VMEM)
    return pl.pallas_call(
        newton_schulz_kernel,
        out_shape=jax.ShapeDtypeStruct((count, D), bf16),
        in_specs=[pl.BlockSpec(memory_space=pltpu.SMEM)] + [vmem] * 10,
        out_specs=vmem,
        scratch_shapes=[pltpu.VMEM((D, D), f32)]
        + [pltpu.VMEM((D, D), bf16)] * 3
        + [pltpu.VMEM((count, D), f32), pltpu.VMEM((8 * late_parts[0].shape[0], D), bf16)],
        compiler_params=pltpu.CompilerParams(vmem_limit_bytes=48 * 2**20),
        cost_estimate=pl.CostEstimate(
            flops=15 * 2 * D**3 + 10 * count * D * D, bytes_accessed=10 * D * D, transcendentals=0
        ),
    )(is_late.astype(jnp.int32).reshape(1), early_gram, rows, *late_parts)


def pad_rows(rows, count):
    return jnp.pad(rows, ((0, 0), (0, count - rows.shape[1]), (0, 0)))


def shards(tokens, cotangent, lengths, gains, gain_first, gain_second, *matrices):
    weights, moments = matrices[:7], matrices[7:]
    xh, z, xl, y, c = (lax.axis_index(a) for a in ("xh", "z", "xl", "y", "c"))
    home = xh == c
    gain_attn = gains[:D]
    gain_mlp = gains[D : 2 * D]
    gain_query = gains[2 * D : 2 * D + HD]
    gain_key = gains[2 * D + HD :]

    w_qkv = jnp.concatenate([w.astype(bf16) for w in weights[:3]], axis=1)
    start, position = stream_layout(trade(lengths, home)[0], TP * 128)
    inputs, w_qkv, cotangent, moments = lax.optimization_barrier(
        (trade(tokens, home), w_qkv, cotangent, moments)
    )
    inputs = inputs.astype(f32)
    scale_one = rms_scale(inputs)
    normed = gather_rows((inputs * scale_one * gain_attn).astype(bf16), z, c)
    w_qkv = trade_copied(w_qkv, home)
    cot_own = trade(cotangent, home)
    cosine, sine = rotary_tables(position, HD)
    start = start[None, :]

    x_own, x_plane = c * 2 + xl, xh * 2 + xl

    def old_rows(columns, count, first=False):
        def take():
            rows = lax.dynamic_slice_in_dim(columns, y * count, count, 0 if first else 1)
            return rows if first else rows.T

        return take

    def padded(take, count):
        return lambda: pad_rows(take()[None], count)[0]

    old_early = lax.switch(
        x_own,
        [
            old_rows(moments[4], EARLY),
            old_rows(moments[5], EARLY),
            old_rows(moments[6], EARLY, True),
            lambda: jnp.zeros((EARLY, D), f32),
        ],
    )
    old_late = lax.switch(
        x_own,
        [
            old_rows(moments[0], LATE),
            padded(old_rows(moments[1], LATE // 2), LATE),
            padded(old_rows(moments[2], LATE // 2), LATE),
            old_rows(moments[3], LATE, True),
        ],
    )
    old = jnp.concatenate([old_early, old_late], axis=0)
    others = tuple(w.astype(bf16) for w in weights[3:])
    normed, w_qkv, cot_own, cosine, sine, start, old, others = lax.optimization_barrier(
        (normed, w_qkv, cot_own, cosine, sine, start, old, others)
    )

    tables = (cosine, sine, start, gain_query[:, None], gain_key[:, None])
    pre = lax.dot_general(w_qkv, normed, (((0,), (1,)), ((), ())), preferred_element_type=f32)
    w_out, w_gate, w_up, w_down = (trade_copied(w, home) for w in others)
    cot = gather_rows(cot_own, z, c)
    query_use, key_t, key_use, value_use, attended, attn_use, log_total = attention(pre, *tables)

    middle = inputs + scatter_over_z(scatter_over_core(lambda a: t_dot(a, w_out), (attn_use,), 1, c), z)
    scale_two = rms_scale(middle)
    normed_two = gather_rows((middle * scale_two * gain_mlp).astype(bf16), z, c)
    old = trade(old, home)
    old_early, old_late = old[:EARLY], old[EARLY:]
    dhidden = dot_t(cot, w_down)
    normed_two, dhidden = lax.optimization_barrier((normed_two, dhidden))
    gate = dot(normed_two, w_gate)
    upward = dot(normed_two, w_up)
    sigmoid_gate = jax.nn.sigmoid(gate)
    activated = gate * sigmoid_gate
    hidden = (activated * upward).astype(bf16)
    dgate = (dhidden * upward * sigmoid_gate * (1.0 + gate * (1.0 - sigmoid_gate))).astype(bf16)
    dupward = (dhidden * activated).astype(bf16)
    half = scatter_over_core(lambda a, b: dot_t(a, w_gate) + dot_t(b, w_up), (dgate, dupward), 0, c)
    half, early_factors = lax.optimization_barrier((half, (dgate, dupward, hidden)))
    dnormed_two = scatter_over_z(half, z)
    early = jnp.concatenate(
        [
            t_dot(early_factors[0], normed_two).astype(bf16),
            t_dot(early_factors[1], normed_two).astype(bf16),
            t_dot(early_factors[2], cot).astype(bf16),
            jnp.zeros((4 * EARLY, D), bf16),
        ],
        axis=0,
    )
    early_parts = lax.all_to_all(early.reshape(REPLICAS, EARLY, D), PLANE, 0, 0)
    dmiddle_norm, mlp_gain_rows = norm_back(dnormed_two, middle, scale_two, gain_mlp)
    dmiddle = cot_own.astype(f32) + dmiddle_norm
    dbranch = gather_rows(dmiddle.astype(bf16), z, c)
    dbranch, early_parts = lax.optimization_barrier((dbranch, early_parts))

    dattn = dot_t(w_out, dbranch).astype(bf16)
    dpre, query_gain, key_gain = attention_back(
        pre, *tables, query_use, key_t, key_use, value_use, attended, log_total, dattn
    )
    late_grad = dot(dpre, normed).astype(bf16)
    late = jnp.concatenate(
        [
            late_grad[:256].reshape(4, 64, D),
            pad_rows(late_grad[256:384].reshape(4, 32, D), LATE),
            pad_rows(late_grad[384:].reshape(4, 32, D), LATE),
            dot(attn_use, dbranch).astype(bf16).reshape(4, 64, D),
        ],
        axis=0,
    )
    late, dpre, hidden, early_parts = lax.optimization_barrier((late, dpre, hidden, early_parts))
    late_parts = lax.all_to_all(late, PLANE, 0, 0)
    early_sum = jnp.sum(early_parts.astype(f32), axis=0)
    early_own = (momentum_decay * old_early + early_sum).astype(bf16)
    early_all = lax.all_gather(early_own, ("y", "c", "z"), axis=0, tiled=True)
    dnormed = scatter_over_core(
        lambda a: lax.dot_general(a, w_qkv, (((0,), (1,)), ((), ())), preferred_element_type=f32),
        (dpre,),
        1,
        c,
    )
    dnormed = scatter_over_z(dnormed, z)
    output = middle + scatter_over_z(scatter_over_core(lambda a: dot(a, w_down), (hidden,), 0, c), z)
    dinput_norm, attn_gain_rows = norm_back(dnormed, inputs, scale_one, gain_attn)
    input_grad = dmiddle + dinput_norm
    gain_sum = jnp.concatenate(
        [
            jnp.sum(attn_gain_rows, axis=0),
            jnp.sum(mlp_gain_rows, axis=0),
            query_gain[:, 0],
            key_gain[:, 0],
        ]
    )
    late_parts, output, input_grad, gain_sum = lax.optimization_barrier(
        (late_parts, output, input_grad, gain_sum)
    )
    late_sum = jnp.sum(late_parts.astype(f32), axis=0)
    late_own = (momentum_decay * old_late + late_sum).astype(bf16)

    by_y = [late_own] + [lax.ppermute(late_own, "y", [(i, i ^ k) for i in range(4)]) for k in (3, 2, 1)]
    late_line = jnp.concatenate(by_y, axis=0)
    late_all = [late_line] + [over_z(late_line, k) for k in (1, 3, 2)]
    late_all += [over_core(part) for part in late_all]
    early_gram = t_dot(early_all, early_all)

    for axis, step, size in (("z", 1, 4), ("z", 2, 4), ("xh", 1, 2)):
        gain_sum = gain_sum + lax.ppermute(gain_sum, axis, [(i, i ^ step) for i in range(size)])
    gain_rows = jnp.pad(gain_sum, (0, 3 * D - gain_sum.shape[0])).reshape(3, D)
    gain_high = gain_rows.astype(bf16)
    gain_low = (gain_rows - gain_high.astype(f32)).astype(bf16)

    early_rows = lax.dynamic_index_in_dim(early_all.reshape(4, 8, EARLY, D), c * 4 + z, 1, False)
    early_rows = early_rows.reshape(REPLICAS, 3, 8, D)
    early_rows = pad_rows(lax.dynamic_index_in_dim(early_rows, jnp.minimum(y, 2), 1, False), PIECE)
    late_rows = jnp.stack([by_y[1], by_y[2], by_y[3], by_y[0]], axis=0)
    late_rows = jnp.where(
        (x_plane == 0) | (x_plane == 3),
        late_rows.reshape(REPLICAS, PIECE, D),
        pad_rows(late_rows[:, :32].reshape(REPLICAS, 8, D), PIECE),
    )
    home_sum = trade(jnp.concatenate([early_sum, late_sum], axis=0).astype(bf16), home)
    home_sum = jnp.concatenate([home_sum, gain_high, gain_low, jnp.zeros((2, D), bf16)], axis=0)
    early_gram, late_all, home_sum = lax.optimization_barrier((early_gram, late_all, home_sum))
    home_all = lax.all_gather(home_sum, ("xl", "y", "c"), axis=0)
    orth = newton_schulz(
        y == 3,
        early_gram,
        jnp.where(y == 3, late_rows, early_rows).reshape(REPLICAS * PIECE, D),
        late_all,
    )
    orth, output, input_grad = lax.optimization_barrier((trade(orth, home), output, input_grad))
    pieces = lax.all_to_all(orth.reshape(REPLICAS, PIECE, D), ("xl", "y", "c"), 0, 0)
    results = trade(jnp.concatenate([output, input_grad], axis=0).astype(bf16), home)
    output = results[:128]
    input_grad = jnp.where(home, input_grad, results[128:].astype(f32))

    gain_all = home_all[:, EARLY + LATE :].astype(f32)
    gain_grad = jnp.sum(gain_all[:, :3] + gain_all[:, 3:6], axis=0).reshape(3 * D)[: 2 * D + 2 * HD]
    new_first = adam_first * gain_first + (1.0 - adam_first) * gain_grad
    new_second = adam_second * gain_second + (1.0 - adam_second) * gain_grad * gain_grad
    step_first = new_first / (1.0 - adam_first**STEP)
    step_second = new_second / (1.0 - adam_second**STEP)
    new_gains = gains - gain_rate * step_first / (jnp.sqrt(step_second) + adam_epsilon)

    home_all = home_all.reshape(2, 4, 2, -1, D)
    home_early, home_late = home_all[..., :EARLY, :], home_all[..., EARLY : EARLY + LATE, :]
    home_sums = (
        home_late[0, :, 0].reshape(256, D),
        home_late[1, :, 0, :32].reshape(128, D),
        home_late[0, :, 1, :32].reshape(128, D),
        home_late[1, :, 1].reshape(256, D),
        home_early[0, :, 0].reshape(384, D),
        home_early[1, :, 0].reshape(384, D),
        home_early[0, :, 1].reshape(384, D),
    )
    new_moments = [
        momentum_decay * moments[i]
        + (home_sums[i].astype(f32) if i in SPLIT_FIRST else turned(home_sums[i]))
        for i in range(7)
    ]

    place = xl * 8 + y * 2 + c
    kept = []
    for i in range(7):
        axis = 0 if i in SPLIT_FIRST else 1
        per = weights[i].shape[axis] // REPLICAS
        kept.append(lax.dynamic_slice_in_dim(weights[i], place * per, per, axis) * (1.0 - weight_shrink))
    pieces, new_moments, kept = lax.optimization_barrier((pieces, new_moments, kept))
    pieces = pieces.reshape(2, 4, 2, PIECE, D)
    updates = (
        pieces[0, 3, 0],
        pieces[1, 3, 0, :8],
        pieces[0, 3, 1, :8],
        pieces[1, 3, 1],
        pieces[0, :3, 0, :8].reshape(24, D),
        pieces[1, :3, 0, :8].reshape(24, D),
        pieces[0, :3, 1, :8].reshape(24, D),
    )
    new_weights = []
    for i in range(7):
        update = updates[i].astype(f32)
        rate = update_rate * SPREADS[i] * math.sqrt(max(FULL_SHAPES[i]))
        new_weights.append(kept[i] - rate * (update if i in SPLIT_FIRST else update.T))

    return (
        output,
        input_grad,
        new_first,
        new_second,
        new_gains,
        *new_moments,
        *new_weights,
    )


def solution(mesh):
    fine = Mesh(mesh.devices.reshape(2, 4, 2, 4, 2), ("xh", "z", "xl", "y", "c"))
    shard = ("xh", "z")
    replica = ("xl", "y", "c")
    rows = P(replica + shard, None)
    split = tuple(P(shard, None) if i in SPLIT_FIRST else P(None, shard) for i in range(7))
    pieces = tuple(
        P(shard + replica, None) if i in SPLIT_FIRST else P(None, shard + replica) for i in range(7)
    )
    in_specs = (rows, rows, P(replica, None), P(), P(), P()) + split + split
    out_specs = (rows, rows, P(), P(), P()) + split + pieces
    return jax.shard_map(shards, mesh=fine, in_specs=in_specs, out_specs=out_specs, check_vma=False)
```

```python
import math

import jax
import jax.numpy as jnp
from jax import lax
from jax.experimental import pallas as pl
from jax.experimental.pallas import tpu as pltpu
from jax.sharding import Mesh, PartitionSpec as P

D = 1024
H = 16
KV = 8
HD = 128
FF = 3072
NS_ITERS = 5
STEP = 10

norm_epsilon = 1e-06
rotary_base = 1000000.0
momentum_decay = 0.95
poly_first = 3.4445
poly_second = -4.775
poly_third = 2.0315
orth_epsilon = 1e-07
update_rate = 0.5
weight_shrink = 0.002
adam_first = 0.9
adam_second = 0.999
adam_epsilon = 1e-08
gain_rate = 0.8

f32 = jnp.float32
bf16 = jnp.bfloat16

PLANE = ("xh", "xl", "y")
REPLICAS = 16
BLOCK = 128
TOKENS = 8 * BLOCK
EARLY = 96
LATE = 64
PIECE = 16
FIRST_PACK = ((0, 256), (256, 128), (384, 128), (512, 256))
SECOND_PACK = ((0, 384), (384, 384), (768, 384))
SPLIT_FIRST = (3, 6)
FULL_SHAPES = ((D, H * HD), (D, KV * HD), (D, KV * HD), (H * HD, D), (D, FF), (D, FF), (FF, D))
SPREADS = (
    D ** (-0.5),
    D ** (-0.5),
    D ** (-0.5),
    max(H * HD // 256, 4) ** (-0.5),
    D ** (-0.5),
    D ** (-0.5),
    FF ** (-0.5),
)
RATES = tuple(update_rate * s * math.sqrt(max(f)) for s, f in zip(SPREADS, FULL_SHAPES))


def dot(a, b):
    return jnp.dot(a, b, preferred_element_type=f32)


def dot_t(a, b):
    return lax.dot_general(a, b, (((1,), (1,)), ((), ())), preferred_element_type=f32)


def t_dot(a, b):
    return lax.dot_general(a, b, (((0,), (0,)), ((), ())), preferred_element_type=f32)


def vmem_call(kernel, outs, scratch, operands, flops, scalars=0, bytes_accessed=8 * 2**20, limit=16):
    vmem, smem = (pl.BlockSpec(memory_space=m) for m in (pltpu.VMEM, pltpu.SMEM))
    return pl.pallas_call(
        kernel,
        out_shape=tuple(jax.ShapeDtypeStruct(shape, dtype) for shape, dtype in outs),
        in_specs=[smem] * scalars + [vmem] * (len(operands) - scalars),
        out_specs=tuple(vmem for _ in outs),
        scratch_shapes=[pltpu.VMEM(shape, dtype) for shape, dtype in scratch],
        compiler_params=pltpu.CompilerParams(vmem_limit_bytes=limit * 2**20),
        cost_estimate=pl.CostEstimate(flops=flops, bytes_accessed=bytes_accessed, transcendentals=0),
    )(*operands)


def trade(x, home):
    other = lax.ppermute(x, ("xh", "c"), [(1, 2), (2, 1)])
    return jnp.where(home, x, other)


def trade_copied(x, home):
    other = lax.ppermute(x, ("xh", "c"), [(0, 2), (3, 1)])
    return jnp.where(home, x, other)


def over_z(x, k):
    return lax.ppermute(x, "z", [(i, i ^ k) for i in range(4)])


def over_core(x):
    return lax.ppermute(x, "c", [(0, 1), (1, 0)])


def gather_blocks(block, side=()):
    near = over_z(block, 1)
    far = over_z(block, 3)
    across = over_z(block, 2)
    near, side = lax.optimization_barrier((near, side))
    line = [block, near, across, far]
    return line + [over_core(part) for part in line], side


def scatter_over_z(half, side=()):
    sent = half.astype(bf16)
    parts = [over_z(sent[k * BLOCK : (k + 1) * BLOCK], k) for k in (1, 3, 2)]
    parts[0], side = lax.optimization_barrier((parts[0], side))
    return half[:BLOCK] + sum(part.astype(f32) for part in parts), side


def rms_scale(values):
    return lax.rsqrt(jnp.mean(values * values, axis=-1, keepdims=True) + norm_epsilon)


def rotary_tables(position, head_width):
    half_width = head_width // 2
    freq_steps = jnp.arange(half_width, dtype=f32)
    inverse = rotary_base ** (-2.0 * freq_steps / head_width)
    angles = inverse[:, None] * position.astype(f32)[None, :]
    return (jnp.cos(angles), jnp.sin(angles))


def stream_layout(lengths_row, stream_rows):
    ends_at = jnp.cumsum(lengths_row)
    places = jnp.arange(stream_rows, dtype=jnp.int32)
    passed = (places[:, None] >= ends_at[None, :]).astype(jnp.int32)
    start = jnp.sum(passed * lengths_row[None, :], axis=1)
    return (start, places - start)


def norm_back(upstream, values, scale, gain):
    weighted = upstream * gain
    inner = jnp.mean(weighted * values, axis=-1, keepdims=True)
    grad_values = scale * (weighted - values * scale * scale * inner)
    return (grad_values, upstream * values * scale)


def pack_kernel(scale_ref, q, k, v, o, g, u, d, first_ref, second_ref):
    scale = scale_ref[0]
    for (at, count), ref in zip(FIRST_PACK, (q, k, v)):
        first_ref[at : at + count, :] = (ref[...] * scale).T.astype(bf16)
    at, count = FIRST_PACK[3]
    first_ref[at : at + count, :] = (o[...] * scale).astype(bf16)
    at, count = SECOND_PACK[0]
    second_ref[at : at + count, :] = (d[...] * scale).astype(bf16)
    for (at, count), ref in zip(SECOND_PACK[1:], (g, u)):
        second_ref[at : at + count, :] = (ref[...] * scale).T.astype(bf16)


def pack(matrices, scale):
    return vmem_call(
        pack_kernel,
        (((768, D), bf16), ((1152, D), bf16)),
        (),
        (jnp.asarray(scale, f32).reshape(1), *matrices),
        10**6,
        1,
        12 * 2**20,
    )


def turn(values, cosine, sine):
    front, back = values[: HD // 2], values[HD // 2 :]
    return jnp.concatenate([front * cosine - back * sine, back * cosine + front * sine], axis=0)


def column_scale(values):
    return lax.rsqrt(jnp.mean(values * values, axis=0, keepdims=True) + norm_epsilon)


def block_mask(start_ref, at, count, keys):
    key = lax.broadcasted_iota(jnp.int32, (keys, count), 0)
    token = at + lax.broadcasted_iota(jnp.int32, (keys, count), 1)
    allowed = (key >= start_ref[:, at : at + count]) & (key <= token)
    return jnp.concatenate([allowed, allowed], axis=1)


def both_heads(ref, at, count):
    return jnp.concatenate([ref[:HD, at : at + count], ref[HD : 2 * HD, at : at + count]], axis=1)


def in_order(order_ref, block):
    return pl.ds(pl.multiple_of(order_ref[block] * BLOCK, BLOCK), BLOCK)


def attention_kernel(order_ref, cosine_ref, sine_ref, start_ref, gain_query_ref, gain_key_ref, weight_ref, *refs):
    blocks = refs[:8]
    pre_ref, query_ref, key_t_ref, key_ref, value_ref, attended_ref, attn_ref, log_ref, normed, value_t = refs[8:]
    for i, block in enumerate(blocks):
        normed[in_order(order_ref, i), :] = block[...]
    pre_ref[...] = dot_t(weight_ref[: 4 * HD, :], normed[...])
    cosine, sine = cosine_ref[...], sine_ref[...]
    for head in range(3):
        values = pre_ref[head * HD : (head + 1) * HD, :]
        gain = gain_query_ref[...] if head < 2 else gain_key_ref[...]
        turned_low = turn(values * column_scale(values) * gain, cosine, sine).astype(bf16)
        if head < 2:
            query_ref[head * HD : (head + 1) * HD, :] = turned_low
        else:
            key_t_ref[...] = turned_low
            key_ref[...] = turned_low.T
    low = pre_ref[3 * HD :, :].astype(bf16)
    value_t[...] = low
    value_ref[...] = low.T
    count = 2 * BLOCK
    for at in range(0, TOKENS, count):
        keys = at + count
        scores = dot(key_ref[:keys, :], both_heads(query_ref, at, count)) * HD ** (-0.5)
        masked = jnp.where(block_mask(start_ref, at, count, keys), scores, -1e30)
        peak = jnp.max(masked, axis=0, keepdims=True)
        raised = jnp.exp(masked - peak)
        total = jnp.sum(raised, axis=0, keepdims=True)
        probs = (raised * (1.0 / total)).astype(bf16)
        attended = dot(value_t[:, :keys], probs)
        log_total = peak + jnp.log(total)
        for head in range(2):
            span = slice(head * count, (head + 1) * count)
            attended_ref[head * HD : (head + 1) * HD, at:keys] = attended[:, span]
            log_ref[head : head + 1, at:keys] = log_total[:, span]
    for i in range(8):
        attn_ref[:, i * BLOCK : (i + 1) * BLOCK] = attended_ref[:, in_order(order_ref, i)].astype(bf16)


def attention(order, tables, weight, blocks):
    outs = (
        ((4 * HD, TOKENS), f32),
        ((2 * HD, TOKENS), bf16),
        ((HD, TOKENS), bf16),
        ((TOKENS, HD), bf16),
        ((TOKENS, HD), bf16),
        ((2 * HD, TOKENS), f32),
        ((2 * HD, TOKENS), bf16),
        ((2, TOKENS), f32),
    )
    scratch = (((TOKENS, D), bf16), ((HD, TOKENS), bf16))
    return vmem_call(attention_kernel, outs, scratch, (order, *tables, weight, *blocks), 2 * 10**9, 1)


def norm_back_columns(upstream, values, gain):
    scale = column_scale(values)
    weighted = upstream * gain
    inner = jnp.mean(weighted * values, axis=0, keepdims=True)
    grad = scale * (weighted - values * (scale * scale * inner))
    return grad, jnp.sum(upstream * values * scale, axis=1, keepdims=True)


def attention_back_kernel(order_ref, cosine_ref, sine_ref, start_ref, gain_query_ref, gain_key_ref, weight_ref,
                          pre_ref, query_ref, key_t_ref, key_ref, value_ref, attended_ref, log_ref, momentum_ref, *refs):
    normed_blocks, dbranch_blocks = refs[:8], refs[8:16]
    dpre_ref, late_ref, query_gain_ref, key_gain_ref, dquery, dkey, dvalue, dattn_ref, dpre, normed, dbranch = refs[16:]
    for i in range(8):
        dbranch[in_order(order_ref, i), :] = dbranch_blocks[i][...]
    dattn_ref[...] = dot_t(weight_ref[4 * HD :, :], dbranch[...]).astype(bf16)
    dkey[...] = jnp.zeros_like(dkey)
    dvalue[...] = jnp.zeros_like(dvalue)
    count = 2 * BLOCK
    for at in range(0, TOKENS, count):
        keys = at + count
        query = both_heads(query_ref, at, count)
        dattn = both_heads(dattn_ref, at, count)
        row_dot = jnp.sum(dattn.astype(f32) * both_heads(attended_ref, at, count), axis=0, keepdims=True)
        log_total = jnp.concatenate([log_ref[:1, at:keys], log_ref[1:, at:keys]], axis=1)
        scores = dot(key_ref[:keys, :], query) * HD ** (-0.5)
        allowed = block_mask(start_ref, at, count, keys)
        probs = jnp.where(allowed, jnp.exp(scores - log_total), 0.0)
        dprobs = dot(value_ref[:keys, :], dattn)
        dscores = (probs * (dprobs - row_dot)).astype(bf16)
        grad = dot(key_t_ref[:, :keys], dscores)
        for head in range(2):
            dquery[head * HD : (head + 1) * HD, at:keys] = grad[:, head * count : (head + 1) * count]
        dkey[:, :keys] += dot_t(query, dscores)
        dvalue[:, :keys] += dot_t(dattn, probs.astype(bf16))
    cosine, sine = cosine_ref[...], sine_ref[...]
    query_gain = jnp.zeros_like(query_gain_ref)
    for head in range(3):
        span = slice(head * HD, (head + 1) * HD)
        upstream = (dquery[span, :] if head < 2 else dkey[...]) * HD ** (-0.5)
        gain = gain_query_ref[...] if head < 2 else gain_key_ref[...]
        grad, gain_part = norm_back_columns(turn(upstream, cosine, -sine), pre_ref[span, :], gain)
        dpre[span, :] = grad.astype(bf16)
        if head < 2:
            query_gain = query_gain + gain_part
        else:
            key_gain_ref[...] = gain_part
    query_gain_ref[...] = query_gain
    dpre[3 * HD :, :] = dvalue[...].astype(bf16)
    for i in range(8):
        dpre_ref[:, i * BLOCK : (i + 1) * BLOCK] = dpre[:, in_order(order_ref, i)]
        normed[in_order(order_ref, i), :] = normed_blocks[i][...]
    grads = dot(dpre[...], normed[...]) + momentum_ref[: 4 * HD, :].astype(f32)
    late_ref[:256, :] = grads[:256].astype(bf16)
    late_ref[256:768, :] = jnp.zeros((512, D), bf16)
    for i in range(4):
        late_ref[256 + 64 * i : 288 + 64 * i, :] = grads[256 + 32 * i : 288 + 32 * i].astype(bf16)
        late_ref[512 + 64 * i : 544 + 64 * i, :] = grads[384 + 32 * i : 416 + 32 * i].astype(bf16)
    out_grad = dot(attended_ref[...].astype(bf16), dbranch[...])
    late_ref[768:, :] = (out_grad + momentum_ref[4 * HD :, :].astype(f32)).astype(bf16)


def attention_back(order, tables, weight, kept, momentum, normed, dbranch):
    outs = (
        ((4 * HD, TOKENS), bf16),
        ((REPLICAS * LATE, D), bf16),
        ((HD, 1), f32),
        ((HD, 1), f32),
    )
    scratch = (
        ((2 * HD, TOKENS), f32),
        ((HD, TOKENS), f32),
        ((HD, TOKENS), f32),
        ((2 * HD, TOKENS), bf16),
        ((4 * HD, TOKENS), bf16),
        ((TOKENS, D), bf16),
        ((TOKENS, D), bf16),
    )
    operands = (order, *tables, weight, *kept, momentum, *normed, *dbranch)
    return vmem_call(attention_back_kernel, outs, scratch, operands, 5 * 10**9, 1, limit=24)


def feed_forward_kernel(weight_ref, *refs):
    normed_blocks, cot_blocks = refs[:8], refs[8:16]
    hidden_ref, grads_ref, away_ref, kept_ref, normed, cot = refs[16:]
    for i in range(8):
        span = slice(i * BLOCK, (i + 1) * BLOCK)
        normed[span, :] = normed_blocks[i][...]
        cot[span, :] = cot_blocks[i][...]
    width = SECOND_PACK[0][1]
    for part, out_ref in ((1, away_ref), (0, kept_ref)):
        span = slice(part * TOKENS // 2, (part + 1) * TOKENS // 2)
        both = dot_t(normed[span, :], weight_ref[width:, :])
        dhidden = dot_t(cot[span, :], weight_ref[:width, :])
        gate, upward = both[:, :width], both[:, width:]
        sigmoid_gate = jax.nn.sigmoid(gate)
        activated = gate * sigmoid_gate
        hidden_ref[span, :] = (activated * upward).astype(bf16)
        dgate = dhidden * upward * sigmoid_gate * (1.0 + gate * (1.0 - sigmoid_gate))
        grads_ref[span, :width] = dgate.astype(bf16)
        grads_ref[span, width:] = (dhidden * activated).astype(bf16)
        out_ref[...] = dot(grads_ref[span, :], weight_ref[width:, :]).astype(out_ref.dtype)


def feed_forward(weight, normed, cot):
    outs = (
        ((TOKENS, 384), bf16),
        ((TOKENS, 768), bf16),
        ((TOKENS // 2, D), bf16),
        ((TOKENS // 2, D), f32),
    )
    scratch = (((TOKENS, D), bf16), ((TOKENS, D), bf16))
    return vmem_call(feed_forward_kernel, outs, scratch, (weight, *normed, *cot), 4 * 10**9)


def early_kernel(hidden_ref, grads_ref, momentum_ref, *refs):
    normed_blocks, cot_blocks = refs[:8], refs[8:16]
    out_ref, normed, cot = refs[16:]
    for i in range(8):
        span = slice(i * BLOCK, (i + 1) * BLOCK)
        normed[span, :] = normed_blocks[i][...]
        cot[span, :] = cot_blocks[i][...]
    out_ref[:768, :] = (t_dot(grads_ref[...], normed[...]) + momentum_ref[384:, :].astype(f32)).astype(bf16)
    out_ref[768:1152, :] = (t_dot(hidden_ref[...], cot[...]) + momentum_ref[:384, :].astype(f32)).astype(bf16)
    out_ref[1152:, :] = jnp.zeros((384, D), bf16)


def early_gradients(hidden, grads, momentum, normed, cot):
    outs = (((REPLICAS * EARLY, D), bf16),)
    scratch = (((TOKENS, D), bf16), ((TOKENS, D), bf16))
    operands = (hidden, grads, momentum, *normed, *cot)
    return vmem_call(early_kernel, outs, scratch, operands, 3 * 10**9)[0]


def newton_schulz_kernel(late_ref, early_ref, rows_ref, *refs):
    parts, (out_ref, full, low, rest, once, rows, stacked) = refs[:8], refs[8:]

    @pl.when(late_ref[0] == 0)
    def _():
        full[...] = t_dot(early_ref[...], early_ref[...])

    @pl.when(late_ref[0] == 1)
    def _():
        count = parts[0].shape[0]
        for i, part in enumerate(parts):
            stacked[i * count : (i + 1) * count, :] = part[...]
        full[...] = t_dot(stacked[...], stacked[...])

    eye = lax.broadcasted_iota(jnp.int32, (128, 128), 0) == lax.broadcasted_iota(jnp.int32, (128, 128), 1)
    diagonal = jnp.zeros((128, 128), f32)
    for i in range(D // 128):
        span = slice(i * 128, (i + 1) * 128)
        diagonal = diagonal + jnp.where(eye, full[span, span], 0.0)
    total = jnp.sum(diagonal, axis=(0, 1), keepdims=True) + orth_epsilon
    inverse = lax.rsqrt(total)
    scaled = full[...] * (inverse * inverse)
    full[...] = scaled
    low[...] = scaled.astype(bf16)
    rows[...] = rows_ref[...].astype(f32) * inverse
    for iteration in range(NS_ITERS):
        rest[...] = (poly_second * full[...] + poly_third * dot(low[...], low[...])).astype(bf16)
        rows[...] = poly_first * rows[...] + dot(rows[...].astype(bf16), rest[...])
        if iteration + 1 < NS_ITERS:
            value = poly_first * full[...] + dot(rest[...], low[...])
            full[...] = value
            once[...] = value.astype(bf16)
            value = poly_first * full[...] + dot(rest[...], once[...])
            full[...] = value
            low[...] = value.astype(bf16)
    out_ref[...] = rows[...].astype(bf16)


def newton_schulz(is_late, early_all, rows, late_parts):
    count = rows.shape[0]
    scratch = (
        ((D, D), f32),
        ((D, D), bf16),
        ((D, D), bf16),
        ((D, D), bf16),
        ((count, D), f32),
        ((8 * late_parts[0].shape[0], D), bf16),
    )
    operands = (is_late.astype(jnp.int32).reshape(1), early_all, rows, *late_parts)
    return vmem_call(
        newton_schulz_kernel, (((count, D), bf16),), scratch, operands, 17 * 2 * D**3 + 10 * count * D * D, 1, limit=40
    )[0]


def momentum_kernel(all_ref, q, k, v, o, g, u, d):
    def rows(column, at, count):
        entries = [(column % 2 * 4 + y) * 2 + column // 2 for y in range(4)]
        return jnp.concatenate([all_ref[entry, at : at + count, :] for entry in entries], axis=0).astype(f32)

    q[...] = rows(0, EARLY, 64).T
    k[...] = rows(1, EARLY, 32).T
    v[...] = rows(2, EARLY, 32).T
    o[...] = rows(3, EARLY, 64)
    g[...] = rows(0, 0, EARLY).T
    u[...] = rows(1, 0, EARLY).T
    d[...] = rows(2, 0, EARLY)


def weight_kernel(half_ref, pieces_ref, *refs):
    kept, outs = refs[:7], refs[7:]
    half = half_ref[0]

    def rows(column, ys, count):
        return jnp.concatenate(
            [pieces_ref[column * 8 + y * 2 + half][:count, :] for y in ys], axis=0
        ).astype(f32)

    late, early = (3,), (0, 1, 2)
    updates = (
        rows(0, late, 16),
        rows(1, late, 8),
        rows(2, late, 8),
        rows(3, late, 16),
        rows(0, early, 8),
        rows(1, early, 8),
        rows(2, early, 8),
    )
    for i in range(7):
        update = updates[i] if i in SPLIT_FIRST else updates[i].T
        outs[i][...] = kept[i][...] - RATES[i] * update


def pad_rows(rows, count):
    return jnp.pad(rows, ((0, 0), (0, count - rows.shape[1]), (0, 0)))


def shards(tokens, cotangent, lengths, gains, gain_first, gain_second, *matrices):
    weights, moments = matrices[:7], matrices[7:]
    xh, z, xl, y, c = (lax.axis_index(a) for a in ("xh", "z", "xl", "y", "c"))
    home = xh == c
    gain_attn = gains[:D]
    gain_mlp = gains[D : 2 * D]
    gain_query = gains[2 * D : 2 * D + HD]
    gain_key = gains[2 * D + HD :]
    order = jnp.stack([(c ^ (i // 4)) * 4 + (z ^ (i % 4)) for i in range(8)]).astype(jnp.int32)

    codes = jnp.concatenate([lengths[0] // 32, lengths[0] % 32]).astype(bf16)
    codes = jnp.pad(codes[None], ((0, 15), (0, D - codes.shape[0])))
    first_weights, second_weights = pack(weights, 1.0)
    arrived = trade(jnp.concatenate([tokens, cotangent, codes], axis=0), home)
    arrived, first_weights, moments = lax.optimization_barrier((arrived, first_weights, moments))
    inputs = arrived[:BLOCK].astype(f32)
    scale_one = rms_scale(inputs)
    normed, _ = gather_blocks((inputs * scale_one * gain_attn).astype(bf16))
    cot_own = arrived[BLOCK : 2 * BLOCK]
    codes = arrived[2 * BLOCK, :12].astype(jnp.int32)
    start, position = stream_layout(codes[:6] * 32 + codes[6:], TOKENS)
    first_weights = trade_copied(first_weights, home)
    first_momentum, second_momentum = pack(moments, jnp.where(home, momentum_decay / 8, 0.0))
    tables = (*rotary_tables(position, HD), start[None, :], gain_query[:, None], gain_key[:, None])
    normed, first_weights, tables, cot_own, first_momentum, second_momentum = lax.optimization_barrier(
        (normed, first_weights, tables, cot_own, first_momentum, second_momentum)
    )

    cot, _ = gather_blocks(cot_own)
    pre, query_use, key_t, key_use, value_use, attended, attn_use, log_total = attention(
        order, tables, first_weights, normed
    )
    middle_rows = TOKENS // 2
    out_weight = first_weights[4 * HD :]
    away = t_dot(attn_use[:, middle_rows:], out_weight).astype(bf16)
    half = t_dot(attn_use[:, :middle_rows], out_weight) + over_core(away).astype(f32)
    branch, second_weights = scatter_over_z(half, second_weights)
    middle = inputs + branch
    second_weights = trade_copied(second_weights, home)

    scale_two = rms_scale(middle)
    normed_two, _ = gather_blocks((middle * scale_two * gain_mlp).astype(bf16))
    hidden, grads, away, kept = feed_forward(second_weights, normed_two, cot)
    half = kept + over_core(away).astype(f32)
    dnormed_two, (hidden, grads) = scatter_over_z(half, (hidden, grads))
    early = early_gradients(hidden, grads, second_momentum, normed_two, cot)
    dmiddle_norm, mlp_gain_rows = norm_back(dnormed_two, middle, scale_two, gain_mlp)
    dmiddle = cot_own.astype(f32) + dmiddle_norm
    dbranch, (early, hidden) = gather_blocks(dmiddle.astype(bf16), (early, hidden))
    early_parts = lax.all_to_all(early.reshape(REPLICAS, EARLY, D), PLANE, 0, 0)
    down_weight = second_weights[:384]
    out_away = dot(hidden[middle_rows:], down_weight).astype(bf16)
    out_half = dot(hidden[:middle_rows], down_weight) + over_core(out_away).astype(f32)
    dbranch, early_parts = lax.optimization_barrier((dbranch, early_parts))

    dpre, late, query_gain, key_gain = attention_back(
        order,
        tables,
        first_weights,
        (pre, query_use, key_t, key_use, value_use, attended, log_total),
        first_momentum,
        normed,
        dbranch,
    )
    late_parts = lax.all_to_all(late.reshape(REPLICAS, LATE, D), PLANE, 0, 0)
    dpre, early_parts, out_half = lax.optimization_barrier((dpre, early_parts, out_half))
    early_own = jnp.sum(early_parts.astype(f32), axis=0).astype(bf16)
    early_all = lax.all_gather(early_own, ("y", "c", "z"), axis=0, tiled=True)
    in_weight = first_weights[: 4 * HD]
    away = t_dot(dpre[:, middle_rows:], in_weight).astype(bf16)
    half = t_dot(dpre[:, :middle_rows], in_weight) + over_core(away).astype(f32)
    dnormed, _ = scatter_over_z(half)
    output = middle + scatter_over_z(out_half)[0]
    dinput_norm, attn_gain_rows = norm_back(dnormed, inputs, scale_one, gain_attn)
    input_grad = dmiddle + dinput_norm
    gain_rows = jnp.concatenate(
        [
            jnp.sum(attn_gain_rows, axis=0),
            jnp.sum(mlp_gain_rows, axis=0),
            query_gain[:, 0],
            key_gain[:, 0],
            jnp.zeros((D - 2 * HD,), f32),
        ]
    ).reshape(3, D)
    gain_high = gain_rows.astype(bf16)
    gain_low = (gain_rows - gain_high.astype(f32)).astype(bf16)
    results = jnp.concatenate(
        [output.astype(bf16), input_grad.astype(bf16), gain_high, gain_low, jnp.zeros((2, D), bf16)], axis=0
    )
    late_parts, results, early_own = lax.optimization_barrier((late_parts, results, early_own))
    late_own = jnp.sum(late_parts.astype(f32), axis=0).astype(bf16)

    by_y = [late_own] + [lax.ppermute(late_own, "y", [(i, i ^ k) for i in range(4)]) for k in (3, 2, 1)]
    late_line = jnp.concatenate(by_y, axis=0)
    late_all = [late_line] + [over_z(late_line, k) for k in (1, 3, 2)]
    late_all += [over_core(part) for part in late_all]
    results = trade(jnp.concatenate([early_own, late_own, results], axis=0), home)

    x_plane = xh * 2 + xl
    early_rows = lax.dynamic_index_in_dim(early_all.reshape(4, 8, EARLY, D), c * 4 + z, 1, False)
    early_rows = early_rows.reshape(REPLICAS, 3, 8, D)
    early_rows = pad_rows(lax.dynamic_index_in_dim(early_rows, jnp.minimum(y, 2), 1, False), PIECE)
    late_rows = jnp.stack([by_y[1], by_y[2], by_y[3], by_y[0]], axis=0)
    late_rows = jnp.where(
        (x_plane == 0) | (x_plane == 3),
        late_rows.reshape(REPLICAS, PIECE, D),
        pad_rows(late_rows[:, :32].reshape(REPLICAS, 8, D), PIECE),
    )
    own_rows = jnp.where(y == 3, late_rows, early_rows).reshape(REPLICAS * PIECE, D)
    own_rows, early_all, late_all, results = lax.optimization_barrier((own_rows, early_all, late_all, results))
    results, sums = results[EARLY + LATE :], results[: EARLY + LATE]
    home_all = lax.all_gather(
        jnp.concatenate([sums, results[2 * BLOCK :]], axis=0), ("xl", "y", "c"), axis=0
    )
    orth = newton_schulz(y == 3, early_all, own_rows, late_all)
    orth, weights = lax.optimization_barrier((orth, weights))

    mine = (jnp.arange(2) == c)[:, None, None, None]
    sent = jnp.where(mine, orth.reshape(1, REPLICAS, PIECE, D), 0).reshape(2 * REPLICAS, PIECE, D)
    pieces = lax.all_to_all(sent, ("xh", "xl", "y", "c"), 0, 0)

    output = results[:BLOCK]
    input_grad = jnp.where(home, input_grad, results[BLOCK : 2 * BLOCK].astype(f32))
    gain_all = home_all[:, EARLY + LATE :].astype(f32)
    gain_sum = jnp.sum(gain_all[:, :3] + gain_all[:, 3:6], axis=0)
    for axis, step, size in (("z", 1, 4), ("z", 2, 4), ("xh", 1, 2)):
        gain_sum = gain_sum + lax.ppermute(gain_sum, axis, [(i, i ^ step) for i in range(size)])
    gain_grad = gain_sum.reshape(3 * D)[: 2 * D + 2 * HD]
    new_first = adam_first * gain_first + (1.0 - adam_first) * gain_grad
    new_second = adam_second * gain_second + (1.0 - adam_second) * gain_grad * gain_grad
    step_first = new_first / (1.0 - adam_first**STEP)
    step_second = new_second / (1.0 - adam_second**STEP)
    new_gains = gains - gain_rate * step_first / (jnp.sqrt(step_second) + adam_epsilon)
    new_moments = vmem_call(
        momentum_kernel, tuple((m.shape, f32) for m in moments), (), (home_all,), 10**6, 0, 14 * 2**20
    )
    place = xl * 8 + y * 2 + c
    kept = []
    for i in range(7):
        axis = 0 if i in SPLIT_FIRST else 1
        per = weights[i].shape[axis] // REPLICAS
        kept.append(lax.dynamic_slice_in_dim(weights[i], place * per, per, axis) * (1.0 - weight_shrink))
    pieces, new_moments, kept, new_gains = lax.optimization_barrier((pieces, new_moments, kept, new_gains))
    new_weights = vmem_call(
        weight_kernel,
        tuple((part.shape, f32) for part in kept),
        (),
        (xh.astype(jnp.int32).reshape(1), pieces, *kept),
        10**6,
        1,
        4 * 2**20,
    )
    return (output, input_grad, new_first, new_second, new_gains, *new_moments, *new_weights)


def solution(mesh):
    fine = Mesh(mesh.devices.reshape(2, 4, 2, 4, 2), ("xh", "z", "xl", "y", "c"))
    shard = ("xh", "z")
    replica = ("xl", "y", "c")
    rows = P(replica + shard, None)
    split = tuple(P(shard, None) if i in SPLIT_FIRST else P(None, shard) for i in range(7))
    pieces = tuple(
        P(shard + replica, None) if i in SPLIT_FIRST else P(None, shard + replica) for i in range(7)
    )
    in_specs = (rows, rows, P(replica, None), P(), P(), P()) + split + split
    out_specs = (rows, rows, P(), P(), P()) + split + pieces
    return jax.shard_map(shards, mesh=fine, in_specs=in_specs, out_specs=out_specs, check_vma=False)
```

```python
import math

import jax
import jax.numpy as jnp
from jax import lax
from jax.experimental import pallas as pl
from jax.experimental.pallas import tpu as pltpu
from jax.sharding import Mesh, PartitionSpec as P

D = 1024
H = 16
KV = 8
HD = 128
FF = 3072
NS_ITERS = 5
STEP = 10

norm_epsilon = 1e-06
rotary_base = 1000000.0
momentum_decay = 0.95
poly_first = 3.4445
poly_second = -4.775
poly_third = 2.0315
orth_epsilon = 1e-07
update_rate = 0.5
weight_shrink = 0.002
adam_first = 0.9
adam_second = 0.999
adam_epsilon = 1e-08
gain_rate = 0.8

f32 = jnp.float32
bf16 = jnp.bfloat16

PLANE = ("xh", "xl", "y")
REPLICAS = 16
BLOCK = 128
TOKENS = 8 * BLOCK
EARLY = 96
LATE = 64
PIECE = 16
FIRST_PACK = ((0, 256), (256, 128), (384, 128), (512, 256))
SECOND_PACK = ((0, 384), (384, 384), (768, 384))
SPLIT_FIRST = (3, 6)
FULL_SHAPES = ((D, H * HD), (D, KV * HD), (D, KV * HD), (H * HD, D), (D, FF), (D, FF), (FF, D))
SPREADS = (
    D ** (-0.5),
    D ** (-0.5),
    D ** (-0.5),
    max(H * HD // 256, 4) ** (-0.5),
    D ** (-0.5),
    D ** (-0.5),
    FF ** (-0.5),
)
RATES = tuple(update_rate * s * math.sqrt(max(f)) for s, f in zip(SPREADS, FULL_SHAPES))


def dot(a, b):
    return jnp.dot(a, b, preferred_element_type=f32)


def dot_t(a, b):
    return lax.dot_general(a, b, (((1,), (1,)), ((), ())), preferred_element_type=f32)


def t_dot(a, b):
    return lax.dot_general(a, b, (((0,), (0,)), ((), ())), preferred_element_type=f32)


def vmem_call(kernel, outs, scratch, operands, flops, scalars=0, bytes_accessed=8 * 2**20, limit=16, fetched=0):
    vmem, smem, anywhere = (pl.BlockSpec(memory_space=m) for m in (pltpu.VMEM, pltpu.SMEM, pl.ANY))
    scratch_shapes = [pltpu.VMEM(shape, dtype) for shape, dtype in scratch]
    if fetched:
        scratch_shapes.append(pltpu.SemaphoreType.DMA((fetched,)))
    return pl.pallas_call(
        kernel,
        out_shape=tuple(jax.ShapeDtypeStruct(shape, dtype) for shape, dtype in outs),
        in_specs=[smem] * scalars + [vmem] * (len(operands) - scalars - fetched) + [anywhere] * fetched,
        out_specs=tuple(vmem for _ in outs),
        scratch_shapes=scratch_shapes,
        compiler_params=pltpu.CompilerParams(vmem_limit_bytes=limit * 2**20),
        cost_estimate=pl.CostEstimate(flops=flops, bytes_accessed=bytes_accessed, transcendentals=0),
    )(*operands)


def fetch(sources, targets, sems, first=0):
    copies = [
        pltpu.make_async_copy(source, target, sems.at[first + i])
        for i, (source, target) in enumerate(zip(sources, targets))
    ]
    for copy in copies:
        copy.start()
    return copies


def wait(copies):
    for copy in copies:
        copy.wait()


def block_views(stacked):
    count = stacked.shape[0] // 8
    return [stacked.at[i * count : (i + 1) * count, :] for i in range(8)]


def trade(x, home):
    other = lax.ppermute(x, ("xh", "c"), [(1, 2), (2, 1)])
    return jnp.where(home, x, other)


def trade_copied(x, home):
    other = lax.ppermute(x, ("xh", "c"), [(0, 2), (3, 1)])
    return jnp.where(home, x, other)


def over_z(x, k):
    return lax.ppermute(x, "z", [(i, i ^ k) for i in range(4)])


def over_core(x):
    return lax.ppermute(x, "c", [(0, 1), (1, 0)])


def gather_blocks(block, side=()):
    near, far, across = (over_z(block, k) for k in (1, 3, 2))
    other, side = lax.optimization_barrier((over_core(block), side))
    return [block, near, across, far, other] + [over_core(part) for part in (near, across, far)], side


def scatter_over_z(half):
    sent = half.astype(bf16)
    parts = [over_z(sent[k * BLOCK : (k + 1) * BLOCK], k) for k in (1, 3, 2)]
    return half[:BLOCK] + sum(part.astype(f32) for part in parts)


def rms_scale(values):
    return lax.rsqrt(jnp.mean(values * values, axis=-1, keepdims=True) + norm_epsilon)


def rotary_tables(position, head_width):
    half_width = head_width // 2
    freq_steps = jnp.arange(half_width, dtype=f32)
    inverse = rotary_base ** (-2.0 * freq_steps / head_width)
    angles = inverse[:, None] * position.astype(f32)[None, :]
    return (jnp.cos(angles), jnp.sin(angles))


def stream_layout(lengths_row, stream_rows):
    ends_at = jnp.cumsum(lengths_row)
    places = jnp.arange(stream_rows, dtype=jnp.int32)
    passed = (places[:, None] >= ends_at[None, :]).astype(jnp.int32)
    start = jnp.sum(passed * lengths_row[None, :], axis=1)
    return (start, places - start)


def norm_back(upstream, values, scale, gain):
    weighted = upstream * gain
    inner = jnp.mean(weighted * values, axis=-1, keepdims=True)
    grad_values = scale * (weighted - values * scale * scale * inner)
    return (grad_values, upstream * values * scale)


def pack_kernel(scale_ref, *refs):
    sources, (first_ref, second_ref), targets, sems = refs[:7], refs[7:9], refs[9:16], refs[16]
    copies = fetch(sources, targets, sems)
    scale = scale_ref[0]
    places = tuple((first_ref, *at) for at in FIRST_PACK) + tuple(
        (second_ref, *SECOND_PACK[i]) for i in (1, 2, 0)
    )
    for i, (out_ref, at, count) in enumerate(places):
        copies[i].wait()
        values = targets[i][...] * scale
        out_ref[at : at + count, :] = (values if i in SPLIT_FIRST else values.T).astype(bf16)


def pack(matrices, scale):
    return vmem_call(
        pack_kernel,
        (((768, D), bf16), ((1152, D), bf16)),
        tuple((m.shape, f32) for m in matrices),
        (jnp.asarray(scale, f32).reshape(1), *matrices),
        10**6,
        1,
        12 * 2**20,
        20,
        7,
    )


def turn(values, cosine, sine):
    front, back = values[: HD // 2], values[HD // 2 :]
    return jnp.concatenate([front * cosine - back * sine, back * cosine + front * sine], axis=0)


def column_scale(values):
    return lax.rsqrt(jnp.mean(values * values, axis=0, keepdims=True) + norm_epsilon)


def block_mask(start_ref, at, count, keys):
    key = lax.broadcasted_iota(jnp.int32, (keys, count), 0)
    token = at + lax.broadcasted_iota(jnp.int32, (keys, count), 1)
    allowed = (key >= start_ref[:, at : at + count]) & (key <= token)
    return jnp.concatenate([allowed, allowed], axis=1)


def both_heads(ref, at, count):
    return jnp.concatenate([ref[:HD, at : at + count], ref[HD : 2 * HD, at : at + count]], axis=1)


def in_order(order_ref, block):
    return pl.ds(pl.multiple_of(order_ref[block] * BLOCK, BLOCK), BLOCK)


def attention_kernel(order_ref, cosine_ref, sine_ref, start_ref, gain_query_ref, gain_key_ref, weight_ref, *refs):
    blocks = refs[:8]
    pre_ref, query_ref, key_t_ref, key_ref, value_ref, attended_ref, attn_ref, log_ref, normed = refs[8:17]
    value_t, stacked, sems = refs[17:]
    views = block_views(stacked)
    copies = fetch(blocks, views, sems)
    for i in range(8):
        copies[i].wait()
        normed[in_order(order_ref, i), :] = views[i][...]
    pre_ref[...] = dot_t(weight_ref[: 4 * HD, :], normed[...])
    cosine, sine = cosine_ref[...], sine_ref[...]
    for head in range(3):
        values = pre_ref[head * HD : (head + 1) * HD, :]
        gain = gain_query_ref[...] if head < 2 else gain_key_ref[...]
        turned_low = turn(values * column_scale(values) * gain, cosine, sine).astype(bf16)
        if head < 2:
            query_ref[head * HD : (head + 1) * HD, :] = turned_low
        else:
            key_t_ref[...] = turned_low
            key_ref[...] = turned_low.T
    low = pre_ref[3 * HD :, :].astype(bf16)
    value_t[...] = low
    value_ref[...] = low.T
    count = 2 * BLOCK
    for at in range(0, TOKENS, count):
        keys = at + count
        scores = dot(key_ref[:keys, :], both_heads(query_ref, at, count)) * HD ** (-0.5)
        masked = jnp.where(block_mask(start_ref, at, count, keys), scores, -1e30)
        peak = jnp.max(masked, axis=0, keepdims=True)
        raised = jnp.exp(masked - peak)
        total = jnp.sum(raised, axis=0, keepdims=True)
        probs = (raised * (1.0 / total)).astype(bf16)
        attended = dot(value_t[:, :keys], probs)
        log_total = peak + jnp.log(total)
        for head in range(2):
            span = slice(head * count, (head + 1) * count)
            attended_ref[head * HD : (head + 1) * HD, at:keys] = attended[:, span]
            log_ref[head : head + 1, at:keys] = log_total[:, span]
    for i in range(8):
        attn_ref[:, i * BLOCK : (i + 1) * BLOCK] = attended_ref[:, in_order(order_ref, i)].astype(bf16)


def attention(order, tables, weight, blocks):
    outs = (
        ((4 * HD, TOKENS), f32),
        ((2 * HD, TOKENS), bf16),
        ((HD, TOKENS), bf16),
        ((TOKENS, HD), bf16),
        ((TOKENS, HD), bf16),
        ((2 * HD, TOKENS), f32),
        ((2 * HD, TOKENS), bf16),
        ((2, TOKENS), f32),
        ((TOKENS, D), bf16),
    )
    scratch = (((HD, TOKENS), bf16), ((TOKENS, D), bf16))
    operands = (order, *tables, weight, *blocks)
    return vmem_call(attention_kernel, outs, scratch, operands, 2 * 10**9, 1, fetched=8)


def norm_back_columns(upstream, values, gain):
    scale = column_scale(values)
    weighted = upstream * gain
    inner = jnp.mean(weighted * values, axis=0, keepdims=True)
    grad = scale * (weighted - values * (scale * scale * inner))
    return grad, jnp.sum(upstream * values * scale, axis=1, keepdims=True)


def attention_back_kernel(order_ref, cosine_ref, sine_ref, start_ref, gain_query_ref, gain_key_ref,
                          query_ref, key_t_ref, key_ref, value_ref, log_ref, *refs):
    dbranch_blocks, (weight_hbm, attended_hbm, pre_hbm, normed_hbm, momentum_hbm) = refs[:8], refs[8:13]
    dpre_ref, late_ref, query_gain_ref, key_gain_ref = refs[13:17]
    dquery, dkey, dvalue, dattn_ref, dpre, stacked, dbranch = refs[17:24]
    weight_ref, attended_ref, pre_ref, normed, momentum_ref, sems = refs[24:]
    views = block_views(stacked)
    copies = fetch(
        (*dbranch_blocks, weight_hbm.at[4 * HD :, :], attended_hbm, pre_hbm, normed_hbm, momentum_hbm),
        (*views, weight_ref, attended_ref, pre_ref, normed, momentum_ref),
        sems,
    )
    for i in range(8):
        copies[i].wait()
        dbranch[in_order(order_ref, i), :] = views[i][...]
    copies[8].wait()
    dattn_ref[...] = dot_t(weight_ref[...], dbranch[...]).astype(bf16)
    copies[9].wait()
    dkey[...] = jnp.zeros_like(dkey)
    dvalue[...] = jnp.zeros_like(dvalue)
    count = 2 * BLOCK
    for at in range(0, TOKENS, count):
        keys = at + count
        query = both_heads(query_ref, at, count)
        dattn = both_heads(dattn_ref, at, count)
        row_dot = jnp.sum(dattn.astype(f32) * both_heads(attended_ref, at, count), axis=0, keepdims=True)
        log_total = jnp.concatenate([log_ref[:1, at:keys], log_ref[1:, at:keys]], axis=1)
        scores = dot(key_ref[:keys, :], query) * HD ** (-0.5)
        allowed = block_mask(start_ref, at, count, keys)
        probs = jnp.where(allowed, jnp.exp(scores - log_total), 0.0)
        dprobs = dot(value_ref[:keys, :], dattn)
        dscores = (probs * (dprobs - row_dot)).astype(bf16)
        grad = dot(key_t_ref[:, :keys], dscores)
        for head in range(2):
            dquery[head * HD : (head + 1) * HD, at:keys] = grad[:, head * count : (head + 1) * count]
        dkey[:, :keys] += dot_t(query, dscores)
        dvalue[:, :keys] += dot_t(dattn, probs.astype(bf16))
    wait(copies[10:])
    cosine, sine = cosine_ref[...], sine_ref[...]
    query_gain = jnp.zeros_like(query_gain_ref)
    for head in range(3):
        span = slice(head * HD, (head + 1) * HD)
        upstream = (dquery[span, :] if head < 2 else dkey[...]) * HD ** (-0.5)
        gain = gain_query_ref[...] if head < 2 else gain_key_ref[...]
        grad, gain_part = norm_back_columns(turn(upstream, cosine, -sine), pre_ref[span, :], gain)
        dpre[span, :] = grad.astype(bf16)
        if head < 2:
            query_gain = query_gain + gain_part
        else:
            key_gain_ref[...] = gain_part
    query_gain_ref[...] = query_gain
    dpre[3 * HD :, :] = dvalue[...].astype(bf16)
    for i in range(8):
        dpre_ref[:, i * BLOCK : (i + 1) * BLOCK] = dpre[:, in_order(order_ref, i)]
    grads = dot(dpre[...], normed[...]) + momentum_ref[: 4 * HD, :].astype(f32)
    late_ref[:256, :] = grads[:256].astype(bf16)
    late_ref[256:768, :] = jnp.zeros((512, D), bf16)
    for i in range(4):
        late_ref[256 + 64 * i : 288 + 64 * i, :] = grads[256 + 32 * i : 288 + 32 * i].astype(bf16)
        late_ref[512 + 64 * i : 544 + 64 * i, :] = grads[384 + 32 * i : 416 + 32 * i].astype(bf16)
    out_grad = dot(attended_ref[...].astype(bf16), dbranch[...])
    late_ref[768:, :] = (out_grad + momentum_ref[4 * HD :, :].astype(f32)).astype(bf16)


def attention_back(order, tables, weight, kept, momentum, dbranch):
    pre, query, key_t, key, value, attended, log_total, normed = kept
    outs = (
        ((4 * HD, TOKENS), bf16),
        ((REPLICAS * LATE, D), bf16),
        ((HD, 1), f32),
        ((HD, 1), f32),
    )
    scratch = (
        ((2 * HD, TOKENS), f32),
        ((HD, TOKENS), f32),
        ((HD, TOKENS), f32),
        ((2 * HD, TOKENS), bf16),
        ((4 * HD, TOKENS), bf16),
        ((TOKENS, D), bf16),
        ((TOKENS, D), bf16),
        ((2 * HD, D), bf16),
        (attended.shape, f32),
        (pre.shape, f32),
        (normed.shape, bf16),
        (momentum.shape, bf16),
    )
    operands = (order, *tables, query, key_t, key, value, log_total, *dbranch, weight, attended, pre, normed, momentum)
    return vmem_call(attention_back_kernel, outs, scratch, operands, 5 * 10**9, 1, limit=32, fetched=13)


def feed_forward_kernel(weight_ref, *refs):
    normed_blocks, cot_blocks = refs[:8], refs[8:16]
    hidden_ref, grads_ref, away_ref, kept_ref, normed, cot, sems = refs[16:]
    copies = fetch((*normed_blocks, *cot_blocks), (*block_views(normed), *block_views(cot)), sems)
    width = SECOND_PACK[0][1]
    for part, out_ref in ((1, away_ref), (0, kept_ref)):
        for i in range(4 * part, 4 * part + 4):
            copies[i].wait()
            copies[8 + i].wait()
        span = slice(part * TOKENS // 2, (part + 1) * TOKENS // 2)
        both = dot_t(normed[span, :], weight_ref[width:, :])
        dhidden = dot_t(cot[span, :], weight_ref[:width, :])
        gate, upward = both[:, :width], both[:, width:]
        sigmoid_gate = jax.nn.sigmoid(gate)
        activated = gate * sigmoid_gate
        hidden_ref[span, :] = (activated * upward).astype(bf16)
        dgate = dhidden * upward * sigmoid_gate * (1.0 + gate * (1.0 - sigmoid_gate))
        grads_ref[span, :width] = dgate.astype(bf16)
        grads_ref[span, width:] = (dhidden * activated).astype(bf16)
        out_ref[...] = dot(grads_ref[span, :], weight_ref[width:, :]).astype(out_ref.dtype)


def feed_forward(weight, normed, cot):
    outs = (
        ((TOKENS, 384), bf16),
        ((TOKENS, 768), bf16),
        ((TOKENS // 2, D), bf16),
        ((TOKENS // 2, D), f32),
        ((TOKENS, D), bf16),
        ((TOKENS, D), bf16),
    )
    return vmem_call(feed_forward_kernel, outs, (), (weight, *normed, *cot), 4 * 10**9, fetched=16)


def early_kernel(hidden_ref, grads_ref, momentum_ref, normed, cot, out_ref):
    out_ref[:768, :] = (t_dot(grads_ref[...], normed[...]) + momentum_ref[384:, :].astype(f32)).astype(bf16)
    out_ref[768:1152, :] = (t_dot(hidden_ref[...], cot[...]) + momentum_ref[:384, :].astype(f32)).astype(bf16)
    out_ref[1152:, :] = jnp.zeros((384, D), bf16)


def early_gradients(*operands):
    return vmem_call(early_kernel, (((REPLICAS * EARLY, D), bf16),), (), operands, 3 * 10**9)[0]


def gram_kernel(rows_ref, out_ref):
    out_ref[...] = t_dot(rows_ref[...], rows_ref[...])


def newton_schulz_kernel(late_ref, rows_ref, *refs):
    gram_hbm, parts, (out_ref, full, low, rest, once, rows, stacked, sems) = refs[0], refs[1:9], refs[9:]

    @pl.when(late_ref[0] == 0)
    def _():
        copy = pltpu.make_async_copy(gram_hbm, full, sems.at[0])
        copy.start()
        copy.wait()

    @pl.when(late_ref[0] == 1)
    def _():
        wait(fetch(parts, block_views(stacked), sems, 1))
        full[...] = t_dot(stacked[...], stacked[...])

    eye = lax.broadcasted_iota(jnp.int32, (128, 128), 0) == lax.broadcasted_iota(jnp.int32, (128, 128), 1)
    diagonal = jnp.zeros((128, 128), f32)
    for i in range(D // 128):
        span = slice(i * 128, (i + 1) * 128)
        diagonal = diagonal + jnp.where(eye, full[span, span], 0.0)
    total = jnp.sum(diagonal, axis=(0, 1), keepdims=True) + orth_epsilon
    inverse = lax.rsqrt(total)
    scaled = full[...] * (inverse * inverse)
    full[...] = scaled
    low[...] = scaled.astype(bf16)
    rows[...] = rows_ref[...].astype(f32) * inverse
    for iteration in range(NS_ITERS):
        rest[...] = (poly_second * full[...] + poly_third * dot(low[...], low[...])).astype(bf16)
        rows[...] = poly_first * rows[...] + dot(rows[...].astype(bf16), rest[...])
        if iteration + 1 < NS_ITERS:
            value = poly_first * full[...] + dot(rest[...], low[...])
            full[...] = value
            once[...] = value.astype(bf16)
            value = poly_first * full[...] + dot(rest[...], once[...])
            full[...] = value
            low[...] = value.astype(bf16)
    out_ref[...] = rows[...].astype(bf16)


def newton_schulz(is_late, early_gram, rows, late_parts):
    count = rows.shape[0]
    scratch = (
        ((D, D), f32),
        ((D, D), bf16),
        ((D, D), bf16),
        ((D, D), bf16),
        ((count, D), f32),
        ((8 * late_parts[0].shape[0], D), bf16),
    )
    operands = (is_late.astype(jnp.int32).reshape(1), rows, early_gram, *late_parts)
    flops = 15 * 2 * D**3 + 10 * count * D * D
    return vmem_call(
        newton_schulz_kernel, (((count, D), bf16),), scratch, operands, flops, 1, limit=40, fetched=9
    )[0]


def momentum_kernel(all_hbm, q, k, v, o, g, u, d, all_ref, sems):
    wait(fetch((all_hbm,), (all_ref,), sems))

    def rows(column, at, count):
        entries = [(column % 2 * 4 + y) * 2 + column // 2 for y in range(4)]
        return jnp.concatenate([all_ref[entry, at : at + count, :] for entry in entries], axis=0).astype(f32)

    q[...] = rows(0, EARLY, 64).T
    k[...] = rows(1, EARLY, 32).T
    v[...] = rows(2, EARLY, 32).T
    o[...] = rows(3, EARLY, 64)
    g[...] = rows(0, 0, EARLY).T
    u[...] = rows(1, 0, EARLY).T
    d[...] = rows(2, 0, EARLY)


def weight_kernel(half_ref, pieces_ref, *refs):
    kept, outs = refs[:7], refs[7:]
    half = half_ref[0]

    def rows(column, ys, count):
        return jnp.concatenate(
            [pieces_ref[column * 8 + y * 2 + half][:count, :] for y in ys], axis=0
        ).astype(f32)

    late, early = (3,), (0, 1, 2)
    updates = (
        rows(0, late, 16),
        rows(1, late, 8),
        rows(2, late, 8),
        rows(3, late, 16),
        rows(0, early, 8),
        rows(1, early, 8),
        rows(2, early, 8),
    )
    for i in range(7):
        outs[i][...] = kept[i][...] - RATES[i] * updates[i]


def pad_rows(rows, count):
    return jnp.pad(rows, ((0, 0), (0, count - rows.shape[1]), (0, 0)))


def shards(tokens, cotangent, lengths, gains, gain_first, gain_second, *matrices):
    weights, moments = matrices[:7], matrices[7:]
    xh, z, xl, y, c = (lax.axis_index(a) for a in ("xh", "z", "xl", "y", "c"))
    home = xh == c
    gain_attn = gains[:D]
    gain_mlp = gains[D : 2 * D]
    gain_query = gains[2 * D : 2 * D + HD]
    gain_key = gains[2 * D + HD :]
    order = jnp.stack([(c ^ (i // 4)) * 4 + (z ^ (i % 4)) for i in range(8)]).astype(jnp.int32)

    codes = jnp.concatenate([lengths[0] // 32, lengths[0] % 32]).astype(bf16)
    codes = jnp.pad(codes[None], ((0, 15), (0, D - codes.shape[0])))
    first_weights, second_weights = pack(weights, 1.0)
    arrived = trade(jnp.concatenate([tokens, cotangent, codes], axis=0), home)
    arrived, first_weights, moments = lax.optimization_barrier((arrived, first_weights, moments))
    inputs = arrived[:BLOCK].astype(f32)
    scale_one = rms_scale(inputs)
    normed, first_weights = gather_blocks((inputs * scale_one * gain_attn).astype(bf16), first_weights)
    cot_own = arrived[BLOCK : 2 * BLOCK]
    codes = arrived[2 * BLOCK, :12].astype(jnp.int32)
    start, position = stream_layout(codes[:6] * 32 + codes[6:], TOKENS)
    first_weights = trade_copied(first_weights, home)
    tables = (*rotary_tables(position, HD), start[None, :], gain_query[:, None], gain_key[:, None])
    normed, first_weights, tables, cot_own, second_weights = lax.optimization_barrier(
        (normed, first_weights, tables, cot_own, second_weights)
    )

    cot, _ = gather_blocks(cot_own)
    second_weights = trade_copied(second_weights, home)
    pre, query_use, key_t, key_use, value_use, attended, attn_use, log_total, normed = attention(
        order, tables, first_weights, normed
    )
    middle_rows = TOKENS // 2
    out_weight = first_weights[4 * HD :]
    away = t_dot(attn_use[:, middle_rows:], out_weight).astype(bf16)
    half = t_dot(attn_use[:, :middle_rows], out_weight) + over_core(away).astype(f32)
    half, cot[1:4], moments = lax.optimization_barrier((half, cot[1:4], moments))
    middle = inputs + scatter_over_z(half)

    scale_two = rms_scale(middle)
    normed_two, moments = gather_blocks((middle * scale_two * gain_mlp).astype(bf16), moments)
    first_momentum, second_momentum = pack(moments, jnp.where(home, momentum_decay / 8, 0.0))
    normed_two, cot, first_momentum, second_momentum = lax.optimization_barrier(
        (normed_two, cot, first_momentum, second_momentum)
    )
    hidden, grads, away, kept, normed_two, cot = feed_forward(second_weights, normed_two, cot)
    early = early_gradients(hidden, grads, second_momentum, normed_two, cot)
    half, early = lax.optimization_barrier((kept + over_core(away).astype(f32), early))
    early_parts = lax.all_to_all(early.reshape(REPLICAS, EARLY, D), PLANE, 0, 0)
    dnormed_two = scatter_over_z(half)
    dmiddle_norm, mlp_gain_rows = norm_back(dnormed_two, middle, scale_two, gain_mlp)
    dmiddle = cot_own.astype(f32) + dmiddle_norm
    dbranch, _ = gather_blocks(dmiddle.astype(bf16))

    dpre, late, query_gain, key_gain = attention_back(
        order,
        tables,
        first_weights,
        (pre, query_use, key_t, key_use, value_use, attended, log_total, normed),
        first_momentum,
        dbranch,
    )
    late_parts = lax.all_to_all(late.reshape(REPLICAS, LATE, D), PLANE, 0, 0)
    head_gains = jnp.concatenate([query_gain, key_gain], axis=1)
    other_gains, dpre, early_parts, hidden = lax.optimization_barrier(
        (over_core(head_gains), dpre, early_parts, hidden)
    )
    head_gains = 0.5 * (head_gains + other_gains)
    early_own = jnp.sum(early_parts.astype(f32), axis=0).astype(bf16)
    early_all = lax.all_gather(early_own, ("y", "c", "z"), axis=0, tiled=True)
    down_weight = second_weights[:384]
    out_away = dot(hidden[middle_rows:], down_weight).astype(bf16)
    out_half = dot(hidden[:middle_rows], down_weight) + over_core(out_away).astype(f32)
    in_weight = first_weights[: 4 * HD]
    away = t_dot(dpre[:, middle_rows:], in_weight).astype(bf16)
    half = t_dot(dpre[:, :middle_rows], in_weight) + over_core(away).astype(f32)
    dnormed = scatter_over_z(half)
    branch_out = scatter_over_z(out_half)
    late_parts, dnormed, branch_out, early_own = lax.optimization_barrier(
        (late_parts, dnormed, branch_out, early_own)
    )
    late_own = jnp.sum(late_parts.astype(f32), axis=0).astype(bf16)

    by_y = [late_own] + [lax.ppermute(late_own, "y", [(i, i ^ k) for i in range(4)]) for k in (3, 2, 1)]
    late_line = jnp.concatenate(by_y, axis=0)
    late_all, (dnormed, branch_out) = gather_blocks(late_line, (dnormed, branch_out))
    output = middle + branch_out
    dinput_norm, attn_gain_rows = norm_back(dnormed, inputs, scale_one, gain_attn)
    input_grad = dmiddle + dinput_norm
    gain_rows = jnp.concatenate(
        [
            jnp.sum(attn_gain_rows, axis=0),
            jnp.sum(mlp_gain_rows, axis=0),
            head_gains[:, 0],
            head_gains[:, 1],
            jnp.zeros((D - 2 * HD,), f32),
        ]
    ).reshape(3, D)
    gain_high = gain_rows.astype(bf16)
    gain_low = (gain_rows - gain_high.astype(f32)).astype(bf16)
    results = jnp.concatenate(
        [output.astype(bf16), input_grad.astype(bf16), gain_high, gain_low, jnp.zeros((2, D), bf16)], axis=0
    )
    results = trade(jnp.concatenate([early_own, late_own, results], axis=0), home)

    x_plane = xh * 2 + xl
    early_rows = lax.dynamic_index_in_dim(early_all.reshape(4, 8, EARLY, D), c * 4 + z, 1, False)
    early_rows = early_rows.reshape(REPLICAS, 3, 8, D)
    early_rows = pad_rows(lax.dynamic_index_in_dim(early_rows, jnp.minimum(y, 2), 1, False), PIECE)
    late_rows = jnp.stack([by_y[1], by_y[2], by_y[3], by_y[0]], axis=0)
    late_rows = jnp.where(
        (x_plane == 0) | (x_plane == 3),
        late_rows.reshape(REPLICAS, PIECE, D),
        pad_rows(late_rows[:, :32].reshape(REPLICAS, 8, D), PIECE),
    )
    own_rows = jnp.where(y == 3, late_rows, early_rows).reshape(REPLICAS * PIECE, D)
    early_gram = vmem_call(
        gram_kernel, (((D, D), f32),), (), (early_all,), 6 * 2**30, limit=24
    )[0]
    own_rows, early_gram, late_all, results = lax.optimization_barrier((own_rows, early_gram, late_all, results))
    results, sums = results[EARLY + LATE :], results[: EARLY + LATE]
    home_all = lax.all_gather(
        jnp.concatenate([sums, results[2 * BLOCK :]], axis=0), ("xl", "y", "c"), axis=0
    )
    orth = newton_schulz(y == 3, early_gram, own_rows, late_all)
    orth, weights = lax.optimization_barrier((orth, weights))

    mine = (jnp.arange(2) == c)[:, None, None, None]
    sent = jnp.where(mine, orth.reshape(1, REPLICAS, PIECE, D), 0).reshape(2 * REPLICAS, PIECE, D)
    pieces = lax.all_to_all(sent, ("xh", "xl", "y", "c"), 0, 0)

    output = results[:BLOCK]
    input_grad = jnp.where(home, input_grad, results[BLOCK : 2 * BLOCK].astype(f32))
    gain_all = home_all[:, EARLY + LATE :].astype(f32)
    gain_sum = jnp.sum(gain_all[:, :3] + gain_all[:, 3:6], axis=0)
    for axis, step, size in (("z", 1, 4), ("z", 2, 4), ("xh", 1, 2)):
        gain_sum = gain_sum + lax.ppermute(gain_sum, axis, [(i, i ^ step) for i in range(size)])
    gain_grad = gain_sum.reshape(3 * D)[: 2 * D + 2 * HD]
    new_first = adam_first * gain_first + (1.0 - adam_first) * gain_grad
    new_second = adam_second * gain_second + (1.0 - adam_second) * gain_grad * gain_grad
    step_first = new_first / (1.0 - adam_first**STEP)
    step_second = new_second / (1.0 - adam_second**STEP)
    new_gains = gains - gain_rate * step_first / (jnp.sqrt(step_second) + adam_epsilon)
    new_moments = vmem_call(
        momentum_kernel,
        tuple((m.shape, f32) for m in moments),
        ((home_all.shape, bf16),),
        (home_all,),
        10**6,
        0,
        14 * 2**20,
        fetched=1,
    )
    place = xl * 8 + y * 2 + c
    kept = []
    for i in range(7):
        axis = 0 if i in SPLIT_FIRST else 1
        per = weights[i].shape[axis] // REPLICAS
        part = lax.dynamic_slice_in_dim(weights[i], place * per, per, axis) * (1.0 - weight_shrink)
        kept.append(part.T if axis else part)
    pieces, new_moments, kept, new_gains = lax.optimization_barrier((pieces, new_moments, kept, new_gains))
    new_weights = vmem_call(
        weight_kernel,
        tuple((part.shape, f32) for part in kept),
        (),
        (xh.astype(jnp.int32).reshape(1), pieces, *kept),
        10**6,
        1,
        4 * 2**20,
    )
    new_weights = [w if i in SPLIT_FIRST else w.T for i, w in enumerate(new_weights)]
    return (output, input_grad, new_first, new_second, new_gains, *new_moments, *new_weights)


def solution(mesh):
    fine = Mesh(mesh.devices.reshape(2, 4, 2, 4, 2), ("xh", "z", "xl", "y", "c"))
    shard = ("xh", "z")
    replica = ("xl", "y", "c")
    rows = P(replica + shard, None)
    split = tuple(P(shard, None) if i in SPLIT_FIRST else P(None, shard) for i in range(7))
    pieces = tuple(
        P(shard + replica, None) if i in SPLIT_FIRST else P(None, shard + replica) for i in range(7)
    )
    in_specs = (rows, rows, P(replica, None), P(), P(), P()) + split + split
    out_specs = (rows, rows, P(), P(), P()) + split + pieces
    return jax.shard_map(shards, mesh=fine, in_specs=in_specs, out_specs=out_specs, check_vma=False)
```

```python
import math

import jax
import jax.numpy as jnp
from jax import lax
from jax.experimental import pallas as pl
from jax.experimental.pallas import tpu as pltpu
from jax.sharding import Mesh, PartitionSpec as P

D = 1024
H = 16
KV = 8
HD = 128
FF = 3072
NS_ITERS = 5
STEP = 10

norm_epsilon = 1e-06
rotary_base = 1000000.0
momentum_decay = 0.95
poly_first = 3.4445
poly_second = -4.775
poly_third = 2.0315
orth_epsilon = 1e-07
update_rate = 0.5
weight_shrink = 0.002
adam_first = 0.9
adam_second = 0.999
adam_epsilon = 1e-08
gain_rate = 0.8

f32 = jnp.float32
bf16 = jnp.bfloat16

PLANE = ("xh", "xl", "y")
REPLICAS = 16
BLOCK = 128
TOKENS = 8 * BLOCK
EARLY = 96
LATE = 64
PIECE = 16
FIRST_PACK = ((0, 256), (256, 128), (384, 128), (512, 256))
SECOND_PACK = ((0, 384), (384, 384), (768, 384))
SPLIT_FIRST = (3, 6)
FULL_SHAPES = ((D, H * HD), (D, KV * HD), (D, KV * HD), (H * HD, D), (D, FF), (D, FF), (FF, D))
SPREADS = (
    D ** (-0.5),
    D ** (-0.5),
    D ** (-0.5),
    max(H * HD // 256, 4) ** (-0.5),
    D ** (-0.5),
    D ** (-0.5),
    FF ** (-0.5),
)
RATES = tuple(update_rate * s * math.sqrt(max(f)) for s, f in zip(SPREADS, FULL_SHAPES))


def dot(a, b):
    return jnp.dot(a, b, preferred_element_type=f32)


def dot_t(a, b):
    return lax.dot_general(a, b, (((1,), (1,)), ((), ())), preferred_element_type=f32)


def t_dot(a, b):
    return lax.dot_general(a, b, (((0,), (0,)), ((), ())), preferred_element_type=f32)


def vmem_call(kernel, outs, scratch, operands, flops, scalars=0, bytes_accessed=8 * 2**20, limit=16, fetched=0):
    vmem, smem, anywhere = (pl.BlockSpec(memory_space=m) for m in (pltpu.VMEM, pltpu.SMEM, pl.ANY))
    scratch_shapes = [pltpu.VMEM(shape, dtype) for shape, dtype in scratch]
    if fetched:
        scratch_shapes.append(pltpu.SemaphoreType.DMA((fetched,)))
    return pl.pallas_call(
        kernel,
        out_shape=tuple(jax.ShapeDtypeStruct(shape, dtype) for shape, dtype in outs),
        in_specs=[smem] * scalars + [vmem] * (len(operands) - scalars - fetched) + [anywhere] * fetched,
        out_specs=tuple(vmem for _ in outs),
        scratch_shapes=scratch_shapes,
        compiler_params=pltpu.CompilerParams(vmem_limit_bytes=limit * 2**20),
        cost_estimate=pl.CostEstimate(flops=flops, bytes_accessed=bytes_accessed, transcendentals=0),
    )(*operands)


def fetch(sources, targets, sems, first=0):
    copies = [
        pltpu.make_async_copy(source, target, sems.at[first + i])
        for i, (source, target) in enumerate(zip(sources, targets))
    ]
    for copy in copies:
        copy.start()
    return copies


def wait(copies):
    for copy in copies:
        copy.wait()


def trade(x, home):
    other = lax.ppermute(x, ("xh", "c"), [(1, 2), (2, 1)])
    return jnp.where(home, x, other)


def trade_copied(x, home):
    other = lax.ppermute(x, ("xh", "c"), [(0, 2), (3, 1)])
    return jnp.where(home, x, other)


def over_z(x, k):
    return lax.ppermute(x, "z", [(i, i ^ k) for i in range(4)])


def over_core(x):
    return lax.ppermute(x, "c", [(0, 1), (1, 0)])


def gather_line(block, beside=()):
    near, far, across = (over_z(block, k) for k in (1, 3, 2))
    line = jnp.concatenate([block, near, across, far], axis=0)
    line, beside = lax.optimization_barrier((line, beside))
    return (line, over_core(line)), beside


def scatter_over_z(half):
    sent = half.astype(bf16)
    parts = [over_z(sent[k * BLOCK : (k + 1) * BLOCK], k) for k in (1, 3, 2)]
    return half[:BLOCK] + sum(part.astype(f32) for part in parts)


def rms_scale(values):
    return lax.rsqrt(jnp.mean(values * values, axis=-1, keepdims=True) + norm_epsilon)


def rotary_tables(position, head_width):
    half_width = head_width // 2
    freq_steps = jnp.arange(half_width, dtype=f32)
    inverse = rotary_base ** (-2.0 * freq_steps / head_width)
    angles = inverse[:, None] * position.astype(f32)[None, :]
    return (jnp.cos(angles), jnp.sin(angles))


def stream_layout(lengths_row, stream_rows):
    ends_at = jnp.cumsum(lengths_row)
    places = jnp.arange(stream_rows, dtype=jnp.int32)
    passed = (places[:, None] >= ends_at[None, :]).astype(jnp.int32)
    start = jnp.sum(passed * lengths_row[None, :], axis=1)
    return (start, places - start)


def norm_back(upstream, values, scale, gain):
    weighted = upstream * gain
    inner = jnp.mean(weighted * values, axis=-1, keepdims=True)
    grad_values = scale * (weighted - values * scale * scale * inner)
    return (grad_values, upstream * values * scale)


def pack_kernel(scale_ref, *refs):
    sources, (first_ref, second_ref), targets, sems = refs[:7], refs[7:9], refs[9:16], refs[16]
    copies = fetch(sources, targets, sems)
    scale = scale_ref[0]
    places = tuple((first_ref, *at) for at in FIRST_PACK) + tuple(
        (second_ref, *SECOND_PACK[i]) for i in (1, 2, 0)
    )
    for i, (out_ref, at, count) in enumerate(places):
        copies[i].wait()
        values = targets[i][...] * scale
        out_ref[at : at + count, :] = (values if i in SPLIT_FIRST else values.T).astype(bf16)


def pack(matrices, scale):
    return vmem_call(
        pack_kernel,
        (((768, D), bf16), ((1152, D), bf16)),
        tuple((m.shape, f32) for m in matrices),
        (jnp.asarray(scale, f32).reshape(1), *matrices),
        10**6,
        1,
        12 * 2**20,
        20,
        7,
    )


def turn(values, cosine, sine):
    front, back = values[: HD // 2], values[HD // 2 :]
    return jnp.concatenate([front * cosine - back * sine, back * cosine + front * sine], axis=0)


def column_scale(values):
    return lax.rsqrt(jnp.mean(values * values, axis=0, keepdims=True) + norm_epsilon)


def block_mask(start_ref, at, count, keys):
    key = lax.broadcasted_iota(jnp.int32, (keys, count), 0)
    token = at + lax.broadcasted_iota(jnp.int32, (keys, count), 1)
    allowed = (key >= start_ref[:, at : at + count]) & (key <= token)
    return jnp.concatenate([allowed, allowed], axis=1)


def both_heads(ref, at, count):
    return jnp.concatenate([ref[:HD, at : at + count], ref[HD : 2 * HD, at : at + count]], axis=1)


def in_order(order_ref, block):
    return pl.ds(pl.multiple_of(order_ref[block] * BLOCK, BLOCK), BLOCK)


def attention_kernel(order_ref, cosine_ref, sine_ref, start_ref, gain_query_ref, gain_key_ref, weight_ref, *refs):
    lines = refs[:2]
    pre_ref, query_ref, key_t_ref, key_ref, value_ref, attended_ref, attn_ref, log_ref, normed, value_t = refs[2:]
    for i in range(8):
        normed[in_order(order_ref, i), :] = lines[i // 4][i % 4 * BLOCK : (i % 4 + 1) * BLOCK, :]
    pre_ref[...] = dot_t(weight_ref[: 4 * HD, :], normed[...])
    cosine, sine = cosine_ref[...], sine_ref[...]
    for head in range(3):
        values = pre_ref[head * HD : (head + 1) * HD, :]
        gain = gain_query_ref[...] if head < 2 else gain_key_ref[...]
        turned_low = turn(values * column_scale(values) * gain, cosine, sine).astype(bf16)
        if head < 2:
            query_ref[head * HD : (head + 1) * HD, :] = turned_low
        else:
            key_t_ref[...] = turned_low
            key_ref[...] = turned_low.T
    low = pre_ref[3 * HD :, :].astype(bf16)
    value_t[...] = low
    value_ref[...] = low.T
    count = 2 * BLOCK
    for at in range(0, TOKENS, count):
        keys = at + count
        scores = dot(key_ref[:keys, :], both_heads(query_ref, at, count)) * HD ** (-0.5)
        masked = jnp.where(block_mask(start_ref, at, count, keys), scores, -1e30)
        peak = jnp.max(masked, axis=0, keepdims=True)
        raised = jnp.exp(masked - peak)
        total = jnp.sum(raised, axis=0, keepdims=True)
        probs = (raised * (1.0 / total)).astype(bf16)
        attended = dot(value_t[:, :keys], probs)
        log_total = peak + jnp.log(total)
        for head in range(2):
            span = slice(head * count, (head + 1) * count)
            attended_ref[head * HD : (head + 1) * HD, at:keys] = attended[:, span]
            log_ref[head : head + 1, at:keys] = log_total[:, span]
    for i in range(8):
        attn_ref[:, i * BLOCK : (i + 1) * BLOCK] = attended_ref[:, in_order(order_ref, i)].astype(bf16)


def attention(order, tables, weight, lines):
    outs = (
        ((4 * HD, TOKENS), f32),
        ((2 * HD, TOKENS), bf16),
        ((HD, TOKENS), bf16),
        ((TOKENS, HD), bf16),
        ((TOKENS, HD), bf16),
        ((2 * HD, TOKENS), f32),
        ((2 * HD, TOKENS), bf16),
        ((2, TOKENS), f32),
        ((TOKENS, D), bf16),
    )
    operands = (order, *tables, weight, *lines)
    return vmem_call(attention_kernel, outs, (((HD, TOKENS), bf16),), operands, 2 * 10**9, 1)


def norm_back_columns(upstream, values, gain):
    scale = column_scale(values)
    weighted = upstream * gain
    inner = jnp.mean(weighted * values, axis=0, keepdims=True)
    grad = scale * (weighted - values * (scale * scale * inner))
    return grad, jnp.sum(upstream * values * scale, axis=1, keepdims=True)


def attention_back_kernel(order_ref, cosine_ref, sine_ref, start_ref, gain_query_ref, gain_key_ref,
                          query_ref, key_t_ref, key_ref, value_ref, log_ref, weight_ref, *refs):
    lines, (attended_hbm, pre_hbm, normed_hbm, momentum_hbm) = refs[:2], refs[2:6]
    away_ref, kept_ref, late_ref, query_gain_ref, key_gain_ref = refs[6:11]
    dquery, dkey, dvalue, dattn_ref, dpre, dpre_blocks, dbranch = refs[11:18]
    attended_ref, pre_ref, normed, momentum_ref, sems = refs[18:]
    copies = fetch(
        (attended_hbm, pre_hbm, normed_hbm, momentum_hbm), (attended_ref, pre_ref, normed, momentum_ref), sems
    )
    for i in range(8):
        dbranch[in_order(order_ref, i), :] = lines[i // 4][i % 4 * BLOCK : (i % 4 + 1) * BLOCK, :]
    dattn_ref[...] = dot_t(weight_ref[4 * HD :, :], dbranch[...]).astype(bf16)
    copies[0].wait()
    dkey[...] = jnp.zeros_like(dkey)
    dvalue[...] = jnp.zeros_like(dvalue)
    count = 2 * BLOCK
    for at in range(0, TOKENS, count):
        keys = at + count
        query = both_heads(query_ref, at, count)
        dattn = both_heads(dattn_ref, at, count)
        row_dot = jnp.sum(dattn.astype(f32) * both_heads(attended_ref, at, count), axis=0, keepdims=True)
        log_total = jnp.concatenate([log_ref[:1, at:keys], log_ref[1:, at:keys]], axis=1)
        scores = dot(key_ref[:keys, :], query) * HD ** (-0.5)
        allowed = block_mask(start_ref, at, count, keys)
        probs = jnp.where(allowed, jnp.exp(scores - log_total), 0.0)
        dprobs = dot(value_ref[:keys, :], dattn)
        dscores = (probs * (dprobs - row_dot)).astype(bf16)
        grad = dot(key_t_ref[:, :keys], dscores)
        for head in range(2):
            dquery[head * HD : (head + 1) * HD, at:keys] = grad[:, head * count : (head + 1) * count]
        dkey[:, :keys] += dot_t(query, dscores)
        dvalue[:, :keys] += dot_t(dattn, probs.astype(bf16))
    wait(copies[1:])
    cosine, sine = cosine_ref[...], sine_ref[...]
    query_gain = jnp.zeros_like(query_gain_ref)
    for head in range(3):
        span = slice(head * HD, (head + 1) * HD)
        upstream = (dquery[span, :] if head < 2 else dkey[...]) * HD ** (-0.5)
        gain = gain_query_ref[...] if head < 2 else gain_key_ref[...]
        grad, gain_part = norm_back_columns(turn(upstream, cosine, -sine), pre_ref[span, :], gain)
        dpre[span, :] = grad.astype(bf16)
        if head < 2:
            query_gain = query_gain + gain_part
        else:
            key_gain_ref[...] = gain_part
    query_gain_ref[...] = query_gain
    dpre[3 * HD :, :] = dvalue[...].astype(bf16)
    for i in range(8):
        dpre_blocks[:, i * BLOCK : (i + 1) * BLOCK] = dpre[:, in_order(order_ref, i)]
    away_ref[...] = t_dot(dpre_blocks[:, TOKENS // 2 :], weight_ref[: 4 * HD, :]).astype(bf16)
    kept_ref[...] = t_dot(dpre_blocks[:, : TOKENS // 2], weight_ref[: 4 * HD, :])
    grads = dot(dpre[...], normed[...]) + momentum_ref[: 4 * HD, :].astype(f32)
    late_ref[:256, :] = grads[:256].astype(bf16)
    late_ref[256:768, :] = jnp.zeros((512, D), bf16)
    for i in range(4):
        late_ref[256 + 64 * i : 288 + 64 * i, :] = grads[256 + 32 * i : 288 + 32 * i].astype(bf16)
        late_ref[512 + 64 * i : 544 + 64 * i, :] = grads[384 + 32 * i : 416 + 32 * i].astype(bf16)
    out_grad = dot(attended_ref[...].astype(bf16), dbranch[...])
    late_ref[768:, :] = (out_grad + momentum_ref[4 * HD :, :].astype(f32)).astype(bf16)


def attention_back(order, tables, weight, kept, momentum, dbranch):
    pre, query, key_t, key, value, attended, log_total, normed = kept
    outs = (
        ((TOKENS // 2, D), bf16),
        ((TOKENS // 2, D), f32),
        ((REPLICAS * LATE, D), bf16),
        ((HD, 1), f32),
        ((HD, 1), f32),
    )
    scratch = (
        ((2 * HD, TOKENS), f32),
        ((HD, TOKENS), f32),
        ((HD, TOKENS), f32),
        ((2 * HD, TOKENS), bf16),
        ((4 * HD, TOKENS), bf16),
        ((4 * HD, TOKENS), bf16),
        ((TOKENS, D), bf16),
        (attended.shape, f32),
        (pre.shape, f32),
        (normed.shape, bf16),
        (momentum.shape, bf16),
    )
    operands = (order, *tables, query, key_t, key, value, log_total, weight, *dbranch, attended, pre, normed, momentum)
    return vmem_call(attention_back_kernel, outs, scratch, operands, 6 * 10**9, 1, limit=32, fetched=4)


def feed_forward_kernel(home_ref, order_ref, line_ref, other_ref, cot_ref, own_hbm, traded_hbm,
                        hidden_ref, grads_ref, away_ref, kept_ref, out_away_ref, out_kept_ref, normed, cot,
                        weight_ref, sems):
    @pl.when(home_ref[0] == 1)
    def _():
        pltpu.make_async_copy(own_hbm, weight_ref, sems.at[0]).start()

    @pl.when(home_ref[0] == 0)
    def _():
        pltpu.make_async_copy(traded_hbm, weight_ref, sems.at[0]).start()

    normed[: TOKENS // 2, :] = line_ref[...]
    normed[TOKENS // 2 :, :] = other_ref[...]
    for i in range(8):
        cot[i * BLOCK : (i + 1) * BLOCK, :] = cot_ref[in_order(order_ref, i), :]
    pltpu.make_async_copy(own_hbm, weight_ref, sems.at[0]).wait()
    width = SECOND_PACK[0][1]
    for part, out_ref, result_ref in ((1, away_ref, out_away_ref), (0, kept_ref, out_kept_ref)):
        span = slice(part * TOKENS // 2, (part + 1) * TOKENS // 2)
        both = dot_t(normed[span, :], weight_ref[width:, :])
        dhidden = dot_t(cot[span, :], weight_ref[:width, :])
        gate, upward = both[:, :width], both[:, width:]
        sigmoid_gate = jax.nn.sigmoid(gate)
        activated = gate * sigmoid_gate
        hidden_ref[span, :] = (activated * upward).astype(bf16)
        dgate = dhidden * upward * sigmoid_gate * (1.0 + gate * (1.0 - sigmoid_gate))
        grads_ref[span, :width] = dgate.astype(bf16)
        grads_ref[span, width:] = (dhidden * activated).astype(bf16)
        out_ref[...] = dot(grads_ref[span, :], weight_ref[width:, :]).astype(out_ref.dtype)
        result_ref[...] = dot(hidden_ref[span, :], weight_ref[:width, :]).astype(result_ref.dtype)


def feed_forward(home, order, normed, cot, own_weight, traded_weight):
    half = (TOKENS // 2, D)
    outs = (
        ((TOKENS, 384), bf16),
        ((TOKENS, 768), bf16),
        (half, bf16),
        (half, f32),
        (half, bf16),
        (half, f32),
        ((TOKENS, D), bf16),
        ((TOKENS, D), bf16),
    )
    operands = (home.astype(jnp.int32).reshape(1), order, *normed, cot, own_weight, traded_weight)
    scratch = ((own_weight.shape, bf16),)
    return vmem_call(feed_forward_kernel, outs, scratch, operands, 5 * 10**9, 2, fetched=2)


def early_kernel(hidden_ref, grads_ref, momentum_ref, normed, cot, out_ref):
    out_ref[:768, :] = (t_dot(grads_ref[...], normed[...]) + momentum_ref[384:, :].astype(f32)).astype(bf16)
    out_ref[768:1152, :] = (t_dot(hidden_ref[...], cot[...]) + momentum_ref[:384, :].astype(f32)).astype(bf16)
    out_ref[1152:, :] = jnp.zeros((384, D), bf16)


def early_gradients(*operands):
    return vmem_call(early_kernel, (((REPLICAS * EARLY, D), bf16),), (), operands, 3 * 10**9)[0]


def gram_kernel(rows_ref, out_ref):
    out_ref[...] = t_dot(rows_ref[...], rows_ref[...])


def newton_schulz_kernel(late_ref, rows_ref, gram_ref, line_ref, other_ref, out_ref, full, low, rest, once, rows):
    @pl.when(late_ref[0] == 0)
    def _():
        full[...] = gram_ref[...]

    @pl.when(late_ref[0] == 1)
    def _():
        full[...] = t_dot(line_ref[...], line_ref[...]) + t_dot(other_ref[...], other_ref[...])

    eye = lax.broadcasted_iota(jnp.int32, (128, 128), 0) == lax.broadcasted_iota(jnp.int32, (128, 128), 1)
    diagonal = jnp.zeros((128, 128), f32)
    for i in range(D // 128):
        span = slice(i * 128, (i + 1) * 128)
        diagonal = diagonal + jnp.where(eye, full[span, span], 0.0)
    total = jnp.sum(diagonal, axis=(0, 1), keepdims=True) + orth_epsilon
    inverse = lax.rsqrt(total)
    scaled = full[...] * (inverse * inverse)
    full[...] = scaled
    low[...] = scaled.astype(bf16)
    rows[...] = rows_ref[...].astype(f32) * inverse
    for iteration in range(NS_ITERS):
        rest[...] = (poly_second * full[...] + poly_third * dot(low[...], low[...])).astype(bf16)
        rows[...] = poly_first * rows[...] + dot(rows[...].astype(bf16), rest[...])
        if iteration + 1 < NS_ITERS:
            value = poly_first * full[...] + dot(rest[...], low[...])
            full[...] = value
            once[...] = value.astype(bf16)
            value = poly_first * full[...] + dot(rest[...], once[...])
            full[...] = value
            low[...] = value.astype(bf16)
    out_ref[...] = rows[...].astype(bf16)


def newton_schulz(is_late, early_gram, rows, late_parts):
    count = rows.shape[0]
    scratch = (
        ((D, D), f32),
        ((D, D), bf16),
        ((D, D), bf16),
        ((D, D), bf16),
        ((count, D), f32),
    )
    operands = (is_late.astype(jnp.int32).reshape(1), rows, early_gram, *late_parts)
    flops = 15 * 2 * D**3 + 10 * count * D * D
    return vmem_call(newton_schulz_kernel, (((count, D), bf16),), scratch, operands, flops, 1, limit=32)[0]


def momentum_kernel(all_hbm, q, k, v, o, g, u, d, all_ref, sems):
    wait(fetch((all_hbm,), (all_ref,), sems))

    def rows(column, at, count):
        entries = [(column % 2 * 4 + y) * 2 + column // 2 for y in range(4)]
        return jnp.concatenate([all_ref[entry, at : at + count, :] for entry in entries], axis=0).astype(f32)

    q[...] = rows(0, EARLY, 64).T
    k[...] = rows(1, EARLY, 32).T
    v[...] = rows(2, EARLY, 32).T
    o[...] = rows(3, EARLY, 64)
    g[...] = rows(0, 0, EARLY).T
    u[...] = rows(1, 0, EARLY).T
    d[...] = rows(2, 0, EARLY)


def weight_kernel(half_ref, pieces_ref, *refs):
    kept, outs = refs[:7], refs[7:]
    half = half_ref[0]

    def rows(column, ys, count):
        return jnp.concatenate(
            [pieces_ref[column * 8 + y * 2 + half][:count, :] for y in ys], axis=0
        ).astype(f32)

    late, early = (3,), (0, 1, 2)
    updates = (
        rows(0, late, 16),
        rows(1, late, 8),
        rows(2, late, 8),
        rows(3, late, 16),
        rows(0, early, 8),
        rows(1, early, 8),
        rows(2, early, 8),
    )
    for i in range(7):
        outs[i][...] = kept[i][...] - RATES[i] * updates[i]


def pad_rows(rows, count):
    return jnp.pad(rows, ((0, 0), (0, count - rows.shape[1]), (0, 0)))


def shards(tokens, cotangent, lengths, gains, gain_first, gain_second, *matrices):
    weights, moments = matrices[:7], matrices[7:]
    xh, z, xl, y, c = (lax.axis_index(a) for a in ("xh", "z", "xl", "y", "c"))
    home = xh == c
    gain_attn = gains[:D]
    gain_mlp = gains[D : 2 * D]
    gain_query = gains[2 * D : 2 * D + HD]
    gain_key = gains[2 * D + HD :]
    order = jnp.stack([(c ^ (i // 4)) * 4 + (z ^ (i % 4)) for i in range(8)]).astype(jnp.int32)

    codes = jnp.concatenate([lengths[0] // 32, lengths[0] % 32]).astype(bf16)
    codes = jnp.pad(codes[None], ((0, 15), (0, D - codes.shape[0])))
    first_weights, second_weights = pack(weights, 1.0)
    arrived = trade(jnp.concatenate([tokens, cotangent, codes], axis=0), home)
    arrived, first_weights, moments = lax.optimization_barrier((arrived, first_weights, moments))
    inputs = arrived[:BLOCK].astype(f32)
    scale_one = rms_scale(inputs)
    own_normed = (inputs * scale_one * gain_attn).astype(bf16)
    cot_own = arrived[BLOCK : 2 * BLOCK]
    codes = arrived[2 * BLOCK, :12].astype(jnp.int32)
    start, position = stream_layout(codes[:6] * 32 + codes[6:], TOKENS)
    first_weights = trade_copied(first_weights, home)
    tables = (*rotary_tables(position, HD), start[None, :], gain_query[:, None], gain_key[:, None])
    momenta = pack(moments, jnp.where(home, momentum_decay / 8, 0.0))
    normed, (first_weights, tables, cot_own, second_weights, momenta) = gather_line(
        own_normed, (first_weights, tables, cot_own, second_weights, momenta)
    )
    first_momentum, second_momentum = momenta

    cot = lax.all_gather(cot_own, ("c", "z"), axis=0, tiled=True)
    traded_weights = lax.ppermute(second_weights, ("xh", "c"), [(0, 2), (3, 1)])
    pre, query_use, key_t, key_use, value_use, attended, attn_use, log_total, normed = attention(
        order, tables, first_weights, normed
    )
    middle_rows = TOKENS // 2
    out_weight = first_weights[4 * HD :]
    away = t_dot(attn_use[:, middle_rows:], out_weight).astype(bf16)
    half = t_dot(attn_use[:, :middle_rows], out_weight) + over_core(away).astype(f32)
    middle = inputs + scatter_over_z(half)

    scale_two = rms_scale(middle)
    place = xl * 8 + y * 2 + c
    middle, weights = lax.optimization_barrier((middle, weights))
    own_parts = []
    for i in range(7):
        axis = 0 if i in SPLIT_FIRST else 1
        per = weights[i].shape[axis] // REPLICAS
        part = lax.dynamic_slice_in_dim(weights[i], place * per, per, axis) * (1.0 - weight_shrink)
        own_parts.append(part.T if axis else part)
    normed_two, own_parts = gather_line((middle * scale_two * gain_mlp).astype(bf16), own_parts)
    hidden, grads, away, kept, out_away, out_half, normed_two, cot = feed_forward(
        home, order, normed_two, cot, second_weights, traded_weights
    )
    early = early_gradients(hidden, grads, second_momentum, normed_two, cot)
    half, out_half, early = lax.optimization_barrier(
        (kept + over_core(away).astype(f32), out_half + over_core(out_away).astype(f32), early)
    )
    early_own = lax.psum_scatter(early, PLANE, scatter_dimension=0, tiled=True)
    dnormed_two = scatter_over_z(half)
    dmiddle_norm, mlp_gain_rows = norm_back(dnormed_two, middle, scale_two, gain_mlp)
    dmiddle = cot_own.astype(f32) + dmiddle_norm
    dbranch, _ = gather_line(dmiddle.astype(bf16))

    away, kept, late, query_gain, key_gain = attention_back(
        order,
        tables,
        first_weights,
        (pre, query_use, key_t, key_use, value_use, attended, log_total, normed),
        first_momentum,
        dbranch,
    )
    late_parts = lax.all_to_all(late.reshape(REPLICAS, LATE, D), PLANE, 0, 0)
    early_all = lax.all_gather(early_own, ("y", "c", "z"), axis=0, tiled=True)
    half = kept + over_core(away).astype(f32)
    dnormed = scatter_over_z(half)
    branch_out = scatter_over_z(out_half)
    late_parts, dnormed, branch_out = lax.optimization_barrier((late_parts, dnormed, branch_out))
    late_own = jnp.sum(late_parts.astype(f32), axis=0).astype(bf16)

    output = middle + branch_out
    dinput_norm, attn_gain_rows = norm_back(dnormed, inputs, scale_one, gain_attn)
    input_grad = dmiddle + dinput_norm
    gain_rows = jnp.concatenate(
        [
            jnp.sum(attn_gain_rows, axis=0),
            jnp.sum(mlp_gain_rows, axis=0),
            query_gain[:, 0],
            key_gain[:, 0],
            jnp.zeros((D - 2 * HD,), f32),
        ]
    ).reshape(3, D)
    gain_high = gain_rows.astype(bf16)
    gain_low = (gain_rows - gain_high.astype(f32)).astype(bf16)
    gain_rows = jnp.concatenate([gain_high, gain_low, jnp.zeros((2, D), bf16)], axis=0)
    by_y = [late_own] + [lax.ppermute(late_own, "y", [(i, i ^ k) for i in range(4)]) for k in (3, 2, 1)]
    late_line = jnp.concatenate(by_y, axis=0)

    x_plane = xh * 2 + xl
    early_rows = lax.dynamic_index_in_dim(early_all.reshape(4, 8, EARLY, D), c * 4 + z, 1, False)
    early_rows = early_rows.reshape(REPLICAS, 3, 8, D)
    early_rows = pad_rows(lax.dynamic_index_in_dim(early_rows, jnp.minimum(y, 2), 1, False), PIECE)
    late_rows = jnp.stack([by_y[1], by_y[2], by_y[3], by_y[0]], axis=0)
    late_rows = jnp.where(
        (x_plane == 0) | (x_plane == 3),
        late_rows.reshape(REPLICAS, PIECE, D),
        pad_rows(late_rows[:, :32].reshape(REPLICAS, 8, D), PIECE),
    )
    own_rows = jnp.where(y == 3, late_rows, early_rows).reshape(REPLICAS * PIECE, D)
    early_gram = vmem_call(gram_kernel, (((D, D), f32),), (), (early_all,), 6 * 2**30, limit=24)[0]
    late_all, (own_rows, early_gram, sums, results) = gather_line(
        late_line,
        (
            own_rows,
            early_gram,
            jnp.concatenate([early_own, late_own, gain_rows], axis=0),
            jnp.concatenate([output.astype(bf16), input_grad.astype(bf16)], axis=0),
        ),
    )
    sums = trade(sums, home)
    late_all, sums = lax.optimization_barrier((late_all, sums))
    home_all = lax.all_gather(sums, ("xl", "y", "c"), axis=0)
    results = trade(results, home)
    orth = newton_schulz(y == 3, early_gram, own_rows, late_all)

    mine = (jnp.arange(2) == c)[:, None, None, None]
    sent = jnp.where(mine, orth.reshape(1, REPLICAS, PIECE, D), 0).reshape(2 * REPLICAS, PIECE, D)
    pieces = lax.all_to_all(sent, ("xh", "xl", "y", "c"), 0, 0)

    output = results[:BLOCK]
    input_grad = jnp.where(home, input_grad, results[BLOCK : 2 * BLOCK].astype(f32))
    gain_all = home_all[:, EARLY + LATE :].astype(f32)
    gain_sum = jnp.sum(gain_all[:, :3] + gain_all[:, 3:6], axis=0)
    for axis, step, size in (("z", 1, 4), ("z", 2, 4), ("xh", 1, 2)):
        gain_sum = gain_sum + lax.ppermute(gain_sum, axis, [(i, i ^ step) for i in range(size)])
    gain_grad = gain_sum.reshape(3 * D)[: 2 * D + 2 * HD]
    new_first = adam_first * gain_first + (1.0 - adam_first) * gain_grad
    new_second = adam_second * gain_second + (1.0 - adam_second) * gain_grad * gain_grad
    step_first = new_first / (1.0 - adam_first**STEP)
    step_second = new_second / (1.0 - adam_second**STEP)
    new_gains = gains - gain_rate * step_first / (jnp.sqrt(step_second) + adam_epsilon)
    new_moments = vmem_call(
        momentum_kernel,
        tuple((m.shape, f32) for m in moments),
        ((home_all.shape, bf16),),
        (home_all,),
        10**6,
        0,
        14 * 2**20,
        fetched=1,
    )
    pieces, new_moments, new_gains = lax.optimization_barrier((pieces, new_moments, new_gains))
    new_weights = vmem_call(
        weight_kernel,
        tuple((part.shape, f32) for part in own_parts),
        (),
        (xh.astype(jnp.int32).reshape(1), pieces, *own_parts),
        10**6,
        1,
        4 * 2**20,
    )
    new_weights = [w if i in SPLIT_FIRST else w.T for i, w in enumerate(new_weights)]
    return (output, input_grad, new_first, new_second, new_gains, *new_moments, *new_weights)


def solution(mesh):
    fine = Mesh(mesh.devices.reshape(2, 4, 2, 4, 2), ("xh", "z", "xl", "y", "c"))
    shard = ("xh", "z")
    replica = ("xl", "y", "c")
    rows = P(replica + shard, None)
    split = tuple(P(shard, None) if i in SPLIT_FIRST else P(None, shard) for i in range(7))
    pieces = tuple(
        P(shard + replica, None) if i in SPLIT_FIRST else P(None, shard + replica) for i in range(7)
    )
    in_specs = (rows, rows, P(replica, None), P(), P(), P()) + split + split
    out_specs = (rows, rows, P(), P(), P()) + split + pieces
    return jax.shard_map(shards, mesh=fine, in_specs=in_specs, out_specs=out_specs, check_vma=False)
```

```python
import math

import jax
import jax.numpy as jnp
from jax import lax
from jax.experimental import pallas as pl
from jax.experimental.pallas import tpu as pltpu
from jax.sharding import Mesh, PartitionSpec as P

D = 1024
H = 16
KV = 8
HD = 128
FF = 3072
NS_ITERS = 5
STEP = 10

norm_epsilon = 1e-06
rotary_base = 1000000.0
momentum_decay = 0.95
poly_first = 3.4445
poly_second = -4.775
poly_third = 2.0315
orth_epsilon = 1e-07
update_rate = 0.5
weight_shrink = 0.002
adam_first = 0.9
adam_second = 0.999
adam_epsilon = 1e-08
gain_rate = 0.8

f32 = jnp.float32
bf16 = jnp.bfloat16

PLANE = ("xh", "xl", "y")
REPLICAS = 16
BLOCK = 128
TOKENS = 8 * BLOCK
EARLY = 96
LATE = 64
PIECE = 16
FIRST_PACK = ((0, 256), (256, 128), (384, 128), (512, 256))
SECOND_PACK = ((0, 384), (384, 384), (768, 384))
SPLIT_FIRST = (3, 6)
FULL_SHAPES = ((D, H * HD), (D, KV * HD), (D, KV * HD), (H * HD, D), (D, FF), (D, FF), (FF, D))
SPREADS = (
    D ** (-0.5),
    D ** (-0.5),
    D ** (-0.5),
    max(H * HD // 256, 4) ** (-0.5),
    D ** (-0.5),
    D ** (-0.5),
    FF ** (-0.5),
)
RATES = tuple(update_rate * s * math.sqrt(max(f)) for s, f in zip(SPREADS, FULL_SHAPES))


def dot(a, b):
    return jnp.dot(a, b, preferred_element_type=f32)


def dot_t(a, b):
    return lax.dot_general(a, b, (((1,), (1,)), ((), ())), preferred_element_type=f32)


def t_dot(a, b):
    return lax.dot_general(a, b, (((0,), (0,)), ((), ())), preferred_element_type=f32)


def vmem_call(kernel, outs, scratch, operands, flops, scalars=0, bytes_accessed=8 * 2**20, limit=16, fetched=0, stored=0):
    vmem, smem, anywhere = (pl.BlockSpec(memory_space=m) for m in (pltpu.VMEM, pltpu.SMEM, pl.ANY))
    scratch_shapes = [pltpu.VMEM(shape, dtype) for shape, dtype in scratch]
    if fetched + stored:
        scratch_shapes.append(pltpu.SemaphoreType.DMA((fetched + stored,)))
    return pl.pallas_call(
        kernel,
        out_shape=tuple(jax.ShapeDtypeStruct(shape, dtype) for shape, dtype in outs),
        in_specs=[smem] * scalars + [vmem] * (len(operands) - scalars - fetched) + [anywhere] * fetched,
        out_specs=(vmem,) * (len(outs) - stored) + (anywhere,) * stored,
        scratch_shapes=scratch_shapes,
        compiler_params=pltpu.CompilerParams(vmem_limit_bytes=limit * 2**20),
        cost_estimate=pl.CostEstimate(flops=flops, bytes_accessed=bytes_accessed, transcendentals=0),
    )(*operands)


def fetch(sources, targets, sems, first=0):
    copies = [
        pltpu.make_async_copy(source, target, sems.at[first + i])
        for i, (source, target) in enumerate(zip(sources, targets))
    ]
    for copy in copies:
        copy.start()
    return copies


def wait(copies):
    for copy in copies:
        copy.wait()


def trade(x, home):
    other = lax.ppermute(x, ("xh", "c"), [(1, 2), (2, 1)])
    return jnp.where(home, x, other)


def trade_copied(x, home):
    other = lax.ppermute(x, ("xh", "c"), [(0, 2), (3, 1)])
    return jnp.where(home, x, other)


def over_z(x, k):
    return lax.ppermute(x, "z", [(i, i ^ k) for i in range(4)])


def over_core(x):
    return lax.ppermute(x, "c", [(0, 1), (1, 0)])


def gather_line(block, beside=()):
    near, far, across = (over_z(block, k) for k in (1, 3, 2))
    line = jnp.concatenate([block, near, across, far], axis=0)
    line, beside = lax.optimization_barrier((line, beside))
    return (line, over_core(line)), beside


def scatter_over_z(half):
    sent = half.astype(bf16)
    parts = [over_z(sent[k * BLOCK : (k + 1) * BLOCK], k) for k in (1, 3, 2)]
    return half[:BLOCK] + sum(part.astype(f32) for part in parts)


def rms_scale(values):
    return lax.rsqrt(jnp.mean(values * values, axis=-1, keepdims=True) + norm_epsilon)


def rotary_tables(position, head_width):
    half_width = head_width // 2
    freq_steps = jnp.arange(half_width, dtype=f32)
    inverse = rotary_base ** (-2.0 * freq_steps / head_width)
    angles = inverse[:, None] * position.astype(f32)[None, :]
    return (jnp.cos(angles), jnp.sin(angles))


def stream_layout(lengths_row, stream_rows):
    ends_at = jnp.cumsum(lengths_row)
    places = jnp.arange(stream_rows, dtype=jnp.int32)
    passed = (places[:, None] >= ends_at[None, :]).astype(jnp.int32)
    start = jnp.sum(passed * lengths_row[None, :], axis=1)
    return (start, places - start)


def norm_back(upstream, values, scale, gain):
    weighted = upstream * gain
    inner = jnp.mean(weighted * values, axis=-1, keepdims=True)
    grad_values = scale * (weighted - values * scale * scale * inner)
    return (grad_values, upstream * values * scale)


def pack_kernel(scale_ref, *refs):
    sources, (first_ref, second_ref), targets, sems = refs[:7], refs[7:9], refs[9:16], refs[16]
    copies = fetch(sources, targets, sems)
    scale = scale_ref[0]
    places = tuple((first_ref, *at) for at in FIRST_PACK) + tuple(
        (second_ref, *SECOND_PACK[i]) for i in (1, 2, 0)
    )
    for i, (out_ref, at, count) in enumerate(places):
        copies[i].wait()
        values = targets[i][...] * scale
        out_ref[at : at + count, :] = (values if i in SPLIT_FIRST else values.T).astype(bf16)


def pack(matrices, scale):
    return vmem_call(
        pack_kernel,
        (((768, D), bf16), ((1152, D), bf16)),
        tuple((m.shape, f32) for m in matrices),
        (jnp.asarray(scale, f32).reshape(1), *matrices),
        10**6,
        1,
        12 * 2**20,
        20,
        7,
    )


def turn(values, cosine, sine):
    front, back = values[: HD // 2], values[HD // 2 :]
    return jnp.concatenate([front * cosine - back * sine, back * cosine + front * sine], axis=0)


def column_scale(values):
    return lax.rsqrt(jnp.mean(values * values, axis=0, keepdims=True) + norm_epsilon)


def block_mask(start_ref, at, count, keys):
    key = lax.broadcasted_iota(jnp.int32, (keys, count), 0)
    token = at + lax.broadcasted_iota(jnp.int32, (keys, count), 1)
    allowed = (key >= start_ref[:, at : at + count]) & (key <= token)
    return jnp.concatenate([allowed, allowed], axis=1)


def both_heads(ref, at, count):
    return jnp.concatenate([ref[:HD, at : at + count], ref[HD : 2 * HD, at : at + count]], axis=1)


def in_order(order_ref, block):
    return pl.ds(pl.multiple_of(order_ref[block] * BLOCK, BLOCK), BLOCK)


def attention_kernel(order_ref, cosine_ref, sine_ref, start_ref, gain_query_ref, gain_key_ref, weight_ref, *refs):
    lines, (query_ref, key_t_ref, key_ref, value_ref, log_ref, away_ref, kept_ref) = refs[:2], refs[2:9]
    stores, (pre_ref, attended_ref, normed, value_t, attn, sems) = refs[9:12], refs[12:]
    for i in range(8):
        normed[in_order(order_ref, i), :] = lines[i // 4][i % 4 * BLOCK : (i % 4 + 1) * BLOCK, :]
    copies = fetch((normed,), stores[2:], sems)
    pre_ref[...] = dot_t(weight_ref[: 4 * HD, :], normed[...])
    copies += fetch((pre_ref,), stores[:1], sems, 1)
    cosine, sine = cosine_ref[...], sine_ref[...]
    for head in range(3):
        values = pre_ref[head * HD : (head + 1) * HD, :]
        gain = gain_query_ref[...] if head < 2 else gain_key_ref[...]
        turned_low = turn(values * column_scale(values) * gain, cosine, sine).astype(bf16)
        if head < 2:
            query_ref[head * HD : (head + 1) * HD, :] = turned_low
        else:
            key_t_ref[...] = turned_low
            key_ref[...] = turned_low.T
    low = pre_ref[3 * HD :, :].astype(bf16)
    value_t[...] = low
    value_ref[...] = low.T
    count = 2 * BLOCK
    for at in range(0, TOKENS, count):
        keys = at + count
        scores = dot(key_ref[:keys, :], both_heads(query_ref, at, count)) * HD ** (-0.5)
        masked = jnp.where(block_mask(start_ref, at, count, keys), scores, -1e30)
        peak = jnp.max(masked, axis=0, keepdims=True)
        raised = jnp.exp(masked - peak)
        total = jnp.sum(raised, axis=0, keepdims=True)
        probs = (raised * (1.0 / total)).astype(bf16)
        attended = dot(value_t[:, :keys], probs)
        log_total = peak + jnp.log(total)
        for head in range(2):
            span = slice(head * count, (head + 1) * count)
            attended_ref[head * HD : (head + 1) * HD, at:keys] = attended[:, span]
            log_ref[head : head + 1, at:keys] = log_total[:, span]
    copies += fetch((attended_ref,), stores[1:2], sems, 2)
    for i in range(8):
        attn[:, i * BLOCK : (i + 1) * BLOCK] = attended_ref[:, in_order(order_ref, i)].astype(bf16)
    away_ref[...] = t_dot(attn[:, TOKENS // 2 :], weight_ref[4 * HD :, :]).astype(bf16)
    kept_ref[...] = t_dot(attn[:, : TOKENS // 2], weight_ref[4 * HD :, :])
    wait(copies)


def attention(order, tables, weight, lines):
    outs = (
        ((2 * HD, TOKENS), bf16),
        ((HD, TOKENS), bf16),
        ((TOKENS, HD), bf16),
        ((TOKENS, HD), bf16),
        ((2, TOKENS), f32),
        ((TOKENS // 2, D), bf16),
        ((TOKENS // 2, D), f32),
        ((4 * HD, TOKENS), f32),
        ((2 * HD, TOKENS), f32),
        ((TOKENS, D), bf16),
    )
    scratch = (
        ((4 * HD, TOKENS), f32),
        ((2 * HD, TOKENS), f32),
        ((TOKENS, D), bf16),
        ((HD, TOKENS), bf16),
        ((2 * HD, TOKENS), bf16),
    )
    operands = (order, *tables, weight, *lines)
    return vmem_call(attention_kernel, outs, scratch, operands, 3 * 10**9, 1, limit=20, stored=3)


def norm_back_columns(upstream, values, gain):
    scale = column_scale(values)
    weighted = upstream * gain
    inner = jnp.mean(weighted * values, axis=0, keepdims=True)
    grad = scale * (weighted - values * (scale * scale * inner))
    return grad, jnp.sum(upstream * values * scale, axis=1, keepdims=True)


def attention_back_kernel(order_ref, cosine_ref, sine_ref, start_ref, gain_query_ref, gain_key_ref,
                          query_ref, key_t_ref, key_ref, value_ref, log_ref, gain_attn_ref, weight_ref, *refs):
    lines, (attended_hbm, pre_hbm, normed_hbm, momentum_hbm) = refs[:2], refs[2:6]
    away_ref, kept_ref, late_ref, query_gain_ref, key_gain_ref, attn_gain_ref = refs[6:12]
    dquery, dkey, dvalue, dattn_ref, dpre, dpre_blocks, dbranch = refs[12:19]
    attended_ref, pre_ref, normed, momentum_ref, sems = refs[19:]
    copies = fetch(
        (attended_hbm, pre_hbm, normed_hbm, momentum_hbm), (attended_ref, pre_ref, normed, momentum_ref), sems
    )
    for i in range(8):
        dbranch[in_order(order_ref, i), :] = lines[i // 4][i % 4 * BLOCK : (i % 4 + 1) * BLOCK, :]
    dattn_ref[...] = dot_t(weight_ref[4 * HD :, :], dbranch[...]).astype(bf16)
    copies[0].wait()
    dkey[...] = jnp.zeros_like(dkey)
    dvalue[...] = jnp.zeros_like(dvalue)
    count = 2 * BLOCK
    for at in range(0, TOKENS, count):
        keys = at + count
        query = both_heads(query_ref, at, count)
        dattn = both_heads(dattn_ref, at, count)
        row_dot = jnp.sum(dattn.astype(f32) * both_heads(attended_ref, at, count), axis=0, keepdims=True)
        log_total = jnp.concatenate([log_ref[:1, at:keys], log_ref[1:, at:keys]], axis=1)
        scores = dot(key_ref[:keys, :], query) * HD ** (-0.5)
        allowed = block_mask(start_ref, at, count, keys)
        probs = jnp.where(allowed, jnp.exp(scores - log_total), 0.0)
        dprobs = dot(value_ref[:keys, :], dattn)
        dscores = (probs * (dprobs - row_dot)).astype(bf16)
        grad = dot(key_t_ref[:, :keys], dscores)
        for head in range(2):
            dquery[head * HD : (head + 1) * HD, at:keys] = grad[:, head * count : (head + 1) * count]
        dkey[:, :keys] += dot_t(query, dscores)
        dvalue[:, :keys] += dot_t(dattn, probs.astype(bf16))
    wait(copies[1:])
    cosine, sine = cosine_ref[...], sine_ref[...]
    query_gain = jnp.zeros_like(query_gain_ref)
    for head in range(3):
        span = slice(head * HD, (head + 1) * HD)
        upstream = (dquery[span, :] if head < 2 else dkey[...]) * HD ** (-0.5)
        gain = gain_query_ref[...] if head < 2 else gain_key_ref[...]
        grad, gain_part = norm_back_columns(turn(upstream, cosine, -sine), pre_ref[span, :], gain)
        dpre[span, :] = grad.astype(bf16)
        if head < 2:
            query_gain = query_gain + gain_part
        else:
            key_gain_ref[...] = gain_part
    query_gain_ref[...] = query_gain
    dpre[3 * HD :, :] = dvalue[...].astype(bf16)
    for i in range(8):
        dpre_blocks[:, i * BLOCK : (i + 1) * BLOCK] = dpre[:, in_order(order_ref, i)]
    away_ref[...] = t_dot(dpre_blocks[:, TOKENS // 2 :], weight_ref[: 4 * HD, :]).astype(bf16)
    kept_ref[...] = t_dot(dpre_blocks[:, : TOKENS // 2], weight_ref[: 4 * HD, :])
    grads = dot(dpre[...], normed[...])
    weighted = weight_ref[: 4 * HD, :].astype(f32) * grads
    attn_gain_ref[...] = jnp.sum(weighted, axis=0, keepdims=True) / gain_attn_ref[...]
    grads = grads + momentum_ref[: 4 * HD, :].astype(f32)
    late_ref[:256, :] = grads[:256].astype(bf16)
    late_ref[256:768, :] = jnp.zeros((512, D), bf16)
    for i in range(4):
        late_ref[256 + 64 * i : 288 + 64 * i, :] = grads[256 + 32 * i : 288 + 32 * i].astype(bf16)
        late_ref[512 + 64 * i : 544 + 64 * i, :] = grads[384 + 32 * i : 416 + 32 * i].astype(bf16)
    out_grad = dot(attended_ref[...].astype(bf16), dbranch[...])
    late_ref[768:, :] = (out_grad + momentum_ref[4 * HD :, :].astype(f32)).astype(bf16)


def attention_back(order, tables, gain_attn, weight, kept, momentum, dbranch):
    pre, query, key_t, key, value, attended, log_total, normed = kept
    outs = (
        ((TOKENS // 2, D), bf16),
        ((TOKENS // 2, D), f32),
        ((REPLICAS * LATE, D), bf16),
        ((HD, 1), f32),
        ((HD, 1), f32),
        ((1, D), f32),
    )
    scratch = (
        ((2 * HD, TOKENS), f32),
        ((HD, TOKENS), f32),
        ((HD, TOKENS), f32),
        ((2 * HD, TOKENS), bf16),
        ((4 * HD, TOKENS), bf16),
        ((4 * HD, TOKENS), bf16),
        ((TOKENS, D), bf16),
        (attended.shape, f32),
        (pre.shape, f32),
        (normed.shape, bf16),
        (momentum.shape, bf16),
    )
    operands = (
        *(order, *tables, query, key_t, key, value, log_total, gain_attn, weight),
        *(*dbranch, attended, pre, normed, momentum),
    )
    return vmem_call(attention_back_kernel, outs, scratch, operands, 6 * 10**9, 1, limit=32, fetched=4)


def feed_forward_kernel(home_ref, line_ref, other_ref, cot_line_ref, cot_other_ref, own_hbm, traded_hbm,
                        hidden_ref, grads_ref, away_ref, kept_ref, out_away_ref, out_kept_ref, normed, cot,
                        weight_ref, sems):
    @pl.when(home_ref[0] == 1)
    def _():
        pltpu.make_async_copy(own_hbm, weight_ref, sems.at[0]).start()

    @pl.when(home_ref[0] == 0)
    def _():
        pltpu.make_async_copy(traded_hbm, weight_ref, sems.at[0]).start()

    normed[: TOKENS // 2, :] = line_ref[...]
    normed[TOKENS // 2 :, :] = other_ref[...]
    cot[: TOKENS // 2, :] = cot_line_ref[...]
    cot[TOKENS // 2 :, :] = cot_other_ref[...]
    pltpu.make_async_copy(own_hbm, weight_ref, sems.at[0]).wait()
    width = SECOND_PACK[0][1]
    for part, out_ref, result_ref in ((1, away_ref, out_away_ref), (0, kept_ref, out_kept_ref)):
        span = slice(part * TOKENS // 2, (part + 1) * TOKENS // 2)
        both = dot_t(normed[span, :], weight_ref[width:, :])
        dhidden = dot_t(cot[span, :], weight_ref[:width, :])
        gate, upward = both[:, :width], both[:, width:]
        sigmoid_gate = jax.nn.sigmoid(gate)
        activated = gate * sigmoid_gate
        hidden_ref[span, :] = (activated * upward).astype(bf16)
        dgate = dhidden * upward * sigmoid_gate * (1.0 + gate * (1.0 - sigmoid_gate))
        grads_ref[span, :width] = dgate.astype(bf16)
        grads_ref[span, width:] = (dhidden * activated).astype(bf16)
        out_ref[...] = dot(grads_ref[span, :], weight_ref[width:, :]).astype(out_ref.dtype)
        result_ref[...] = dot(hidden_ref[span, :], weight_ref[:width, :]).astype(result_ref.dtype)


def feed_forward(home, normed, cot, own_weight, traded_weight):
    half = (TOKENS // 2, D)
    outs = (
        ((TOKENS, 384), bf16),
        ((TOKENS, 768), bf16),
        (half, bf16),
        (half, f32),
        (half, bf16),
        (half, f32),
        ((TOKENS, D), bf16),
        ((TOKENS, D), bf16),
    )
    operands = (home.astype(jnp.int32).reshape(1), *normed, *cot, own_weight, traded_weight)
    scratch = ((own_weight.shape, bf16),)
    return vmem_call(feed_forward_kernel, outs, scratch, operands, 5 * 10**9, 1, fetched=2)


def early_kernel(hidden_ref, grads_ref, momentum_ref, normed, cot, out_ref):
    out_ref[:768, :] = (t_dot(grads_ref[...], normed[...]) + momentum_ref[384:, :].astype(f32)).astype(bf16)
    out_ref[768:1152, :] = (t_dot(hidden_ref[...], cot[...]) + momentum_ref[:384, :].astype(f32)).astype(bf16)
    out_ref[1152:, :] = jnp.zeros((384, D), bf16)


def early_gradients(*operands):
    return vmem_call(early_kernel, (((REPLICAS * EARLY, D), bf16),), (), operands, 3 * 10**9)[0]


def gram_kernel(rows_ref, out_ref):
    out_ref[...] = t_dot(rows_ref[...], rows_ref[...])


def choose_gram_kernel(late_ref, gram_ref, line_ref, out_ref):
    @pl.when(late_ref[0] == 0)
    def _():
        out_ref[...] = gram_ref[...]

    @pl.when(late_ref[0] == 1)
    def _():
        out_ref[...] = t_dot(line_ref[...], line_ref[...])


def newton_schulz_kernel(late_ref, rows_ref, gram_ref, other_ref, out_ref, full, low, rest, once, rows):
    full[...] = gram_ref[...]

    @pl.when(late_ref[0] == 1)
    def _():
        full[...] += t_dot(other_ref[...], other_ref[...])

    eye = lax.broadcasted_iota(jnp.int32, (128, 128), 0) == lax.broadcasted_iota(jnp.int32, (128, 128), 1)
    diagonal = jnp.zeros((128, 128), f32)
    for i in range(D // 128):
        span = slice(i * 128, (i + 1) * 128)
        diagonal = diagonal + jnp.where(eye, full[span, span], 0.0)
    total = jnp.sum(diagonal, axis=(0, 1), keepdims=True) + orth_epsilon
    inverse = lax.rsqrt(total)
    scaled = full[...] * (inverse * inverse)
    full[...] = scaled
    low[...] = scaled.astype(bf16)
    rows[...] = rows_ref[...].astype(f32) * inverse
    for iteration in range(NS_ITERS):
        rest[...] = (poly_second * full[...] + poly_third * dot(low[...], low[...])).astype(bf16)
        rows[...] = poly_first * rows[...] + dot(rows[...].astype(bf16), rest[...])
        if iteration + 1 < NS_ITERS:
            value = poly_first * full[...] + dot(rest[...], low[...])
            full[...] = value
            once[...] = value.astype(bf16)
            value = poly_first * full[...] + dot(rest[...], once[...])
            full[...] = value
            low[...] = value.astype(bf16)
    out_ref[...] = rows[...].astype(bf16)


def newton_schulz(is_late, gram, rows, late_rows):
    count = rows.shape[0]
    scratch = (
        ((D, D), f32),
        ((D, D), bf16),
        ((D, D), bf16),
        ((D, D), bf16),
        ((count, D), f32),
    )
    operands = (is_late, rows, gram, late_rows)
    flops = 15 * 2 * D**3 + 10 * count * D * D
    return vmem_call(newton_schulz_kernel, (((count, D), bf16),), scratch, operands, flops, 1, limit=32)[0]


def momentum_kernel(all_hbm, q, k, v, o, g, u, d, all_ref, sems):
    wait(fetch((all_hbm,), (all_ref,), sems))

    def rows(column, at, count):
        entries = [(column % 2 * 4 + y) * 2 + column // 2 for y in range(4)]
        return jnp.concatenate([all_ref[entry, at : at + count, :] for entry in entries], axis=0).astype(f32)

    q[...] = rows(0, EARLY, 64).T
    k[...] = rows(1, EARLY, 32).T
    v[...] = rows(2, EARLY, 32).T
    o[...] = rows(3, EARLY, 64)
    g[...] = rows(0, 0, EARLY).T
    u[...] = rows(1, 0, EARLY).T
    d[...] = rows(2, 0, EARLY)


def weight_kernel(half_ref, pieces_ref, *refs):
    kept, outs = refs[:7], refs[7:]
    half = half_ref[0]

    def rows(column, ys, count):
        return jnp.concatenate(
            [pieces_ref[column * 8 + y * 2 + half][:count, :] for y in ys], axis=0
        ).astype(f32)

    late, early = (3,), (0, 1, 2)
    updates = (
        rows(0, late, 16),
        rows(1, late, 8),
        rows(2, late, 8),
        rows(3, late, 16),
        rows(0, early, 8),
        rows(1, early, 8),
        rows(2, early, 8),
    )
    for i in range(7):
        outs[i][...] = kept[i][...] - RATES[i] * updates[i]


def pad_rows(rows, count):
    return jnp.pad(rows, ((0, 0), (0, count - rows.shape[1]), (0, 0)))


def shards(tokens, cotangent, lengths, gains, gain_first, gain_second, *matrices):
    weights, moments = matrices[:7], matrices[7:]
    xh, z, xl, y, c = (lax.axis_index(a) for a in ("xh", "z", "xl", "y", "c"))
    home = xh == c
    gain_attn = gains[:D]
    gain_mlp = gains[D : 2 * D]
    gain_query = gains[2 * D : 2 * D + HD]
    gain_key = gains[2 * D + HD :]
    order = jnp.stack([(c ^ (i // 4)) * 4 + (z ^ (i % 4)) for i in range(8)]).astype(jnp.int32)

    codes = jnp.concatenate([lengths[0] // 32, lengths[0] % 32]).astype(bf16)
    codes = jnp.pad(codes[None], ((0, 15), (0, D - codes.shape[0])))
    first_weights, second_weights = pack(weights, 1.0)
    arrived = trade(jnp.concatenate([tokens, cotangent, codes], axis=0), home)
    arrived, first_weights, moments = lax.optimization_barrier((arrived, first_weights, moments))
    inputs = arrived[:BLOCK].astype(f32)
    scale_one = rms_scale(inputs)
    own_normed = (inputs * scale_one * gain_attn).astype(bf16)
    cot_own = arrived[BLOCK : 2 * BLOCK]
    codes = arrived[2 * BLOCK, :12].astype(jnp.int32)
    start, position = stream_layout(codes[:6] * 32 + codes[6:], TOKENS)
    first_weights = trade_copied(first_weights, home)
    tables = (*rotary_tables(position, HD), start[None, :], gain_query[:, None], gain_key[:, None])
    momenta = pack(moments, jnp.where(home, momentum_decay / 8, 0.0))
    both = jnp.concatenate([own_normed, cot_own], axis=0)
    near, far, across = (over_z(both, k) for k in (1, 3, 2))
    parts = (both, near, across, far)
    line = jnp.concatenate([part[:BLOCK] for part in parts], axis=0)
    cot_line = jnp.concatenate([part[BLOCK:] for part in parts], axis=0)
    line, cot_line, first_weights, tables, second_weights, momenta = lax.optimization_barrier(
        (line, cot_line, first_weights, tables, second_weights, momenta)
    )
    first_momentum, second_momentum = momenta

    traded_weights = lax.ppermute(second_weights, ("xh", "c"), [(0, 2), (3, 1)])
    query_use, key_t, key_use, value_use, log_total, away, kept, pre, attended, normed = attention(
        order, tables, first_weights, (line, over_core(line))
    )
    cot = (cot_line, over_core(cot_line))
    half = kept + over_core(away).astype(f32)
    middle = inputs + scatter_over_z(half)

    scale_two = rms_scale(middle)
    place = xl * 8 + y * 2 + c
    middle, weights = lax.optimization_barrier((middle, weights))
    own_parts = []
    for i in range(7):
        axis = 0 if i in SPLIT_FIRST else 1
        per = weights[i].shape[axis] // REPLICAS
        part = lax.dynamic_slice_in_dim(weights[i], place * per, per, axis) * (1.0 - weight_shrink)
        own_parts.append(part.T if axis else part)
    normed_two, own_parts = gather_line((middle * scale_two * gain_mlp).astype(bf16), own_parts)
    hidden, grads, away, kept, out_away, out_half, normed_two, cot = feed_forward(
        home, normed_two, cot, second_weights, traded_weights
    )
    early = early_gradients(hidden, grads, second_momentum, normed_two, cot)
    half, early = lax.optimization_barrier((kept + over_core(away).astype(f32), early))
    early_parts = lax.all_to_all(early.reshape(REPLICAS, EARLY, D), PLANE, 0, 0)
    dnormed_two = scatter_over_z(half)
    dmiddle_norm, mlp_gain_rows = norm_back(dnormed_two, middle, scale_two, gain_mlp)
    dmiddle = cot_own.astype(f32) + dmiddle_norm
    dbranch, early_own = gather_line(
        dmiddle.astype(bf16), jnp.sum(early_parts.astype(f32), axis=0).astype(bf16)
    )
    early_all = lax.all_gather(early_own, ("y", "c", "z"), axis=0, tiled=True)

    away, kept, late, query_gain, key_gain, attn_gain = attention_back(
        order,
        tables,
        gain_attn[None, :],
        first_weights,
        (pre, query_use, key_t, key_use, value_use, attended, log_total, normed),
        first_momentum,
        dbranch,
    )
    late_parts = lax.all_to_all(late.reshape(REPLICAS, LATE, D), PLANE, 0, 0)
    half, out_away, out_half = lax.optimization_barrier(
        (kept + over_core(away).astype(f32), out_away, out_half)
    )
    dnormed = scatter_over_z(half)
    branch_out = scatter_over_z(out_half + over_core(out_away).astype(f32))
    gain_rows = jnp.concatenate(
        [
            attn_gain[0],
            jnp.sum(mlp_gain_rows, axis=0),
            query_gain[:, 0],
            key_gain[:, 0],
            jnp.zeros((D - 2 * HD,), f32),
        ]
    ).reshape(3, D)
    for axis, step, size in (("z", 1, 4), ("z", 2, 4), ("c", 1, 2)):
        gain_rows = gain_rows + lax.ppermute(gain_rows, axis, [(i, i ^ step) for i in range(size)])
    gain_high = gain_rows.astype(bf16)
    gain_low = (gain_rows - gain_high.astype(f32)).astype(bf16)
    gain_rows = jnp.concatenate([gain_high, gain_low, jnp.zeros((2, D), bf16)], axis=0)
    early_home = trade(jnp.concatenate([early_own, gain_rows], axis=0), home)
    early_gram = vmem_call(gram_kernel, (((D, D), f32),), (), (early_all,), 6 * 2**30, limit=24)[0]
    early_rows = lax.dynamic_index_in_dim(early_all.reshape(4, 8, EARLY, D), c * 4 + z, 1, False)
    early_rows = early_rows.reshape(REPLICAS, 3, 8, D)
    early_rows = pad_rows(lax.dynamic_index_in_dim(early_rows, jnp.minimum(y, 2), 1, False), PIECE)
    late_parts, dnormed, branch_out, early_home, early_gram, early_rows = lax.optimization_barrier(
        (late_parts, dnormed, branch_out, early_home, early_gram, early_rows)
    )
    late_own = jnp.sum(late_parts.astype(f32), axis=0).astype(bf16)

    output = middle + branch_out
    dinput_norm, _ = norm_back(dnormed, inputs, scale_one, gain_attn)
    input_grad = dmiddle + dinput_norm
    by_y = [late_own] + [lax.ppermute(late_own, "y", [(i, i ^ k) for i in range(4)]) for k in (3, 2, 1)]
    late_line = jnp.concatenate(by_y, axis=0)

    x_plane = xh * 2 + xl
    late_rows = jnp.stack([by_y[1], by_y[2], by_y[3], by_y[0]], axis=0)
    late_rows = jnp.where(
        (x_plane == 0) | (x_plane == 3),
        late_rows.reshape(REPLICAS, PIECE, D),
        pad_rows(late_rows[:, :32].reshape(REPLICAS, 8, D), PIECE),
    )
    own_rows = jnp.where(y == 3, late_rows, early_rows).reshape(REPLICAS * PIECE, D)
    is_late = (y == 3).astype(jnp.int32).reshape(1)
    results = jnp.concatenate([output.astype(bf16), input_grad.astype(bf16)], axis=0)
    (late_line, late_other), (own_rows, late_own, results) = gather_line(late_line, (own_rows, late_own, results))
    gram = vmem_call(
        choose_gram_kernel, (((D, D), f32),), (), (is_late, early_gram, late_line), 2 * 2**30, 1, limit=20
    )[0]
    late_home = trade(late_own, home)
    gram, late_other, late_home = lax.optimization_barrier((gram, late_other, late_home))
    home_all = lax.all_gather(
        jnp.concatenate([early_home[:EARLY], late_home, early_home[EARLY:]], axis=0), ("xl", "y", "c"), axis=0
    )
    results = trade(results, home)
    orth = newton_schulz(is_late, gram, own_rows, late_other)

    mine = (jnp.arange(2) == c)[:, None, None, None]
    sent = jnp.where(mine, orth.reshape(1, REPLICAS, PIECE, D), 0).reshape(2 * REPLICAS, PIECE, D)
    pieces = lax.all_to_all(sent, ("xh", "xl", "y", "c"), 0, 0)

    output = results[:BLOCK]
    input_grad = jnp.where(home, input_grad, results[BLOCK : 2 * BLOCK].astype(f32))
    gain_all = home_all[:, EARLY + LATE :].astype(f32)
    gain_sum = jnp.sum(gain_all[:, :3] + gain_all[:, 3:6], axis=0)
    gain_grad = gain_sum.reshape(3 * D)[: 2 * D + 2 * HD]
    new_first = adam_first * gain_first + (1.0 - adam_first) * gain_grad
    new_second = adam_second * gain_second + (1.0 - adam_second) * gain_grad * gain_grad
    step_first = new_first / (1.0 - adam_first**STEP)
    step_second = new_second / (1.0 - adam_second**STEP)
    new_gains = gains - gain_rate * step_first / (jnp.sqrt(step_second) + adam_epsilon)
    new_moments = vmem_call(
        momentum_kernel,
        tuple((m.shape, f32) for m in moments),
        ((home_all.shape, bf16),),
        (home_all,),
        10**6,
        0,
        14 * 2**20,
        fetched=1,
    )
    pieces, new_moments, new_gains = lax.optimization_barrier((pieces, new_moments, new_gains))
    new_weights = vmem_call(
        weight_kernel,
        tuple((part.shape, f32) for part in own_parts),
        (),
        (xh.astype(jnp.int32).reshape(1), pieces, *own_parts),
        10**6,
        1,
        4 * 2**20,
    )
    new_weights = [w if i in SPLIT_FIRST else w.T for i, w in enumerate(new_weights)]
    return (output, input_grad, new_first, new_second, new_gains, *new_moments, *new_weights)


def solution(mesh):
    fine = Mesh(mesh.devices.reshape(2, 4, 2, 4, 2), ("xh", "z", "xl", "y", "c"))
    shard = ("xh", "z")
    replica = ("xl", "y", "c")
    rows = P(replica + shard, None)
    split = tuple(P(shard, None) if i in SPLIT_FIRST else P(None, shard) for i in range(7))
    pieces = tuple(
        P(shard + replica, None) if i in SPLIT_FIRST else P(None, shard + replica) for i in range(7)
    )
    in_specs = (rows, rows, P(replica, None), P(), P(), P()) + split + split
    out_specs = (rows, rows, P(), P(), P()) + split + pieces
    return jax.shard_map(shards, mesh=fine, in_specs=in_specs, out_specs=out_specs, check_vma=False)
```

```python
import math

import jax
import jax.numpy as jnp
from jax import lax
from jax.experimental import pallas as pl
from jax.experimental.pallas import tpu as pltpu
from jax.sharding import Mesh, PartitionSpec as P

D = 1024
H = 16
KV = 8
HD = 128
FF = 3072
NS_ITERS = 5
STEP = 10

norm_epsilon = 1e-06
rotary_base = 1000000.0
momentum_decay = 0.95
poly_first = 3.4445
poly_second = -4.775
poly_third = 2.0315
orth_epsilon = 1e-07
update_rate = 0.5
weight_shrink = 0.002
adam_first = 0.9
adam_second = 0.999
adam_epsilon = 1e-08
gain_rate = 0.8

f32 = jnp.float32
bf16 = jnp.bfloat16

PLANE = ("xh", "xl", "y")
REPLICAS = 16
BLOCK = 128
TOKENS = 8 * BLOCK
EARLY = 96
LATE = 64
PIECE = 16
FIRST_PACK = ((0, 256), (256, 128), (384, 128), (512, 256))
SECOND_PACK = ((0, 384), (384, 384), (768, 384))
SPLIT_FIRST = (3, 6)
FULL_SHAPES = ((D, H * HD), (D, KV * HD), (D, KV * HD), (H * HD, D), (D, FF), (D, FF), (FF, D))
SPREADS = (
    D ** (-0.5),
    D ** (-0.5),
    D ** (-0.5),
    max(H * HD // 256, 4) ** (-0.5),
    D ** (-0.5),
    D ** (-0.5),
    FF ** (-0.5),
)
RATES = tuple(update_rate * s * math.sqrt(max(f)) for s, f in zip(SPREADS, FULL_SHAPES))


def dot(a, b):
    return jnp.dot(a, b, preferred_element_type=f32)


def dot_t(a, b):
    return lax.dot_general(a, b, (((1,), (1,)), ((), ())), preferred_element_type=f32)


def t_dot(a, b):
    return lax.dot_general(a, b, (((0,), (0,)), ((), ())), preferred_element_type=f32)


def vmem_call(kernel, outs, scratch, operands, flops, scalars=0, bytes_accessed=8 * 2**20, limit=16, fetched=0, stored=0):
    vmem, smem, anywhere = (pl.BlockSpec(memory_space=m) for m in (pltpu.VMEM, pltpu.SMEM, pl.ANY))
    scratch_shapes = [pltpu.VMEM(shape, dtype) for shape, dtype in scratch]
    if fetched + stored:
        scratch_shapes.append(pltpu.SemaphoreType.DMA((fetched + stored,)))
    return pl.pallas_call(
        kernel,
        out_shape=tuple(jax.ShapeDtypeStruct(shape, dtype) for shape, dtype in outs),
        in_specs=[smem] * scalars + [vmem] * (len(operands) - scalars - fetched) + [anywhere] * fetched,
        out_specs=(vmem,) * (len(outs) - stored) + (anywhere,) * stored,
        scratch_shapes=scratch_shapes,
        compiler_params=pltpu.CompilerParams(vmem_limit_bytes=limit * 2**20),
        cost_estimate=pl.CostEstimate(flops=flops, bytes_accessed=bytes_accessed, transcendentals=0),
    )(*operands)


def fetch(sources, targets, sems, first=0):
    copies = [
        pltpu.make_async_copy(source, target, sems.at[first + i])
        for i, (source, target) in enumerate(zip(sources, targets))
    ]
    for copy in copies:
        copy.start()
    return copies


def wait(copies):
    for copy in copies:
        copy.wait()


def trade(x, home):
    other = lax.ppermute(x, ("xh", "c"), [(1, 2), (2, 1)])
    return jnp.where(home, x, other)


def trade_copied(x, home):
    other = lax.ppermute(x, ("xh", "c"), [(0, 2), (3, 1)])
    return jnp.where(home, x, other)


def over_z(x, k):
    return lax.ppermute(x, "z", [(i, i ^ k) for i in range(4)])


def over_core(x):
    return lax.ppermute(x, "c", [(0, 1), (1, 0)])


def gather_line(block, beside=()):
    near, far, across = (over_z(block, k) for k in (1, 3, 2))
    line = jnp.concatenate([block, near, across, far], axis=0)
    line, beside = lax.optimization_barrier((line, beside))
    return (line, over_core(line)), beside


def scatter_over_z(half, beside=()):
    sent = half.astype(bf16)
    parts = [over_z(sent[k * BLOCK : (k + 1) * BLOCK], k) for k in (1, 3, 2)]
    parts, beside = lax.optimization_barrier((parts, beside))
    return half[:BLOCK] + sum(part.astype(f32) for part in parts), beside


def rms_scale(values):
    return lax.rsqrt(jnp.mean(values * values, axis=-1, keepdims=True) + norm_epsilon)


def rotary_tables(position, head_width):
    half_width = head_width // 2
    freq_steps = jnp.arange(half_width, dtype=f32)
    inverse = rotary_base ** (-2.0 * freq_steps / head_width)
    angles = inverse[:, None] * position.astype(f32)[None, :]
    return (jnp.cos(angles), jnp.sin(angles))


def stream_layout(lengths_row, stream_rows):
    ends_at = jnp.cumsum(lengths_row)
    places = jnp.arange(stream_rows, dtype=jnp.int32)
    passed = (places[:, None] >= ends_at[None, :]).astype(jnp.int32)
    start = jnp.sum(passed * lengths_row[None, :], axis=1)
    return (start, places - start)


def norm_back(upstream, values, scale, gain):
    weighted = upstream * gain
    inner = jnp.mean(weighted * values, axis=-1, keepdims=True)
    grad_values = scale * (weighted - values * scale * scale * inner)
    return (grad_values, upstream * values * scale)


def pack_kernel(scale_ref, *refs):
    sources, (first_ref, second_ref), targets, sems = refs[:7], refs[7:9], refs[9:16], refs[16]
    copies = fetch(sources, targets, sems)
    scale = scale_ref[0]
    places = tuple((first_ref, *at) for at in FIRST_PACK) + tuple(
        (second_ref, *SECOND_PACK[i]) for i in (1, 2, 0)
    )
    for i, (out_ref, at, count) in enumerate(places):
        copies[i].wait()
        values = targets[i][...] * scale
        out_ref[at : at + count, :] = (values if i in SPLIT_FIRST else values.T).astype(bf16)


def pack(matrices, scale):
    return vmem_call(
        pack_kernel,
        (((768, D), bf16), ((1152, D), bf16)),
        tuple((m.shape, f32) for m in matrices),
        (jnp.asarray(scale, f32).reshape(1), *matrices),
        10**6,
        1,
        12 * 2**20,
        20,
        7,
    )


def turn(values, cosine, sine):
    front, back = values[: HD // 2], values[HD // 2 :]
    return jnp.concatenate([front * cosine - back * sine, back * cosine + front * sine], axis=0)


def column_scale(values):
    return lax.rsqrt(jnp.mean(values * values, axis=0, keepdims=True) + norm_epsilon)


def block_mask(start_ref, at, count, keys):
    key = lax.broadcasted_iota(jnp.int32, (keys, count), 0)
    token = at + lax.broadcasted_iota(jnp.int32, (keys, count), 1)
    allowed = (key >= start_ref[:, at : at + count]) & (key <= token)
    return jnp.concatenate([allowed, allowed], axis=1)


def both_heads(ref, at, count):
    return jnp.concatenate([ref[:HD, at : at + count], ref[HD : 2 * HD, at : at + count]], axis=1)


def in_order(order_ref, block):
    return pl.ds(pl.multiple_of(order_ref[block] * BLOCK, BLOCK), BLOCK)


def attention_kernel(order_ref, cosine_ref, sine_ref, start_ref, gain_query_ref, gain_key_ref, weight_ref, *refs):
    lines, (away_ref, kept_ref), stores = refs[:2], refs[2:4], refs[4:14]
    scratch, (value_t, attn, sems) = refs[14:22], refs[22:]
    pre_ref, attended_ref, normed, query_ref, key_t_ref, key_ref, value_ref, log_ref = scratch
    for i in range(8):
        normed[in_order(order_ref, i), :] = lines[i // 4][i % 4 * BLOCK : (i % 4 + 1) * BLOCK, :]
    copies = fetch((normed, cosine_ref, sine_ref), (stores[2], *stores[8:]), sems)
    pre_ref[...] = dot_t(weight_ref[: 4 * HD, :], normed[...])
    copies += fetch((pre_ref,), stores[:1], sems, 3)
    cosine, sine = cosine_ref[...], sine_ref[...]
    for head in range(3):
        values = pre_ref[head * HD : (head + 1) * HD, :]
        gain = gain_query_ref[...] if head < 2 else gain_key_ref[...]
        turned_low = turn(values * column_scale(values) * gain, cosine, sine).astype(bf16)
        if head < 2:
            query_ref[head * HD : (head + 1) * HD, :] = turned_low
        else:
            key_t_ref[...] = turned_low
            key_ref[...] = turned_low.T
    low = pre_ref[3 * HD :, :].astype(bf16)
    value_t[...] = low
    value_ref[...] = low.T
    count = 2 * BLOCK
    for at in range(0, TOKENS, count):
        keys = at + count
        scores = dot(key_ref[:keys, :], both_heads(query_ref, at, count)) * HD ** (-0.5)
        masked = jnp.where(block_mask(start_ref, at, count, keys), scores, -1e30)
        peak = jnp.max(masked, axis=0, keepdims=True)
        raised = jnp.exp(masked - peak)
        total = jnp.sum(raised, axis=0, keepdims=True)
        probs = (raised * (1.0 / total)).astype(bf16)
        attended = dot(value_t[:, :keys], probs)
        log_total = peak + jnp.log(total)
        for head in range(2):
            span = slice(head * count, (head + 1) * count)
            attended_ref[head * HD : (head + 1) * HD, at:keys] = attended[:, span]
            log_ref[head : head + 1, at:keys] = log_total[:, span]
    copies += fetch((attended_ref, *scratch[3:]), (stores[1], *stores[3:8]), sems, 4)
    for i in range(8):
        attn[:, i * BLOCK : (i + 1) * BLOCK] = attended_ref[:, in_order(order_ref, i)].astype(bf16)
    away_ref[...] = t_dot(attn[:, TOKENS // 2 :], weight_ref[4 * HD :, :]).astype(bf16)
    kept_ref[...] = t_dot(attn[:, : TOKENS // 2], weight_ref[4 * HD :, :])
    wait(copies)


def attention(order, tables, weight, lines):
    kept = (
        ((4 * HD, TOKENS), f32),
        ((2 * HD, TOKENS), f32),
        ((TOKENS, D), bf16),
        ((2 * HD, TOKENS), bf16),
        ((HD, TOKENS), bf16),
        ((TOKENS, HD), bf16),
        ((TOKENS, HD), bf16),
        ((2, TOKENS), f32),
    )
    outs = (((TOKENS // 2, D), bf16), ((TOKENS // 2, D), f32), *kept, *(((HD // 2, TOKENS), f32),) * 2)
    scratch = (*kept, ((HD, TOKENS), bf16), ((2 * HD, TOKENS), bf16))
    operands = (order, *tables, weight, *lines)
    away, half, *kept = vmem_call(attention_kernel, outs, scratch, operands, 3 * 10**9, 1, limit=20, stored=10)
    return away, half, kept


def norm_back_columns(upstream, values, gain):
    scale = column_scale(values)
    weighted = upstream * gain
    inner = jnp.mean(weighted * values, axis=0, keepdims=True)
    grad = scale * (weighted - values * (scale * scale * inner))
    return grad, jnp.sum(upstream * values * scale, axis=1, keepdims=True)


def attention_back_kernel(order_ref, start_ref, gain_query_ref, gain_key_ref, gain_attn_ref, *refs):
    lines, sources = refs[:2], refs[2:14]
    away_ref, kept_ref, late_ref, query_gain_ref, key_gain_ref, attn_gain_ref = refs[14:20]
    dquery, dkey, dvalue, dattn_ref, dpre, dpre_blocks, dbranch = refs[20:27]
    targets, sems = refs[27:39], refs[39]
    weight_ref, query_ref, key_t_ref, key_ref, value_ref, log_ref, attended_ref = targets[:7]
    pre_ref, normed, cosine_ref, sine_ref, momentum_ref = targets[7:]
    copies = fetch(sources, targets, sems)
    for i in range(8):
        dbranch[in_order(order_ref, i), :] = lines[i // 4][i % 4 * BLOCK : (i % 4 + 1) * BLOCK, :]
    copies[0].wait()
    dattn_ref[...] = dot_t(weight_ref[4 * HD :, :], dbranch[...]).astype(bf16)
    wait(copies[1:7])
    dkey[...] = jnp.zeros_like(dkey)
    dvalue[...] = jnp.zeros_like(dvalue)
    count = 2 * BLOCK
    for at in range(0, TOKENS, count):
        keys = at + count
        query = both_heads(query_ref, at, count)
        dattn = both_heads(dattn_ref, at, count)
        row_dot = jnp.sum(dattn.astype(f32) * both_heads(attended_ref, at, count), axis=0, keepdims=True)
        log_total = jnp.concatenate([log_ref[:1, at:keys], log_ref[1:, at:keys]], axis=1)
        scores = dot(key_ref[:keys, :], query) * HD ** (-0.5)
        allowed = block_mask(start_ref, at, count, keys)
        probs = jnp.where(allowed, jnp.exp(scores - log_total), 0.0)
        dprobs = dot(value_ref[:keys, :], dattn)
        dscores = (probs * (dprobs - row_dot)).astype(bf16)
        grad = dot(key_t_ref[:, :keys], dscores)
        for head in range(2):
            dquery[head * HD : (head + 1) * HD, at:keys] = grad[:, head * count : (head + 1) * count]
        dkey[:, :keys] += dot_t(query, dscores)
        dvalue[:, :keys] += dot_t(dattn, probs.astype(bf16))
    wait(copies[7:])
    cosine, sine = cosine_ref[...], sine_ref[...]
    query_gain = jnp.zeros_like(query_gain_ref)
    for head in range(3):
        span = slice(head * HD, (head + 1) * HD)
        upstream = (dquery[span, :] if head < 2 else dkey[...]) * HD ** (-0.5)
        gain = gain_query_ref[...] if head < 2 else gain_key_ref[...]
        grad, gain_part = norm_back_columns(turn(upstream, cosine, -sine), pre_ref[span, :], gain)
        dpre[span, :] = grad.astype(bf16)
        if head < 2:
            query_gain = query_gain + gain_part
        else:
            key_gain_ref[...] = gain_part
    query_gain_ref[...] = query_gain
    dpre[3 * HD :, :] = dvalue[...].astype(bf16)
    for i in range(8):
        dpre_blocks[:, i * BLOCK : (i + 1) * BLOCK] = dpre[:, in_order(order_ref, i)]
    away_ref[...] = t_dot(dpre_blocks[:, TOKENS // 2 :], weight_ref[: 4 * HD, :]).astype(bf16)
    kept_ref[...] = t_dot(dpre_blocks[:, : TOKENS // 2], weight_ref[: 4 * HD, :])
    grads = dot(dpre[...], normed[...])
    weighted = weight_ref[: 4 * HD, :].astype(f32) * grads
    attn_gain_ref[...] = jnp.sum(weighted, axis=0, keepdims=True) / gain_attn_ref[...]
    grads = grads + momentum_ref[: 4 * HD, :].astype(f32)
    late_ref[:256, :] = grads[:256].astype(bf16)
    late_ref[256:768, :] = jnp.zeros((512, D), bf16)
    for i in range(4):
        late_ref[256 + 64 * i : 288 + 64 * i, :] = grads[256 + 32 * i : 288 + 32 * i].astype(bf16)
        late_ref[512 + 64 * i : 544 + 64 * i, :] = grads[384 + 32 * i : 416 + 32 * i].astype(bf16)
    out_grad = dot(attended_ref[...].astype(bf16), dbranch[...])
    late_ref[768:, :] = (out_grad + momentum_ref[4 * HD :, :].astype(f32)).astype(bf16)


def attention_back(order, tables, gain_attn, weight, kept, momentum, dbranch):
    pre, attended, normed, query, key_t, key, value, log_total, cosine, sine = kept
    outs = (
        ((TOKENS // 2, D), bf16),
        ((TOKENS // 2, D), f32),
        ((REPLICAS * LATE, D), bf16),
        ((HD, 1), f32),
        ((HD, 1), f32),
        ((1, D), f32),
    )
    fetched = (weight, query, key_t, key, value, log_total, attended, pre, normed, cosine, sine, momentum)
    scratch = (
        ((2 * HD, TOKENS), f32),
        ((HD, TOKENS), f32),
        ((HD, TOKENS), f32),
        ((2 * HD, TOKENS), bf16),
        ((4 * HD, TOKENS), bf16),
        ((4 * HD, TOKENS), bf16),
        ((TOKENS, D), bf16),
        *((array.shape, array.dtype) for array in fetched),
    )
    operands = (order, *tables[2:], gain_attn, *dbranch, *fetched)
    return vmem_call(
        attention_back_kernel, outs, scratch, operands, 6 * 10**9, 1, limit=32, fetched=len(fetched)
    )


def feed_forward_kernel(home_ref, line_ref, other_ref, cot_line_ref, cot_other_ref, own_hbm, traded_hbm,
                        hidden_ref, grads_ref, away_ref, kept_ref, out_away_ref, out_kept_ref, normed, cot,
                        weight_ref, sems):
    @pl.when(home_ref[0] == 1)
    def _():
        pltpu.make_async_copy(own_hbm, weight_ref, sems.at[0]).start()

    @pl.when(home_ref[0] == 0)
    def _():
        pltpu.make_async_copy(traded_hbm, weight_ref, sems.at[0]).start()

    normed[: TOKENS // 2, :] = line_ref[...]
    normed[TOKENS // 2 :, :] = other_ref[...]
    cot[: TOKENS // 2, :] = cot_line_ref[...]
    cot[TOKENS // 2 :, :] = cot_other_ref[...]
    pltpu.make_async_copy(own_hbm, weight_ref, sems.at[0]).wait()
    width = SECOND_PACK[0][1]
    for part, out_ref, result_ref in ((1, away_ref, out_away_ref), (0, kept_ref, out_kept_ref)):
        span = slice(part * TOKENS // 2, (part + 1) * TOKENS // 2)
        both = dot_t(normed[span, :], weight_ref[width:, :])
        dhidden = dot_t(cot[span, :], weight_ref[:width, :])
        gate, upward = both[:, :width], both[:, width:]
        sigmoid_gate = jax.nn.sigmoid(gate)
        activated = gate * sigmoid_gate
        hidden_ref[span, :] = (activated * upward).astype(bf16)
        dgate = dhidden * upward * sigmoid_gate * (1.0 + gate * (1.0 - sigmoid_gate))
        grads_ref[span, :width] = dgate.astype(bf16)
        grads_ref[span, width:] = (dhidden * activated).astype(bf16)
        out_ref[...] = dot(grads_ref[span, :], weight_ref[width:, :]).astype(out_ref.dtype)
        result_ref[...] = dot(hidden_ref[span, :], weight_ref[:width, :]).astype(result_ref.dtype)


def feed_forward(home, normed, cot, own_weight, traded_weight):
    half = (TOKENS // 2, D)
    outs = (
        ((TOKENS, 384), bf16),
        ((TOKENS, 768), bf16),
        (half, bf16),
        (half, f32),
        (half, bf16),
        (half, f32),
        ((TOKENS, D), bf16),
        ((TOKENS, D), bf16),
    )
    operands = (home.astype(jnp.int32).reshape(1), *normed, *cot, own_weight, traded_weight)
    scratch = ((own_weight.shape, bf16),)
    return vmem_call(feed_forward_kernel, outs, scratch, operands, 5 * 10**9, 1, fetched=2)


def early_kernel(hidden_ref, grads_ref, momentum_ref, normed, cot, out_ref):
    out_ref[:768, :] = (t_dot(grads_ref[...], normed[...]) + momentum_ref[384:, :].astype(f32)).astype(bf16)
    out_ref[768:1152, :] = (t_dot(hidden_ref[...], cot[...]) + momentum_ref[:384, :].astype(f32)).astype(bf16)
    out_ref[1152:, :] = jnp.zeros((384, D), bf16)


def early_gradients(*operands):
    return vmem_call(early_kernel, (((REPLICAS * EARLY, D), bf16),), (), operands, 3 * 10**9)[0]


def gram_kernel(rows_ref, out_hbm, gram, sems):
    gram[...] = t_dot(rows_ref[...], rows_ref[...])
    wait(fetch((gram,), (out_hbm,), sems))


def line_gram_kernel(late_ref, line_ref, out_ref):
    @pl.when(late_ref[0] == 1)
    def _():
        out_ref[...] = t_dot(line_ref[...], line_ref[...])


def newton_schulz_kernel(late_ref, rows_ref, line_gram_ref, other_ref, early_hbm,
                         out_ref, full, low, rest, once, rows, sems):
    @pl.when(late_ref[0] == 0)
    def _():
        wait(fetch((early_hbm,), (full,), sems))

    @pl.when(late_ref[0] == 1)
    def _():
        full[...] = line_gram_ref[...] + t_dot(other_ref[...], other_ref[...])

    eye = lax.broadcasted_iota(jnp.int32, (128, 128), 0) == lax.broadcasted_iota(jnp.int32, (128, 128), 1)
    diagonal = jnp.zeros((128, 128), f32)
    for i in range(D // 128):
        span = slice(i * 128, (i + 1) * 128)
        diagonal = diagonal + jnp.where(eye, full[span, span], 0.0)
    total = jnp.sum(diagonal, axis=(0, 1), keepdims=True) + orth_epsilon
    inverse = lax.rsqrt(total)
    scaled = full[...] * (inverse * inverse)
    full[...] = scaled
    low[...] = scaled.astype(bf16)
    rows[...] = rows_ref[...].astype(f32) * inverse
    for iteration in range(NS_ITERS):
        rest[...] = (poly_second * full[...] + poly_third * dot(low[...], low[...])).astype(bf16)
        rows[...] = poly_first * rows[...] + dot(rows[...].astype(bf16), rest[...])
        if iteration + 1 < NS_ITERS:
            value = poly_first * full[...] + dot(rest[...], low[...])
            full[...] = value
            once[...] = value.astype(bf16)
            value = poly_first * full[...] + dot(rest[...], once[...])
            full[...] = value
            low[...] = value.astype(bf16)
    out_ref[...] = rows[...].astype(bf16)


def newton_schulz(is_late, early_gram, line_gram, rows, late_rows):
    count = rows.shape[0]
    scratch = (
        ((D, D), f32),
        ((D, D), bf16),
        ((D, D), bf16),
        ((D, D), bf16),
        ((count, D), f32),
    )
    operands = (is_late, rows, line_gram, late_rows, early_gram)
    flops = 15 * 2 * D**3 + 10 * count * D * D
    return vmem_call(newton_schulz_kernel, (((count, D), bf16),), scratch, operands, flops, 1, limit=32, fetched=1)[0]


def momentum_kernel(all_hbm, q, k, v, o, g, u, d, all_ref, sems):
    wait(fetch((all_hbm,), (all_ref,), sems))

    def rows(column, at, count):
        entries = [(column % 2 * 4 + y) * 2 + column // 2 for y in range(4)]
        return jnp.concatenate([all_ref[entry, at : at + count, :] for entry in entries], axis=0).astype(f32)

    q[...] = rows(0, EARLY, 64).T
    k[...] = rows(1, EARLY, 32).T
    v[...] = rows(2, EARLY, 32).T
    o[...] = rows(3, EARLY, 64)
    g[...] = rows(0, 0, EARLY).T
    u[...] = rows(1, 0, EARLY).T
    d[...] = rows(2, 0, EARLY)


def weight_kernel(half_ref, pieces_ref, *refs):
    kept, outs = refs[:7], refs[7:]
    half = half_ref[0]

    def rows(column, ys, count):
        return jnp.concatenate(
            [pieces_ref[column * 8 + y * 2 + half][:count, :] for y in ys], axis=0
        ).astype(f32)

    late, early = (3,), (0, 1, 2)
    updates = (
        rows(0, late, 16),
        rows(1, late, 8),
        rows(2, late, 8),
        rows(3, late, 16),
        rows(0, early, 8),
        rows(1, early, 8),
        rows(2, early, 8),
    )
    for i in range(7):
        outs[i][...] = kept[i][...] - RATES[i] * updates[i]


def pad_rows(rows, count):
    return jnp.pad(rows, ((0, 0), (0, count - rows.shape[1]), (0, 0)))


def shards(tokens, cotangent, lengths, gains, gain_first, gain_second, *matrices):
    weights, moments = matrices[:7], matrices[7:]
    xh, z, xl, y, c = (lax.axis_index(a) for a in ("xh", "z", "xl", "y", "c"))
    home = xh == c
    gain_attn = gains[:D]
    gain_mlp = gains[D : 2 * D]
    gain_query = gains[2 * D : 2 * D + HD]
    gain_key = gains[2 * D + HD :]
    order = jnp.stack([(c ^ (i // 4)) * 4 + (z ^ (i % 4)) for i in range(8)]).astype(jnp.int32)

    codes = jnp.concatenate([lengths[0] // 32, lengths[0] % 32]).astype(bf16)
    codes = jnp.pad(codes[None], ((0, 15), (0, D - codes.shape[0])))
    first_weights, second_weights = pack(weights, 1.0)
    arrived = trade(jnp.concatenate([tokens, cotangent, codes], axis=0), home)
    arrived, first_weights, moments = lax.optimization_barrier((arrived, first_weights, moments))
    inputs = arrived[:BLOCK].astype(f32)
    scale_one = rms_scale(inputs)
    own_normed = (inputs * scale_one * gain_attn).astype(bf16)
    cot_own = arrived[BLOCK : 2 * BLOCK]
    codes = arrived[2 * BLOCK, :12].astype(jnp.int32)
    start, position = stream_layout(codes[:6] * 32 + codes[6:], TOKENS)
    first_weights = trade_copied(first_weights, home)
    tables = (*rotary_tables(position, HD), start[None, :], gain_query[:, None], gain_key[:, None])
    momenta = pack(moments, jnp.where(home, momentum_decay / 8, 0.0))
    both = jnp.concatenate([own_normed, cot_own], axis=0)
    near, far, across = (over_z(both, k) for k in (1, 3, 2))
    parts = (both, near, across, far)
    line = jnp.concatenate([part[:BLOCK] for part in parts], axis=0)
    cot_line = jnp.concatenate([part[BLOCK:] for part in parts], axis=0)
    line, cot_line, first_weights, tables, second_weights, momenta = lax.optimization_barrier(
        (line, cot_line, first_weights, tables, second_weights, momenta)
    )
    first_momentum, second_momentum = momenta

    traded_weights = lax.ppermute(second_weights, ("xh", "c"), [(0, 2), (3, 1)])
    away, kept, for_back = attention(order, tables, first_weights, (line, over_core(line)))
    cot = (cot_line, over_core(cot_line))
    half = kept + over_core(away).astype(f32)
    middle = inputs + scatter_over_z(half)[0]

    scale_two = rms_scale(middle)
    place = xl * 8 + y * 2 + c
    middle, weights = lax.optimization_barrier((middle, weights))
    own_parts = []
    for i in range(7):
        axis = 0 if i in SPLIT_FIRST else 1
        per = weights[i].shape[axis] // REPLICAS
        part = lax.dynamic_slice_in_dim(weights[i], place * per, per, axis) * (1.0 - weight_shrink)
        own_parts.append(part.T if axis else part)
    normed_two, own_parts = gather_line((middle * scale_two * gain_mlp).astype(bf16), own_parts)
    hidden, grads, away, kept, out_away, out_half, normed_two, cot = feed_forward(
        home, normed_two, cot, second_weights, traded_weights
    )
    early = early_gradients(hidden, grads, second_momentum, normed_two, cot)
    dnormed_two, early = scatter_over_z(kept + over_core(away).astype(f32), early)
    early_parts = lax.all_to_all(early.reshape(REPLICAS, EARLY, D), PLANE, 0, 0)
    dmiddle_norm, mlp_gain_rows = norm_back(dnormed_two, middle, scale_two, gain_mlp)
    dmiddle = cot_own.astype(f32) + dmiddle_norm
    dbranch, _ = gather_line(dmiddle.astype(bf16))

    away, kept, late, query_gain, key_gain, attn_gain = attention_back(
        order,
        tables,
        gain_attn[None, :],
        first_weights,
        for_back,
        first_momentum,
        dbranch,
    )
    late_parts = lax.all_to_all(late.reshape(REPLICAS, LATE, D), PLANE, 0, 0)
    half, out_away, out_half, early_parts, mlp_gain_rows, *head_gains = lax.optimization_barrier(
        (kept + over_core(away).astype(f32), out_away, out_half, early_parts, mlp_gain_rows, query_gain, key_gain)
    )
    query_gain, key_gain = head_gains
    early_own = jnp.sum(early_parts.astype(f32), axis=0).astype(bf16)
    early_all = lax.all_gather(early_own, ("y", "c", "z"), axis=0, tiled=True)
    dnormed, _ = scatter_over_z(half)
    branch_out, _ = scatter_over_z(out_half + over_core(out_away).astype(f32))
    gain_rows = jnp.concatenate(
        [
            attn_gain[0],
            jnp.sum(mlp_gain_rows, axis=0),
            query_gain[:, 0],
            key_gain[:, 0],
            jnp.zeros((D - 2 * HD,), f32),
        ]
    ).reshape(3, D)
    for axis, step, size in (("z", 1, 4), ("z", 2, 4), ("c", 1, 2)):
        gain_rows = gain_rows + lax.ppermute(gain_rows, axis, [(i, i ^ step) for i in range(size)])
    gain_high = gain_rows.astype(bf16)
    gain_low = (gain_rows - gain_high.astype(f32)).astype(bf16)
    gain_rows = jnp.concatenate([gain_high, gain_low, jnp.zeros((2, D), bf16)], axis=0)
    early_home = trade(jnp.concatenate([early_own, gain_rows], axis=0), home)
    late_parts, dnormed, branch_out = lax.optimization_barrier((late_parts, dnormed, branch_out))
    late_own = jnp.sum(late_parts.astype(f32), axis=0).astype(bf16)

    output = middle + branch_out
    dinput_norm, _ = norm_back(dnormed, inputs, scale_one, gain_attn)
    input_grad = dmiddle + dinput_norm
    by_y = [late_own] + [lax.ppermute(late_own, "y", [(i, i ^ k) for i in range(4)]) for k in (3, 2, 1)]
    early_gram = vmem_call(
        gram_kernel, (((D, D), f32),), (((D, D), f32),), (early_all,), 6 * 2**30, limit=24, stored=1
    )[0]
    early_rows = lax.dynamic_index_in_dim(early_all.reshape(4, 8, EARLY, D), c * 4 + z, 1, False)
    early_rows = early_rows.reshape(REPLICAS, 3, 8, D)
    early_rows = pad_rows(lax.dynamic_index_in_dim(early_rows, jnp.minimum(y, 2), 1, False), PIECE)
    by_y, early_gram, early_rows = lax.optimization_barrier((by_y, early_gram, early_rows))
    late_line = jnp.concatenate(by_y, axis=0)

    x_plane = xh * 2 + xl
    late_rows = jnp.stack([by_y[1], by_y[2], by_y[3], by_y[0]], axis=0)
    late_rows = jnp.where(
        (x_plane == 0) | (x_plane == 3),
        late_rows.reshape(REPLICAS, PIECE, D),
        pad_rows(late_rows[:, :32].reshape(REPLICAS, 8, D), PIECE),
    )
    own_rows = jnp.where(y == 3, late_rows, early_rows).reshape(REPLICAS * PIECE, D)
    is_late = (y == 3).astype(jnp.int32).reshape(1)
    results = jnp.concatenate([output.astype(bf16), input_grad.astype(bf16)], axis=0)
    (late_line, late_other), (own_rows, late_own, results) = gather_line(late_line, (own_rows, late_own, results))
    line_gram = vmem_call(line_gram_kernel, (((D, D), f32),), (), (is_late, late_line), 2 * 2**30, 1, limit=16)[0]
    late_home = trade(late_own, home)
    line_gram, late_other, late_home, early_home = lax.optimization_barrier(
        (line_gram, late_other, late_home, early_home)
    )
    home_all = lax.all_gather(
        jnp.concatenate([early_home[:EARLY], late_home, early_home[EARLY:]], axis=0), ("xl", "y", "c"), axis=0
    )
    results = trade(results, home)
    orth = newton_schulz(is_late, early_gram, line_gram, own_rows, late_other)

    mine = (jnp.arange(2) == c)[:, None, None, None]
    sent = jnp.where(mine, orth.reshape(1, REPLICAS, PIECE, D), 0).reshape(2 * REPLICAS, PIECE, D)
    pieces = lax.all_to_all(sent, ("xh", "xl", "y", "c"), 0, 0)

    output = results[:BLOCK]
    input_grad = jnp.where(home, input_grad, results[BLOCK : 2 * BLOCK].astype(f32))
    gain_all = home_all[:, EARLY + LATE :].astype(f32)
    gain_sum = jnp.sum(gain_all[:, :3] + gain_all[:, 3:6], axis=0)
    gain_grad = gain_sum.reshape(3 * D)[: 2 * D + 2 * HD]
    new_first = adam_first * gain_first + (1.0 - adam_first) * gain_grad
    new_second = adam_second * gain_second + (1.0 - adam_second) * gain_grad * gain_grad
    step_first = new_first / (1.0 - adam_first**STEP)
    step_second = new_second / (1.0 - adam_second**STEP)
    new_gains = gains - gain_rate * step_first / (jnp.sqrt(step_second) + adam_epsilon)
    new_moments = vmem_call(
        momentum_kernel,
        tuple((m.shape, f32) for m in moments),
        ((home_all.shape, bf16),),
        (home_all,),
        10**6,
        0,
        14 * 2**20,
        fetched=1,
    )
    pieces, new_moments, new_gains = lax.optimization_barrier((pieces, new_moments, new_gains))
    new_weights = vmem_call(
        weight_kernel,
        tuple((part.shape, f32) for part in own_parts),
        (),
        (xh.astype(jnp.int32).reshape(1), pieces, *own_parts),
        10**6,
        1,
        4 * 2**20,
    )
    new_weights = [w if i in SPLIT_FIRST else w.T for i, w in enumerate(new_weights)]
    return (output, input_grad, new_first, new_second, new_gains, *new_moments, *new_weights)


def solution(mesh):
    fine = Mesh(mesh.devices.reshape(2, 4, 2, 4, 2), ("xh", "z", "xl", "y", "c"))
    shard = ("xh", "z")
    replica = ("xl", "y", "c")
    rows = P(replica + shard, None)
    split = tuple(P(shard, None) if i in SPLIT_FIRST else P(None, shard) for i in range(7))
    pieces = tuple(
        P(shard + replica, None) if i in SPLIT_FIRST else P(None, shard + replica) for i in range(7)
    )
    in_specs = (rows, rows, P(replica, None), P(), P(), P()) + split + split
    out_specs = (rows, rows, P(), P(), P()) + split + pieces
    return jax.shard_map(shards, mesh=fine, in_specs=in_specs, out_specs=out_specs, check_vma=False)
```

```python
import math

import jax
import jax.numpy as jnp
from jax import lax
from jax.experimental import pallas as pl
from jax.experimental.pallas import tpu as pltpu
from jax.sharding import Mesh, PartitionSpec as P

D = 1024
H = 16
KV = 8
HD = 128
FF = 3072
NS_ITERS = 5
STEP = 10

norm_epsilon = 1e-06
rotary_base = 1000000.0
momentum_decay = 0.95
poly_first = 3.4445
poly_second = -4.775
poly_third = 2.0315
orth_epsilon = 1e-07
update_rate = 0.5
weight_shrink = 0.002
adam_first = 0.9
adam_second = 0.999
adam_epsilon = 1e-08
gain_rate = 0.8

f32 = jnp.float32
bf16 = jnp.bfloat16

PLANE = ("xh", "xl", "y")
REPLICAS = 16
BLOCK = 128
TOKENS = 8 * BLOCK
EARLY = 96
LATE = 64
PIECE = 16
FIRST_PACK = ((0, 256), (256, 128), (384, 128), (512, 256))
SECOND_PACK = ((0, 384), (384, 384), (768, 384))
SPLIT_FIRST = (3, 6)
FULL_SHAPES = ((D, H * HD), (D, KV * HD), (D, KV * HD), (H * HD, D), (D, FF), (D, FF), (FF, D))
SPREADS = (
    D ** (-0.5),
    D ** (-0.5),
    D ** (-0.5),
    max(H * HD // 256, 4) ** (-0.5),
    D ** (-0.5),
    D ** (-0.5),
    FF ** (-0.5),
)
RATES = tuple(update_rate * s * math.sqrt(max(f)) for s, f in zip(SPREADS, FULL_SHAPES))


def dot(a, b):
    return jnp.dot(a, b, preferred_element_type=f32)


def dot_t(a, b):
    return lax.dot_general(a, b, (((1,), (1,)), ((), ())), preferred_element_type=f32)


def t_dot(a, b):
    return lax.dot_general(a, b, (((0,), (0,)), ((), ())), preferred_element_type=f32)


def vmem_call(kernel, outs, scratch, operands, flops, scalars=0, bytes_accessed=8 * 2**20, limit=16, fetched=0, stored=0):
    vmem, smem, anywhere = (pl.BlockSpec(memory_space=m) for m in (pltpu.VMEM, pltpu.SMEM, pl.ANY))
    scratch_shapes = [pltpu.VMEM(shape, dtype) for shape, dtype in scratch]
    if fetched + stored:
        scratch_shapes.append(pltpu.SemaphoreType.DMA((fetched + stored,)))
    return pl.pallas_call(
        kernel,
        out_shape=tuple(jax.ShapeDtypeStruct(shape, dtype) for shape, dtype in outs),
        in_specs=[smem] * scalars + [vmem] * (len(operands) - scalars - fetched) + [anywhere] * fetched,
        out_specs=(vmem,) * (len(outs) - stored) + (anywhere,) * stored,
        scratch_shapes=scratch_shapes,
        compiler_params=pltpu.CompilerParams(vmem_limit_bytes=limit * 2**20),
        cost_estimate=pl.CostEstimate(flops=flops, bytes_accessed=bytes_accessed, transcendentals=0),
    )(*operands)


def fetch(sources, targets, sems, first=0):
    copies = [
        pltpu.make_async_copy(source, target, sems.at[first + i])
        for i, (source, target) in enumerate(zip(sources, targets))
    ]
    for copy in copies:
        copy.start()
    return copies


def wait(copies):
    for copy in copies:
        copy.wait()


def trade(x, home):
    other = lax.ppermute(x, ("xh", "c"), [(1, 2), (2, 1)])
    return jnp.where(home, x, other)


def trade_copied(x, home):
    other = lax.ppermute(x, ("xh", "c"), [(0, 2), (3, 1)])
    return jnp.where(home, x, other)


def over_z(x, k):
    return lax.ppermute(x, "z", [(i, i ^ k) for i in range(4)])


def over_core(x):
    return lax.ppermute(x, "c", [(0, 1), (1, 0)])


def gather_line(block, beside=()):
    near, far, across = (over_z(block, k) for k in (1, 3, 2))
    line = jnp.concatenate([block, near, across, far], axis=0)
    line, beside = lax.optimization_barrier((line, beside))
    return (line, over_core(line)), beside


def scatter_over_z(half):
    sent = half.astype(bf16)
    parts = [over_z(sent[k * BLOCK : (k + 1) * BLOCK], k) for k in (1, 3, 2)]
    return half[:BLOCK] + sum(part.astype(f32) for part in parts)


def rms_scale(values):
    return lax.rsqrt(jnp.mean(values * values, axis=-1, keepdims=True) + norm_epsilon)


def rotary_tables(position, head_width):
    half_width = head_width // 2
    freq_steps = jnp.arange(half_width, dtype=f32)
    inverse = rotary_base ** (-2.0 * freq_steps / head_width)
    angles = inverse[:, None] * position.astype(f32)[None, :]
    return (jnp.cos(angles), jnp.sin(angles))


def stream_layout(lengths_row, stream_rows):
    ends_at = jnp.cumsum(lengths_row)
    places = jnp.arange(stream_rows, dtype=jnp.int32)
    passed = (places[:, None] >= ends_at[None, :]).astype(jnp.int32)
    start = jnp.sum(passed * lengths_row[None, :], axis=1)
    return (start, places - start)


def norm_back(upstream, values, scale, gain):
    weighted = upstream * gain
    inner = jnp.mean(weighted * values, axis=-1, keepdims=True)
    grad_values = scale * (weighted - values * scale * scale * inner)
    return (grad_values, upstream * values * scale)


def pack_kernel(scale_ref, *refs):
    sources, (first_ref, second_ref), targets, sems = refs[:7], refs[7:9], refs[9:16], refs[16]
    copies = fetch(sources, targets, sems)
    scale = scale_ref[0]
    places = tuple((first_ref, *at) for at in FIRST_PACK) + tuple(
        (second_ref, *SECOND_PACK[i]) for i in (1, 2, 0)
    )
    for i, (out_ref, at, count) in enumerate(places):
        copies[i].wait()
        values = targets[i][...] * scale
        out_ref[at : at + count, :] = (values if i in SPLIT_FIRST else values.T).astype(bf16)


def pack(matrices, scale):
    return vmem_call(
        pack_kernel,
        (((768, D), bf16), ((1152, D), bf16)),
        tuple((m.shape, f32) for m in matrices),
        (jnp.asarray(scale, f32).reshape(1), *matrices),
        10**6,
        1,
        12 * 2**20,
        20,
        7,
    )


def turn(values, cosine, sine):
    front, back = values[: HD // 2], values[HD // 2 :]
    return jnp.concatenate([front * cosine - back * sine, back * cosine + front * sine], axis=0)


def column_scale(values):
    return lax.rsqrt(jnp.mean(values * values, axis=0, keepdims=True) + norm_epsilon)


def block_mask(start_ref, at, count, keys):
    key = lax.broadcasted_iota(jnp.int32, (keys, count), 0)
    token = at + lax.broadcasted_iota(jnp.int32, (keys, count), 1)
    allowed = (key >= start_ref[:, at : at + count]) & (key <= token)
    return jnp.concatenate([allowed, allowed], axis=1)


def both_heads(ref, at, count):
    return jnp.concatenate([ref[:HD, at : at + count], ref[HD : 2 * HD, at : at + count]], axis=1)


def in_order(order_ref, block):
    return pl.ds(pl.multiple_of(order_ref[block] * BLOCK, BLOCK), BLOCK)


def attention_kernel(order_ref, cosine_ref, sine_ref, start_ref, gain_query_ref, gain_key_ref, weight_ref, *refs):
    lines = refs[:2]
    query_ref, key_t_ref, key_ref, value_ref, log_ref, away_ref, kept_ref, pre_ref, attended_ref, normed = refs[2:12]
    value_t, attn = refs[12:]
    for i in range(8):
        normed[in_order(order_ref, i), :] = lines[i // 4][i % 4 * BLOCK : (i % 4 + 1) * BLOCK, :]
    pre_ref[...] = dot_t(weight_ref[: 4 * HD, :], normed[...])
    cosine, sine = cosine_ref[...], sine_ref[...]
    for head in range(3):
        values = pre_ref[head * HD : (head + 1) * HD, :]
        gain = gain_query_ref[...] if head < 2 else gain_key_ref[...]
        turned_low = turn(values * column_scale(values) * gain, cosine, sine).astype(bf16)
        if head < 2:
            query_ref[head * HD : (head + 1) * HD, :] = turned_low
        else:
            key_t_ref[...] = turned_low
            key_ref[...] = turned_low.T
    low = pre_ref[3 * HD :, :].astype(bf16)
    value_t[...] = low
    value_ref[...] = low.T
    count = 2 * BLOCK
    for at in range(0, TOKENS, count):
        keys = at + count
        scores = dot(key_ref[:keys, :], both_heads(query_ref, at, count)) * HD ** (-0.5)
        masked = jnp.where(block_mask(start_ref, at, count, keys), scores, -1e30)
        peak = jnp.max(masked, axis=0, keepdims=True)
        raised = jnp.exp(masked - peak)
        total = jnp.sum(raised, axis=0, keepdims=True)
        probs = (raised * (1.0 / total)).astype(bf16)
        attended = dot(value_t[:, :keys], probs)
        log_total = peak + jnp.log(total)
        for head in range(2):
            span = slice(head * count, (head + 1) * count)
            attended_ref[head * HD : (head + 1) * HD, at:keys] = attended[:, span]
            log_ref[head : head + 1, at:keys] = log_total[:, span]
    for i in range(8):
        attn[:, i * BLOCK : (i + 1) * BLOCK] = attended_ref[:, in_order(order_ref, i)].astype(bf16)
    away_ref[...] = t_dot(attn[:, TOKENS // 2 :], weight_ref[4 * HD :, :]).astype(bf16)
    kept_ref[...] = t_dot(attn[:, : TOKENS // 2], weight_ref[4 * HD :, :])


def attention(order, tables, weight, lines):
    outs = (
        ((2 * HD, TOKENS), bf16),
        ((HD, TOKENS), bf16),
        ((TOKENS, HD), bf16),
        ((TOKENS, HD), bf16),
        ((2, TOKENS), f32),
        ((TOKENS // 2, D), bf16),
        ((TOKENS // 2, D), f32),
        ((4 * HD, TOKENS), f32),
        ((2 * HD, TOKENS), f32),
        ((TOKENS, D), bf16),
    )
    scratch = (((HD, TOKENS), bf16), ((2 * HD, TOKENS), bf16))
    operands = (order, *tables, weight, *lines)
    return vmem_call(attention_kernel, outs, scratch, operands, 3 * 10**9, 1)


def norm_back_columns(upstream, values, gain):
    scale = column_scale(values)
    weighted = upstream * gain
    inner = jnp.mean(weighted * values, axis=0, keepdims=True)
    grad = scale * (weighted - values * (scale * scale * inner))
    return grad, jnp.sum(upstream * values * scale, axis=1, keepdims=True)


def attention_back_kernel(order_ref, cosine_ref, sine_ref, start_ref, gain_query_ref, gain_key_ref,
                          query_ref, key_t_ref, key_ref, value_ref, log_ref, gain_attn_ref, weight_ref, *refs):
    lines, (attended_hbm, pre_hbm, normed_hbm, momentum_hbm) = refs[:2], refs[2:6]
    away_ref, kept_ref, late_ref, query_gain_ref, key_gain_ref, attn_gain_ref = refs[6:12]
    dquery, dkey, dvalue, dattn_ref, dpre, dpre_blocks, dbranch = refs[12:19]
    attended_ref, pre_ref, normed, momentum_ref, sems = refs[19:]
    copies = fetch(
        (attended_hbm, pre_hbm, normed_hbm, momentum_hbm), (attended_ref, pre_ref, normed, momentum_ref), sems
    )
    for i in range(8):
        dbranch[in_order(order_ref, i), :] = lines[i // 4][i % 4 * BLOCK : (i % 4 + 1) * BLOCK, :]
    dattn_ref[...] = dot_t(weight_ref[4 * HD :, :], dbranch[...]).astype(bf16)
    copies[0].wait()
    dkey[...] = jnp.zeros_like(dkey)
    dvalue[...] = jnp.zeros_like(dvalue)
    count = 2 * BLOCK
    for at in range(0, TOKENS, count):
        keys = at + count
        query = both_heads(query_ref, at, count)
        dattn = both_heads(dattn_ref, at, count)
        row_dot = jnp.sum(dattn.astype(f32) * both_heads(attended_ref, at, count), axis=0, keepdims=True)
        log_total = jnp.concatenate([log_ref[:1, at:keys], log_ref[1:, at:keys]], axis=1)
        scores = dot(key_ref[:keys, :], query) * HD ** (-0.5)
        allowed = block_mask(start_ref, at, count, keys)
        probs = jnp.where(allowed, jnp.exp(scores - log_total), 0.0)
        dprobs = dot(value_ref[:keys, :], dattn)
        dscores = (probs * (dprobs - row_dot)).astype(bf16)
        grad = dot(key_t_ref[:, :keys], dscores)
        for head in range(2):
            dquery[head * HD : (head + 1) * HD, at:keys] = grad[:, head * count : (head + 1) * count]
        dkey[:, :keys] += dot_t(query, dscores)
        dvalue[:, :keys] += dot_t(dattn, probs.astype(bf16))
    wait(copies[1:])
    cosine, sine = cosine_ref[...], sine_ref[...]
    query_gain = jnp.zeros_like(query_gain_ref)
    for head in range(3):
        span = slice(head * HD, (head + 1) * HD)
        upstream = (dquery[span, :] if head < 2 else dkey[...]) * HD ** (-0.5)
        gain = gain_query_ref[...] if head < 2 else gain_key_ref[...]
        grad, gain_part = norm_back_columns(turn(upstream, cosine, -sine), pre_ref[span, :], gain)
        dpre[span, :] = grad.astype(bf16)
        if head < 2:
            query_gain = query_gain + gain_part
        else:
            key_gain_ref[...] = gain_part
    query_gain_ref[...] = query_gain
    dpre[3 * HD :, :] = dvalue[...].astype(bf16)
    for i in range(8):
        dpre_blocks[:, i * BLOCK : (i + 1) * BLOCK] = dpre[:, in_order(order_ref, i)]
    away_ref[...] = t_dot(dpre_blocks[:, TOKENS // 2 :], weight_ref[: 4 * HD, :]).astype(bf16)
    kept_ref[...] = t_dot(dpre_blocks[:, : TOKENS // 2], weight_ref[: 4 * HD, :])
    grads = dot(dpre[...], normed[...])
    weighted = weight_ref[: 4 * HD, :].astype(f32) * grads
    attn_gain_ref[...] = jnp.sum(weighted, axis=0, keepdims=True) / gain_attn_ref[...]
    grads = grads + momentum_ref[: 4 * HD, :].astype(f32)
    late_ref[:256, :] = grads[:256].astype(bf16)
    late_ref[256:768, :] = jnp.zeros((512, D), bf16)
    for i in range(4):
        late_ref[256 + 64 * i : 288 + 64 * i, :] = grads[256 + 32 * i : 288 + 32 * i].astype(bf16)
        late_ref[512 + 64 * i : 544 + 64 * i, :] = grads[384 + 32 * i : 416 + 32 * i].astype(bf16)
    out_grad = dot(attended_ref[...].astype(bf16), dbranch[...])
    late_ref[768:, :] = (out_grad + momentum_ref[4 * HD :, :].astype(f32)).astype(bf16)


def attention_back(order, tables, gain_attn, weight, kept, momentum, dbranch):
    pre, query, key_t, key, value, attended, log_total, normed = kept
    outs = (
        ((TOKENS // 2, D), bf16),
        ((TOKENS // 2, D), f32),
        ((REPLICAS * LATE, D), bf16),
        ((HD, 1), f32),
        ((HD, 1), f32),
        ((1, D), f32),
    )
    scratch = (
        ((2 * HD, TOKENS), f32),
        ((HD, TOKENS), f32),
        ((HD, TOKENS), f32),
        ((2 * HD, TOKENS), bf16),
        ((4 * HD, TOKENS), bf16),
        ((4 * HD, TOKENS), bf16),
        ((TOKENS, D), bf16),
        (attended.shape, f32),
        (pre.shape, f32),
        (normed.shape, bf16),
        (momentum.shape, bf16),
    )
    operands = (
        *(order, *tables, query, key_t, key, value, log_total, gain_attn, weight),
        *(*dbranch, attended, pre, normed, momentum),
    )
    return vmem_call(attention_back_kernel, outs, scratch, operands, 6 * 10**9, 1, limit=32, fetched=4)


def feed_forward_kernel(home_ref, line_ref, other_ref, cot_line_ref, cot_other_ref, own_hbm, traded_hbm,
                        hidden_ref, grads_ref, away_ref, kept_ref, out_away_ref, out_kept_ref, normed, cot,
                        weight_ref, sems):
    @pl.when(home_ref[0] == 1)
    def _():
        pltpu.make_async_copy(own_hbm, weight_ref, sems.at[0]).start()

    @pl.when(home_ref[0] == 0)
    def _():
        pltpu.make_async_copy(traded_hbm, weight_ref, sems.at[0]).start()

    normed[: TOKENS // 2, :] = line_ref[...]
    normed[TOKENS // 2 :, :] = other_ref[...]
    cot[: TOKENS // 2, :] = cot_line_ref[...]
    cot[TOKENS // 2 :, :] = cot_other_ref[...]
    pltpu.make_async_copy(own_hbm, weight_ref, sems.at[0]).wait()
    width = SECOND_PACK[0][1]
    for part, out_ref, result_ref in ((1, away_ref, out_away_ref), (0, kept_ref, out_kept_ref)):
        span = slice(part * TOKENS // 2, (part + 1) * TOKENS // 2)
        both = dot_t(normed[span, :], weight_ref[width:, :])
        dhidden = dot_t(cot[span, :], weight_ref[:width, :])
        gate, upward = both[:, :width], both[:, width:]
        sigmoid_gate = jax.nn.sigmoid(gate)
        activated = gate * sigmoid_gate
        hidden_ref[span, :] = (activated * upward).astype(bf16)
        dgate = dhidden * upward * sigmoid_gate * (1.0 + gate * (1.0 - sigmoid_gate))
        grads_ref[span, :width] = dgate.astype(bf16)
        grads_ref[span, width:] = (dhidden * activated).astype(bf16)
        out_ref[...] = dot(grads_ref[span, :], weight_ref[width:, :]).astype(out_ref.dtype)
        result_ref[...] = dot(hidden_ref[span, :], weight_ref[:width, :]).astype(result_ref.dtype)


def feed_forward(home, normed, cot, own_weight, traded_weight):
    half = (TOKENS // 2, D)
    outs = (
        ((TOKENS, 384), bf16),
        ((TOKENS, 768), bf16),
        (half, bf16),
        (half, f32),
        (half, bf16),
        (half, f32),
        ((TOKENS, D), bf16),
        ((TOKENS, D), bf16),
    )
    operands = (home.astype(jnp.int32).reshape(1), *normed, *cot, own_weight, traded_weight)
    scratch = ((own_weight.shape, bf16),)
    return vmem_call(feed_forward_kernel, outs, scratch, operands, 5 * 10**9, 1, fetched=2)


def early_kernel(hidden_ref, grads_ref, momentum_ref, normed, cot, out_ref):
    out_ref[:768, :] = (t_dot(grads_ref[...], normed[...]) + momentum_ref[384:, :].astype(f32)).astype(bf16)
    out_ref[768:1152, :] = (t_dot(hidden_ref[...], cot[...]) + momentum_ref[:384, :].astype(f32)).astype(bf16)
    out_ref[1152:, :] = jnp.zeros((384, D), bf16)


def early_gradients(*operands):
    return vmem_call(early_kernel, (((REPLICAS * EARLY, D), bf16),), (), operands, 3 * 10**9)[0]


def gram_kernel(rows_ref, out_hbm, gram, sems):
    gram[...] = t_dot(rows_ref[...], rows_ref[...])
    wait(fetch((gram,), (out_hbm,), sems))


def line_gram_kernel(late_ref, line_ref, out_ref):
    @pl.when(late_ref[0] == 1)
    def _():
        out_ref[...] = t_dot(line_ref[...], line_ref[...])


def newton_schulz_kernel(late_ref, rows_ref, line_gram_ref, other_ref, early_hbm,
                         out_ref, full, low, rest, once, rows, sems):
    @pl.when(late_ref[0] == 0)
    def _():
        wait(fetch((early_hbm,), (full,), sems))

    @pl.when(late_ref[0] == 1)
    def _():
        full[...] = line_gram_ref[...] + t_dot(other_ref[...], other_ref[...])

    eye = lax.broadcasted_iota(jnp.int32, (128, 128), 0) == lax.broadcasted_iota(jnp.int32, (128, 128), 1)
    diagonal = jnp.zeros((128, 128), f32)
    for i in range(D // 128):
        span = slice(i * 128, (i + 1) * 128)
        diagonal = diagonal + jnp.where(eye, full[span, span], 0.0)
    total = jnp.sum(diagonal, axis=(0, 1), keepdims=True) + orth_epsilon
    inverse = lax.rsqrt(total)
    scaled = full[...] * (inverse * inverse)
    full[...] = scaled
    low[...] = scaled.astype(bf16)
    rows[...] = rows_ref[...].astype(f32) * inverse
    for iteration in range(NS_ITERS):
        rest[...] = (poly_second * full[...] + poly_third * dot(low[...], low[...])).astype(bf16)
        rows[...] = poly_first * rows[...] + dot(rows[...].astype(bf16), rest[...])
        if iteration + 1 < NS_ITERS:
            value = poly_first * full[...] + dot(rest[...], low[...])
            full[...] = value
            once[...] = value.astype(bf16)
            value = poly_first * full[...] + dot(rest[...], once[...])
            full[...] = value
            low[...] = value.astype(bf16)
    out_ref[...] = rows[...].astype(bf16)


def newton_schulz(is_late, early_gram, line_gram, rows, late_rows):
    count = rows.shape[0]
    scratch = (
        ((D, D), f32),
        ((D, D), bf16),
        ((D, D), bf16),
        ((D, D), bf16),
        ((count, D), f32),
    )
    operands = (is_late, rows, line_gram, late_rows, early_gram)
    flops = 15 * 2 * D**3 + 10 * count * D * D
    return vmem_call(newton_schulz_kernel, (((count, D), bf16),), scratch, operands, flops, 1, limit=32, fetched=1)[0]


def momentum_kernel(all_hbm, q, k, v, o, g, u, d, all_ref, sems):
    wait(fetch((all_hbm,), (all_ref,), sems))

    def rows(column, at, count):
        entries = [(column % 2 * 4 + y) * 2 + column // 2 for y in range(4)]
        return jnp.concatenate([all_ref[entry, at : at + count, :] for entry in entries], axis=0).astype(f32)

    q[...] = rows(0, EARLY, 64).T
    k[...] = rows(1, EARLY, 32).T
    v[...] = rows(2, EARLY, 32).T
    o[...] = rows(3, EARLY, 64)
    g[...] = rows(0, 0, EARLY).T
    u[...] = rows(1, 0, EARLY).T
    d[...] = rows(2, 0, EARLY)


def weight_kernel(half_ref, pieces_ref, *refs):
    kept, outs = refs[:7], refs[7:]
    half = half_ref[0]

    def rows(column, ys, count):
        return jnp.concatenate(
            [pieces_ref[column * 8 + y * 2 + half][:count, :] for y in ys], axis=0
        ).astype(f32)

    late, early = (3,), (0, 1, 2)
    updates = (
        rows(0, late, 16),
        rows(1, late, 8),
        rows(2, late, 8),
        rows(3, late, 16),
        rows(0, early, 8),
        rows(1, early, 8),
        rows(2, early, 8),
    )
    for i in range(7):
        outs[i][...] = kept[i][...] - RATES[i] * updates[i]


def pad_rows(rows, count):
    return jnp.pad(rows, ((0, 0), (0, count - rows.shape[1]), (0, 0)))


def shards(tokens, cotangent, lengths, gains, gain_first, gain_second, *matrices):
    weights, moments = matrices[:7], matrices[7:]
    xh, z, xl, y, c = (lax.axis_index(a) for a in ("xh", "z", "xl", "y", "c"))
    home = xh == c
    gain_attn = gains[:D]
    gain_mlp = gains[D : 2 * D]
    gain_query = gains[2 * D : 2 * D + HD]
    gain_key = gains[2 * D + HD :]
    order = jnp.stack([(c ^ (i // 4)) * 4 + (z ^ (i % 4)) for i in range(8)]).astype(jnp.int32)

    codes = jnp.concatenate([lengths[0] // 32, lengths[0] % 32]).astype(bf16)
    codes = jnp.pad(codes[None], ((0, 15), (0, D - codes.shape[0])))
    first_weights, second_weights = pack(weights, 1.0)
    arrived = trade(jnp.concatenate([tokens, cotangent, codes], axis=0), home)
    arrived, first_weights, moments = lax.optimization_barrier((arrived, first_weights, moments))
    inputs = arrived[:BLOCK].astype(f32)
    scale_one = rms_scale(inputs)
    own_normed = (inputs * scale_one * gain_attn).astype(bf16)
    cot_own = arrived[BLOCK : 2 * BLOCK]
    codes = arrived[2 * BLOCK, :12].astype(jnp.int32)
    start, position = stream_layout(codes[:6] * 32 + codes[6:], TOKENS)
    first_weights = trade_copied(first_weights, home)
    tables = (*rotary_tables(position, HD), start[None, :], gain_query[:, None], gain_key[:, None])
    momenta = pack(moments, jnp.where(home, momentum_decay / 8, 0.0))
    both = jnp.concatenate([own_normed, cot_own], axis=0)
    near, far, across = (over_z(both, k) for k in (1, 3, 2))
    parts = (both, near, across, far)
    line = jnp.concatenate([part[:BLOCK] for part in parts], axis=0)
    cot_line = jnp.concatenate([part[BLOCK:] for part in parts], axis=0)
    line, cot_line, first_weights, tables, second_weights, momenta = lax.optimization_barrier(
        (line, cot_line, first_weights, tables, second_weights, momenta)
    )
    first_momentum, second_momentum = momenta

    traded_weights = lax.ppermute(second_weights, ("xh", "c"), [(0, 2), (3, 1)])
    query_use, key_t, key_use, value_use, log_total, away, kept, pre, attended, normed = attention(
        order, tables, first_weights, (line, over_core(line))
    )
    cot = (cot_line, over_core(cot_line))
    half = kept + over_core(away).astype(f32)
    middle = inputs + scatter_over_z(half)

    scale_two = rms_scale(middle)
    place = xl * 8 + y * 2 + c
    middle, weights = lax.optimization_barrier((middle, weights))
    own_parts = []
    for i in range(7):
        axis = 0 if i in SPLIT_FIRST else 1
        per = weights[i].shape[axis] // REPLICAS
        part = lax.dynamic_slice_in_dim(weights[i], place * per, per, axis) * (1.0 - weight_shrink)
        own_parts.append(part.T if axis else part)
    normed_two, own_parts = gather_line((middle * scale_two * gain_mlp).astype(bf16), own_parts)
    hidden, grads, away, kept, out_away, out_half, normed_two, cot = feed_forward(
        home, normed_two, cot, second_weights, traded_weights
    )
    early = early_gradients(hidden, grads, second_momentum, normed_two, cot)
    half, early = lax.optimization_barrier((kept + over_core(away).astype(f32), early))
    early_parts = lax.all_to_all(early.reshape(REPLICAS, EARLY, D), PLANE, 0, 0)
    dnormed_two = scatter_over_z(half)
    dmiddle_norm, mlp_gain_rows = norm_back(dnormed_two, middle, scale_two, gain_mlp)
    dmiddle = cot_own.astype(f32) + dmiddle_norm
    dbranch, early_own = gather_line(
        dmiddle.astype(bf16), jnp.sum(early_parts.astype(f32), axis=0).astype(bf16)
    )
    early_all = lax.all_gather(early_own, ("y", "c", "z"), axis=0, tiled=True)

    away, kept, late, query_gain, key_gain, attn_gain = attention_back(
        order,
        tables,
        gain_attn[None, :],
        first_weights,
        (pre, query_use, key_t, key_use, value_use, attended, log_total, normed),
        first_momentum,
        dbranch,
    )
    late_parts = lax.all_to_all(late.reshape(REPLICAS, LATE, D), PLANE, 0, 0)
    half, out_away, out_half, mlp_gain_rows, attn_gain, query_gain, key_gain = lax.optimization_barrier(
        (kept + over_core(away).astype(f32), out_away, out_half, mlp_gain_rows, attn_gain, query_gain, key_gain)
    )
    dnormed = scatter_over_z(half)
    branch_out = scatter_over_z(out_half + over_core(out_away).astype(f32))
    gain_rows = jnp.concatenate(
        [
            attn_gain[0],
            jnp.sum(mlp_gain_rows, axis=0),
            query_gain[:, 0],
            key_gain[:, 0],
            jnp.zeros((D - 2 * HD,), f32),
        ]
    ).reshape(3, D)
    gain_high = gain_rows.astype(bf16)
    gain_low = (gain_rows - gain_high.astype(f32)).astype(bf16)
    gain_rows = jnp.concatenate([gain_high, gain_low, jnp.zeros((2, D), bf16)], axis=0)
    late_parts, dnormed, branch_out = lax.optimization_barrier((late_parts, dnormed, branch_out))
    late_own = jnp.sum(late_parts.astype(f32), axis=0).astype(bf16)

    output = middle + branch_out
    dinput_norm, _ = norm_back(dnormed, inputs, scale_one, gain_attn)
    input_grad = dmiddle + dinput_norm
    by_y = [late_own] + [lax.ppermute(late_own, "y", [(i, i ^ k) for i in range(4)]) for k in (3, 2, 1)]
    early_gram = vmem_call(
        gram_kernel, (((D, D), f32),), (((D, D), f32),), (early_all,), 6 * 2**30, limit=24, stored=1
    )[0]
    early_rows = lax.dynamic_index_in_dim(early_all.reshape(4, 8, EARLY, D), c * 4 + z, 1, False)
    early_rows = early_rows.reshape(REPLICAS, 3, 8, D)
    early_rows = pad_rows(lax.dynamic_index_in_dim(early_rows, jnp.minimum(y, 2), 1, False), PIECE)
    by_y, early_gram, early_rows = lax.optimization_barrier((by_y, early_gram, early_rows))
    late_line = jnp.concatenate(by_y, axis=0)

    x_plane = xh * 2 + xl
    late_rows = jnp.stack([by_y[1], by_y[2], by_y[3], by_y[0]], axis=0)
    late_rows = jnp.where(
        (x_plane == 0) | (x_plane == 3),
        late_rows.reshape(REPLICAS, PIECE, D),
        pad_rows(late_rows[:, :32].reshape(REPLICAS, 8, D), PIECE),
    )
    own_rows = jnp.where(y == 3, late_rows, early_rows).reshape(REPLICAS * PIECE, D)
    is_late = (y == 3).astype(jnp.int32).reshape(1)
    results = jnp.concatenate([output.astype(bf16), input_grad.astype(bf16)], axis=0)
    sums = jnp.concatenate([early_own, late_own, gain_rows], axis=0)
    (late_line, late_other), (own_rows, sums, results) = gather_line(late_line, (own_rows, sums, results))
    line_gram = vmem_call(line_gram_kernel, (((D, D), f32),), (), (is_late, late_line), 2 * 2**30, 1, limit=16)[0]
    sums = trade(sums, home)
    line_gram, late_other, sums = lax.optimization_barrier((line_gram, late_other, sums))
    home_all = lax.all_gather(sums, ("xl", "y", "c"), axis=0)
    results = trade(results, home)
    orth = newton_schulz(is_late, early_gram, line_gram, own_rows, late_other)

    mine = (jnp.arange(2) == c)[:, None, None, None]
    sent = jnp.where(mine, orth.reshape(1, REPLICAS, PIECE, D), 0).reshape(2 * REPLICAS, PIECE, D)
    pieces = lax.all_to_all(sent, ("xh", "xl", "y", "c"), 0, 0)

    output = results[:BLOCK]
    input_grad = jnp.where(home, input_grad, results[BLOCK : 2 * BLOCK].astype(f32))
    gain_all = home_all[:, EARLY + LATE :].astype(f32)
    gain_sum = jnp.sum(gain_all[:, :3] + gain_all[:, 3:6], axis=0)
    for axis, step, size in (("z", 1, 4), ("z", 2, 4), ("xh", 1, 2)):
        gain_sum = gain_sum + lax.ppermute(gain_sum, axis, [(i, i ^ step) for i in range(size)])
    gain_grad = gain_sum.reshape(3 * D)[: 2 * D + 2 * HD]
    new_first = adam_first * gain_first + (1.0 - adam_first) * gain_grad
    new_second = adam_second * gain_second + (1.0 - adam_second) * gain_grad * gain_grad
    step_first = new_first / (1.0 - adam_first**STEP)
    step_second = new_second / (1.0 - adam_second**STEP)
    new_gains = gains - gain_rate * step_first / (jnp.sqrt(step_second) + adam_epsilon)
    new_moments = vmem_call(
        momentum_kernel,
        tuple((m.shape, f32) for m in moments),
        ((home_all.shape, bf16),),
        (home_all,),
        10**6,
        0,
        14 * 2**20,
        fetched=1,
    )
    pieces, new_moments, new_gains = lax.optimization_barrier((pieces, new_moments, new_gains))
    new_weights = vmem_call(
        weight_kernel,
        tuple((part.shape, f32) for part in own_parts),
        (),
        (xh.astype(jnp.int32).reshape(1), pieces, *own_parts),
        10**6,
        1,
        4 * 2**20,
    )
    new_weights = [w if i in SPLIT_FIRST else w.T for i, w in enumerate(new_weights)]
    return (output, input_grad, new_first, new_second, new_gains, *new_moments, *new_weights)


def solution(mesh):
    fine = Mesh(mesh.devices.reshape(2, 4, 2, 4, 2), ("xh", "z", "xl", "y", "c"))
    shard = ("xh", "z")
    replica = ("xl", "y", "c")
    rows = P(replica + shard, None)
    split = tuple(P(shard, None) if i in SPLIT_FIRST else P(None, shard) for i in range(7))
    pieces = tuple(
        P(shard + replica, None) if i in SPLIT_FIRST else P(None, shard + replica) for i in range(7)
    )
    in_specs = (rows, rows, P(replica, None), P(), P(), P()) + split + split
    out_specs = (rows, rows, P(), P(), P()) + split + pieces
    return jax.shard_map(shards, mesh=fine, in_specs=in_specs, out_specs=out_specs, check_vma=False)
```

```python
import math

import jax
import jax.numpy as jnp
from jax import lax
from jax.experimental import pallas as pl
from jax.experimental.pallas import tpu as pltpu
from jax.sharding import Mesh, PartitionSpec as P

D = 1024
H = 16
KV = 8
HD = 128
FF = 3072
NS_ITERS = 5
STEP = 10

norm_epsilon = 1e-06
rotary_base = 1000000.0
momentum_decay = 0.95
poly_first = 3.4445
poly_second = -4.775
poly_third = 2.0315
orth_epsilon = 1e-07
update_rate = 0.5
weight_shrink = 0.002
adam_first = 0.9
adam_second = 0.999
adam_epsilon = 1e-08
gain_rate = 0.8

f32 = jnp.float32
bf16 = jnp.bfloat16

PLANE = ("xh", "xl", "y")
REPLICAS = 16
BLOCK = 128
TOKENS = 8 * BLOCK
EARLY = 96
LATE = 64
PIECE = 16
FIRST_PACK = ((0, 256), (256, 128), (384, 128), (512, 256))
SECOND_PACK = ((0, 384), (384, 384), (768, 384))
PACK_PLACES = tuple((False, *at) for at in FIRST_PACK) + tuple((True, *SECOND_PACK[i]) for i in (1, 2, 0))
SPLIT_FIRST = (3, 6)
FULL_SHAPES = ((D, H * HD), (D, KV * HD), (D, KV * HD), (H * HD, D), (D, FF), (D, FF), (FF, D))
SPREADS = (
    D ** (-0.5),
    D ** (-0.5),
    D ** (-0.5),
    max(H * HD // 256, 4) ** (-0.5),
    D ** (-0.5),
    D ** (-0.5),
    FF ** (-0.5),
)
RATES = tuple(update_rate * s * math.sqrt(max(f)) for s, f in zip(SPREADS, FULL_SHAPES))


def dot(a, b):
    return jnp.dot(a, b, preferred_element_type=f32)


def dot_t(a, b):
    return lax.dot_general(a, b, (((1,), (1,)), ((), ())), preferred_element_type=f32)


def t_dot(a, b):
    return lax.dot_general(a, b, (((0,), (0,)), ((), ())), preferred_element_type=f32)


def vmem_call(kernel, outs, scratch, operands, flops, scalars=0, bytes_accessed=8 * 2**20, limit=16, fetched=0, stored=0):
    vmem, smem, anywhere = (pl.BlockSpec(memory_space=m) for m in (pltpu.VMEM, pltpu.SMEM, pl.ANY))
    scratch_shapes = [pltpu.VMEM(shape, dtype) for shape, dtype in scratch]
    if fetched + stored:
        scratch_shapes.append(pltpu.SemaphoreType.DMA((fetched + stored,)))
    return pl.pallas_call(
        kernel,
        out_shape=tuple(jax.ShapeDtypeStruct(shape, dtype) for shape, dtype in outs),
        in_specs=[smem] * scalars + [vmem] * (len(operands) - scalars - fetched) + [anywhere] * fetched,
        out_specs=(vmem,) * (len(outs) - stored) + (anywhere,) * stored,
        scratch_shapes=scratch_shapes,
        compiler_params=pltpu.CompilerParams(vmem_limit_bytes=limit * 2**20),
        cost_estimate=pl.CostEstimate(flops=flops, bytes_accessed=bytes_accessed, transcendentals=0),
    )(*operands)


def fetch(sources, targets, sems, first=0):
    copies = [
        pltpu.make_async_copy(source, target, sems.at[first + i])
        for i, (source, target) in enumerate(zip(sources, targets))
    ]
    for copy in copies:
        copy.start()
    return copies


def wait(copies):
    for copy in copies:
        copy.wait()


def trade(x, home):
    other = lax.ppermute(x, ("xh", "c"), [(1, 2), (2, 1)])
    return jnp.where(home, x, other)


def trade_copied(x, home):
    other = lax.ppermute(x, ("xh", "c"), [(0, 2), (3, 1)])
    return jnp.where(home, x, other)


def over_z(x, k):
    return lax.ppermute(x, "z", [(i, i ^ k) for i in range(4)])


def over_core(x):
    return lax.ppermute(x, "c", [(0, 1), (1, 0)])


def gather_line(block, beside=()):
    near, far, across = (over_z(block, k) for k in (1, 3, 2))
    line = jnp.concatenate([block, near, across, far], axis=0)
    line, beside = lax.optimization_barrier((line, beside))
    return (line, over_core(line)), beside


def scatter_over_z(half):
    sent = half.astype(bf16)
    parts = [over_z(sent[k * BLOCK : (k + 1) * BLOCK], k) for k in (1, 3, 2)]
    return half[:BLOCK] + sum(part.astype(f32) for part in parts)


def rms_scale(values):
    return lax.rsqrt(jnp.mean(values * values, axis=-1, keepdims=True) + norm_epsilon)


def rotary_tables(position, head_width):
    half_width = head_width // 2
    freq_steps = jnp.arange(half_width, dtype=f32)
    inverse = rotary_base ** (-2.0 * freq_steps / head_width)
    angles = inverse[:, None] * position.astype(f32)[None, :]
    return (jnp.cos(angles), jnp.sin(angles))


def stream_layout(lengths_row, stream_rows):
    ends_at = jnp.cumsum(lengths_row)
    places = jnp.arange(stream_rows, dtype=jnp.int32)
    passed = (places[:, None] >= ends_at[None, :]).astype(jnp.int32)
    start = jnp.sum(passed * lengths_row[None, :], axis=1)
    return (start, places - start)


def norm_back(upstream, values, scale, gain):
    weighted = upstream * gain
    inner = jnp.mean(weighted * values, axis=-1, keepdims=True)
    grad_values = scale * (weighted - values * scale * scale * inner)
    return (grad_values, upstream * values * scale)


def pack_kernel(scale_ref, *refs):
    sources, (first_ref, second_ref), targets, sems = refs[:7], refs[7:9], refs[9:16], refs[16]
    copies = fetch(sources, targets, sems)
    scale = scale_ref[0]
    for i, (is_second, at, count) in enumerate(PACK_PLACES):
        copies[i].wait()
        values = targets[i][...] * scale
        out_ref = second_ref if is_second else first_ref
        out_ref[at : at + count, :] = (values if i in SPLIT_FIRST else values.T).astype(bf16)


def pack(matrices, scale):
    return vmem_call(
        pack_kernel,
        (((768, D), bf16), ((1152, D), bf16)),
        tuple((m.shape, f32) for m in matrices),
        (jnp.asarray(scale, f32).reshape(1), *matrices),
        10**6,
        1,
        12 * 2**20,
        20,
        7,
    )


def pack_weights_kernel(place_ref, *refs):
    sources, (first_ref, second_ref), own_refs = refs[:7], refs[7:9], refs[9:16]
    targets, turned, sems = refs[16:23], refs[23], refs[24]
    copies = fetch(sources, targets, sems)
    place = place_ref[0]
    for i, (is_second, at, count) in enumerate(PACK_PLACES):
        copies[i].wait()
        values = targets[i]
        if i not in SPLIT_FIRST:
            turned[:count, :] = values[...].T
            values = turned
        out_ref = second_ref if is_second else first_ref
        out_ref[at : at + count, :] = values[:count, :].astype(bf16)
        per = count // REPLICAS
        own_refs[i][...] = values[pl.ds(pl.multiple_of(place * per, 8), per), :] * (1.0 - weight_shrink)


def pack_weights(matrices, place):
    own = tuple(((count // REPLICAS, D), f32) for _, _, count in PACK_PLACES)
    first, second, *own = vmem_call(
        pack_weights_kernel,
        (((768, D), bf16), ((1152, D), bf16), *own),
        (*((m.shape, f32) for m in matrices), ((384, D), f32)),
        (place.astype(jnp.int32).reshape(1), *matrices),
        10**6,
        1,
        12 * 2**20,
        20,
        7,
    )
    return first, second, own


def turn(values, cosine, sine):
    front, back = values[: HD // 2], values[HD // 2 :]
    return jnp.concatenate([front * cosine - back * sine, back * cosine + front * sine], axis=0)


def column_scale(values):
    return lax.rsqrt(jnp.mean(values * values, axis=0, keepdims=True) + norm_epsilon)


def block_mask(start_ref, at, count, keys):
    key = lax.broadcasted_iota(jnp.int32, (keys, count), 0)
    token = at + lax.broadcasted_iota(jnp.int32, (keys, count), 1)
    allowed = (key >= start_ref[:, at : at + count]) & (key <= token)
    return jnp.concatenate([allowed, allowed], axis=1)


def both_heads(ref, at, count):
    return jnp.concatenate([ref[:HD, at : at + count], ref[HD : 2 * HD, at : at + count]], axis=1)


def in_order(order_ref, block):
    return pl.ds(pl.multiple_of(order_ref[block] * BLOCK, BLOCK), BLOCK)


def attention_kernel(order_ref, cosine_ref, sine_ref, start_ref, gain_query_ref, gain_key_ref, weight_ref, *refs):
    lines = refs[:2]
    query_ref, key_t_ref, key_ref, value_ref, log_ref, away_ref, kept_ref, pre_ref, attended_ref, normed = refs[2:12]
    value_t, attn = refs[12:]
    for i in range(8):
        normed[in_order(order_ref, i), :] = lines[i // 4][i % 4 * BLOCK : (i % 4 + 1) * BLOCK, :]
    pre_ref[...] = dot_t(weight_ref[: 4 * HD, :], normed[...])
    cosine, sine = cosine_ref[...], sine_ref[...]
    for head in range(3):
        values = pre_ref[head * HD : (head + 1) * HD, :]
        gain = gain_query_ref[...] if head < 2 else gain_key_ref[...]
        turned_low = turn(values * column_scale(values) * gain, cosine, sine).astype(bf16)
        if head < 2:
            query_ref[head * HD : (head + 1) * HD, :] = turned_low
        else:
            key_t_ref[...] = turned_low
            key_ref[...] = turned_low.T
    low = pre_ref[3 * HD :, :].astype(bf16)
    value_t[...] = low
    value_ref[...] = low.T
    count = 2 * BLOCK
    for at in range(0, TOKENS, count):
        keys = at + count
        scores = dot(key_ref[:keys, :], both_heads(query_ref, at, count)) * HD ** (-0.5)
        masked = jnp.where(block_mask(start_ref, at, count, keys), scores, -1e30)
        peak = jnp.max(masked, axis=0, keepdims=True)
        raised = jnp.exp(masked - peak)
        total = jnp.sum(raised, axis=0, keepdims=True)
        probs = (raised * (1.0 / total)).astype(bf16)
        attended = dot(value_t[:, :keys], probs)
        log_total = peak + jnp.log(total)
        for head in range(2):
            span = slice(head * count, (head + 1) * count)
            attended_ref[head * HD : (head + 1) * HD, at:keys] = attended[:, span]
            log_ref[head : head + 1, at:keys] = log_total[:, span]
    for i in range(8):
        attn[:, i * BLOCK : (i + 1) * BLOCK] = attended_ref[:, in_order(order_ref, i)].astype(bf16)
    away_ref[...] = t_dot(attn[:, TOKENS // 2 :], weight_ref[4 * HD :, :]).astype(bf16)
    kept_ref[...] = t_dot(attn[:, : TOKENS // 2], weight_ref[4 * HD :, :])


def attention(order, tables, weight, lines):
    outs = (
        ((2 * HD, TOKENS), bf16),
        ((HD, TOKENS), bf16),
        ((TOKENS, HD), bf16),
        ((TOKENS, HD), bf16),
        ((2, TOKENS), f32),
        ((TOKENS // 2, D), bf16),
        ((TOKENS // 2, D), f32),
        ((4 * HD, TOKENS), f32),
        ((2 * HD, TOKENS), f32),
        ((TOKENS, D), bf16),
    )
    scratch = (((HD, TOKENS), bf16), ((2 * HD, TOKENS), bf16))
    operands = (order, *tables, weight, *lines)
    return vmem_call(attention_kernel, outs, scratch, operands, 3 * 10**9, 1)


def norm_back_columns(upstream, values, gain):
    scale = column_scale(values)
    weighted = upstream * gain
    inner = jnp.mean(weighted * values, axis=0, keepdims=True)
    grad = scale * (weighted - values * (scale * scale * inner))
    return grad, jnp.sum(upstream * values * scale, axis=1, keepdims=True)


def attention_back_kernel(order_ref, cosine_ref, sine_ref, start_ref, gain_query_ref, gain_key_ref,
                          query_ref, key_t_ref, key_ref, value_ref, log_ref, gain_attn_ref, weight_ref, *refs):
    lines, (attended_hbm, pre_hbm, normed_hbm, momentum_hbm) = refs[:2], refs[2:6]
    away_ref, kept_ref, late_ref, query_gain_ref, key_gain_ref, attn_gain_ref = refs[6:12]
    dquery, dkey, dvalue, dattn_ref, dpre, dpre_blocks, dbranch = refs[12:19]
    attended_ref, pre_ref, normed, momentum_ref, sems = refs[19:]
    copies = fetch(
        (attended_hbm, pre_hbm, normed_hbm, momentum_hbm), (attended_ref, pre_ref, normed, momentum_ref), sems
    )
    for i in range(8):
        dbranch[in_order(order_ref, i), :] = lines[i // 4][i % 4 * BLOCK : (i % 4 + 1) * BLOCK, :]
    dattn_ref[...] = dot_t(weight_ref[4 * HD :, :], dbranch[...]).astype(bf16)
    copies[0].wait()
    dkey[...] = jnp.zeros_like(dkey)
    dvalue[...] = jnp.zeros_like(dvalue)
    count = 2 * BLOCK
    for at in range(0, TOKENS, count):
        keys = at + count
        query = both_heads(query_ref, at, count)
        dattn = both_heads(dattn_ref, at, count)
        row_dot = jnp.sum(dattn.astype(f32) * both_heads(attended_ref, at, count), axis=0, keepdims=True)
        log_total = jnp.concatenate([log_ref[:1, at:keys], log_ref[1:, at:keys]], axis=1)
        scores = dot(key_ref[:keys, :], query) * HD ** (-0.5)
        allowed = block_mask(start_ref, at, count, keys)
        probs = jnp.where(allowed, jnp.exp(scores - log_total), 0.0)
        dprobs = dot(value_ref[:keys, :], dattn)
        dscores = (probs * (dprobs - row_dot)).astype(bf16)
        grad = dot(key_t_ref[:, :keys], dscores)
        for head in range(2):
            dquery[head * HD : (head + 1) * HD, at:keys] = grad[:, head * count : (head + 1) * count]
        dkey[:, :keys] += dot_t(query, dscores)
        dvalue[:, :keys] += dot_t(dattn, probs.astype(bf16))
    wait(copies[1:])
    cosine, sine = cosine_ref[...], sine_ref[...]
    query_gain = jnp.zeros_like(query_gain_ref)
    for head in range(3):
        span = slice(head * HD, (head + 1) * HD)
        upstream = (dquery[span, :] if head < 2 else dkey[...]) * HD ** (-0.5)
        gain = gain_query_ref[...] if head < 2 else gain_key_ref[...]
        grad, gain_part = norm_back_columns(turn(upstream, cosine, -sine), pre_ref[span, :], gain)
        dpre[span, :] = grad.astype(bf16)
        if head < 2:
            query_gain = query_gain + gain_part
        else:
            key_gain_ref[...] = gain_part
    query_gain_ref[...] = query_gain
    dpre[3 * HD :, :] = dvalue[...].astype(bf16)
    for i in range(8):
        dpre_blocks[:, i * BLOCK : (i + 1) * BLOCK] = dpre[:, in_order(order_ref, i)]
    away_ref[...] = t_dot(dpre_blocks[:, TOKENS // 2 :], weight_ref[: 4 * HD, :]).astype(bf16)
    kept_ref[...] = t_dot(dpre_blocks[:, : TOKENS // 2], weight_ref[: 4 * HD, :])
    grads = dot(dpre[...], normed[...])
    weighted = weight_ref[: 4 * HD, :].astype(f32) * grads
    attn_gain_ref[...] = jnp.sum(weighted, axis=0, keepdims=True) / gain_attn_ref[...]
    grads = grads + momentum_ref[: 4 * HD, :].astype(f32)
    late_ref[:256, :] = grads[:256].astype(bf16)
    late_ref[256:768, :] = jnp.zeros((512, D), bf16)
    for i in range(4):
        late_ref[256 + 64 * i : 288 + 64 * i, :] = grads[256 + 32 * i : 288 + 32 * i].astype(bf16)
        late_ref[512 + 64 * i : 544 + 64 * i, :] = grads[384 + 32 * i : 416 + 32 * i].astype(bf16)
    out_grad = dot(attended_ref[...].astype(bf16), dbranch[...])
    late_ref[768:, :] = (out_grad + momentum_ref[4 * HD :, :].astype(f32)).astype(bf16)


def attention_back(order, tables, gain_attn, weight, kept, momentum, dbranch):
    pre, query, key_t, key, value, attended, log_total, normed = kept
    outs = (
        ((TOKENS // 2, D), bf16),
        ((TOKENS // 2, D), f32),
        ((REPLICAS * LATE, D), bf16),
        ((HD, 1), f32),
        ((HD, 1), f32),
        ((1, D), f32),
    )
    scratch = (
        ((2 * HD, TOKENS), f32),
        ((HD, TOKENS), f32),
        ((HD, TOKENS), f32),
        ((2 * HD, TOKENS), bf16),
        ((4 * HD, TOKENS), bf16),
        ((4 * HD, TOKENS), bf16),
        ((TOKENS, D), bf16),
        (attended.shape, f32),
        (pre.shape, f32),
        (normed.shape, bf16),
        (momentum.shape, bf16),
    )
    operands = (
        *(order, *tables, query, key_t, key, value, log_total, gain_attn, weight),
        *(*dbranch, attended, pre, normed, momentum),
    )
    return vmem_call(attention_back_kernel, outs, scratch, operands, 6 * 10**9, 1, limit=20, fetched=4)


def feed_forward_kernel(home_ref, line_ref, other_ref, cot_line_ref, cot_other_ref, own_hbm, traded_hbm,
                        hidden_ref, grads_ref, away_ref, kept_ref, out_away_ref, out_kept_ref, normed, cot,
                        weight_ref, sems):
    @pl.when(home_ref[0] == 1)
    def _():
        pltpu.make_async_copy(own_hbm, weight_ref, sems.at[0]).start()

    @pl.when(home_ref[0] == 0)
    def _():
        pltpu.make_async_copy(traded_hbm, weight_ref, sems.at[0]).start()

    normed[: TOKENS // 2, :] = line_ref[...]
    normed[TOKENS // 2 :, :] = other_ref[...]
    cot[: TOKENS // 2, :] = cot_line_ref[...]
    cot[TOKENS // 2 :, :] = cot_other_ref[...]
    pltpu.make_async_copy(own_hbm, weight_ref, sems.at[0]).wait()
    width = SECOND_PACK[0][1]
    for part, out_ref, result_ref in ((1, away_ref, out_away_ref), (0, kept_ref, out_kept_ref)):
        span = slice(part * TOKENS // 2, (part + 1) * TOKENS // 2)
        both = dot_t(normed[span, :], weight_ref[width:, :])
        dhidden = dot_t(cot[span, :], weight_ref[:width, :])
        gate, upward = both[:, :width], both[:, width:]
        sigmoid_gate = jax.nn.sigmoid(gate)
        activated = gate * sigmoid_gate
        hidden_ref[span, :] = (activated * upward).astype(bf16)
        dgate = dhidden * upward * sigmoid_gate * (1.0 + gate * (1.0 - sigmoid_gate))
        grads_ref[span, :width] = dgate.astype(bf16)
        grads_ref[span, width:] = (dhidden * activated).astype(bf16)
        out_ref[...] = dot(grads_ref[span, :], weight_ref[width:, :]).astype(out_ref.dtype)
        result_ref[...] = dot(hidden_ref[span, :], weight_ref[:width, :]).astype(result_ref.dtype)


def feed_forward(home, normed, cot, own_weight, traded_weight):
    half = (TOKENS // 2, D)
    outs = (
        ((TOKENS, 384), bf16),
        ((TOKENS, 768), bf16),
        (half, bf16),
        (half, f32),
        (half, bf16),
        (half, f32),
        ((TOKENS, D), bf16),
        ((TOKENS, D), bf16),
    )
    operands = (home.astype(jnp.int32).reshape(1), *normed, *cot, own_weight, traded_weight)
    scratch = ((own_weight.shape, bf16),)
    return vmem_call(feed_forward_kernel, outs, scratch, operands, 5 * 10**9, 1, fetched=2)


def early_kernel(hidden_ref, grads_ref, momentum_ref, normed, cot, out_ref):
    out_ref[:768, :] = (t_dot(grads_ref[...], normed[...]) + momentum_ref[384:, :].astype(f32)).astype(bf16)
    out_ref[768:1152, :] = (t_dot(hidden_ref[...], cot[...]) + momentum_ref[:384, :].astype(f32)).astype(bf16)
    out_ref[1152:, :] = jnp.zeros((384, D), bf16)


def early_gradients(*operands):
    return vmem_call(early_kernel, (((REPLICAS * EARLY, D), bf16),), (), operands, 3 * 10**9)[0]


def gram_kernel(rows_ref, out_hbm, gram, sems):
    gram[...] = t_dot(rows_ref[...], rows_ref[...])
    wait(fetch((gram,), (out_hbm,), sems))


def line_gram_kernel(late_ref, line_ref, out_ref):
    @pl.when(late_ref[0] == 1)
    def _():
        out_ref[...] = t_dot(line_ref[...], line_ref[...])


def newton_schulz_kernel(late_ref, rows_ref, line_gram_ref, other_ref, early_hbm,
                         out_ref, full, low, rest, once, rows, sems):
    @pl.when(late_ref[0] == 0)
    def _():
        wait(fetch((early_hbm,), (full,), sems))

    @pl.when(late_ref[0] == 1)
    def _():
        full[...] = line_gram_ref[...] + t_dot(other_ref[...], other_ref[...])

    eye = lax.broadcasted_iota(jnp.int32, (128, 128), 0) == lax.broadcasted_iota(jnp.int32, (128, 128), 1)
    diagonal = jnp.zeros((128, 128), f32)
    for i in range(D // 128):
        span = slice(i * 128, (i + 1) * 128)
        diagonal = diagonal + jnp.where(eye, full[span, span], 0.0)
    total = jnp.sum(diagonal, axis=(0, 1), keepdims=True) + orth_epsilon
    inverse = lax.rsqrt(total)
    scaled = full[...] * (inverse * inverse)
    full[...] = scaled
    low[...] = scaled.astype(bf16)
    rows[...] = rows_ref[...].astype(f32) * inverse
    for iteration in range(NS_ITERS):
        rest[...] = (poly_second * full[...] + poly_third * dot(low[...], low[...])).astype(bf16)
        rows[...] = poly_first * rows[...] + dot(rows[...].astype(bf16), rest[...])
        if iteration + 1 < NS_ITERS:
            value = poly_first * full[...] + dot(rest[...], low[...])
            full[...] = value
            once[...] = value.astype(bf16)
            value = poly_first * full[...] + dot(rest[...], once[...])
            full[...] = value
            low[...] = value.astype(bf16)
    out_ref[...] = rows[...].astype(bf16)


def newton_schulz(is_late, early_gram, line_gram, rows, late_rows):
    count = rows.shape[0]
    scratch = (
        ((D, D), f32),
        ((D, D), bf16),
        ((D, D), bf16),
        ((D, D), bf16),
        ((count, D), f32),
    )
    operands = (is_late, rows, line_gram, late_rows, early_gram)
    flops = 15 * 2 * D**3 + 10 * count * D * D
    return vmem_call(newton_schulz_kernel, (((count, D), bf16),), scratch, operands, flops, 1, limit=20, fetched=1)[0]


def home_rows_kernel(early_ref, late_ref, attn_ref, mlp_ref, query_ref, key_ref, out_ref):
    out_ref[:EARLY, :] = early_ref[...]
    out_ref[EARLY : EARLY + LATE, :] = late_ref[...]
    eye = lax.broadcasted_iota(jnp.int32, (HD, HD), 0) == lax.broadcasted_iota(jnp.int32, (HD, HD), 1)
    heads = [jnp.sum(jnp.where(eye, ref[...], 0.0), axis=0, keepdims=True) for ref in (query_ref, key_ref)]
    rows = jnp.concatenate(
        [
            attn_ref[...],
            jnp.sum(mlp_ref[...], axis=0, keepdims=True),
            jnp.concatenate([*heads, jnp.zeros((1, D - 2 * HD), f32)], axis=1),
            jnp.zeros((5, D), f32),
        ],
        axis=0,
    )
    high = rows.astype(bf16).astype(f32)
    out_ref[EARLY + LATE :, :] = jnp.concatenate([high, rows - high], axis=0).astype(bf16)


def momentum_kernel(all_hbm, q, k, v, o, g, u, d, all_ref, sems):
    wait(fetch((all_hbm,), (all_ref,), sems))

    def rows(column, at, count):
        entries = [(column % 2 * 4 + y) * 2 + column // 2 for y in range(4)]
        return jnp.concatenate([all_ref[entry, at : at + count, :] for entry in entries], axis=0).astype(f32)

    q[...] = rows(0, EARLY, 64).T
    k[...] = rows(1, EARLY, 32).T
    v[...] = rows(2, EARLY, 32).T
    o[...] = rows(3, EARLY, 64)
    g[...] = rows(0, 0, EARLY).T
    u[...] = rows(1, 0, EARLY).T
    d[...] = rows(2, 0, EARLY)


def weight_kernel(half_ref, pieces_ref, *refs):
    kept, outs = refs[:7], refs[7:]
    half = half_ref[0]

    def rows(column, ys, count):
        return jnp.concatenate(
            [pieces_ref[column * 8 + y * 2 + half][:count, :] for y in ys], axis=0
        ).astype(f32)

    late, early = (3,), (0, 1, 2)
    updates = (
        rows(0, late, 16),
        rows(1, late, 8),
        rows(2, late, 8),
        rows(3, late, 16),
        rows(0, early, 8),
        rows(1, early, 8),
        rows(2, early, 8),
    )
    for i in range(7):
        outs[i][...] = kept[i][...] - RATES[i] * updates[i]


def pad_rows(rows, count):
    return jnp.pad(rows, ((0, 0), (0, count - rows.shape[1]), (0, 0)))


def shards(tokens, cotangent, lengths, gains, gain_first, gain_second, *matrices):
    weights, moments = matrices[:7], matrices[7:]
    xh, z, xl, y, c = (lax.axis_index(a) for a in ("xh", "z", "xl", "y", "c"))
    home = xh == c
    gain_attn = gains[:D]
    gain_mlp = gains[D : 2 * D]
    gain_query = gains[2 * D : 2 * D + HD]
    gain_key = gains[2 * D + HD :]
    order = jnp.stack([(c ^ (i // 4)) * 4 + (z ^ (i % 4)) for i in range(8)]).astype(jnp.int32)

    codes = jnp.concatenate([lengths[0] // 32, lengths[0] % 32]).astype(bf16)
    codes = jnp.pad(codes[None], ((0, 15), (0, D - codes.shape[0])))
    first_weights, second_weights, own_parts = pack_weights(weights, xl * 8 + y * 2 + c)
    arrived = trade(jnp.concatenate([tokens, cotangent, codes], axis=0), home)
    arrived, first_weights, moments = lax.optimization_barrier((arrived, first_weights, moments))
    inputs = arrived[:BLOCK].astype(f32)
    scale_one = rms_scale(inputs)
    own_normed = (inputs * scale_one * gain_attn).astype(bf16)
    cot_own = arrived[BLOCK : 2 * BLOCK]
    codes = arrived[2 * BLOCK, :12].astype(jnp.int32)
    start, position = stream_layout(codes[:6] * 32 + codes[6:], TOKENS)
    first_weights = trade_copied(first_weights, home)
    tables = (*rotary_tables(position, HD), start[None, :], gain_query[:, None], gain_key[:, None])
    momenta = pack(moments, jnp.where(home, momentum_decay / 8, 0.0))
    both = jnp.concatenate([own_normed, cot_own], axis=0)
    near, far, across = (over_z(both, k) for k in (1, 3, 2))
    parts = (both, near, across, far)
    line = jnp.concatenate([part[:BLOCK] for part in parts], axis=0)
    cot_line = jnp.concatenate([part[BLOCK:] for part in parts], axis=0)
    line, cot_line, first_weights, tables, second_weights, momenta = lax.optimization_barrier(
        (line, cot_line, first_weights, tables, second_weights, momenta)
    )
    first_momentum, second_momentum = momenta

    traded_weights = lax.ppermute(second_weights, ("xh", "c"), [(0, 2), (3, 1)])
    query_use, key_t, key_use, value_use, log_total, away, kept, pre, attended, normed = attention(
        order, tables, first_weights, (line, over_core(line))
    )
    cot = (cot_line, over_core(cot_line))
    half = kept + over_core(away).astype(f32)
    middle = inputs + scatter_over_z(half)

    scale_two = rms_scale(middle)
    normed_two, _ = gather_line((middle * scale_two * gain_mlp).astype(bf16))
    hidden, grads, away, kept, out_away, out_half, normed_two, cot = feed_forward(
        home, normed_two, cot, second_weights, traded_weights
    )
    early = early_gradients(hidden, grads, second_momentum, normed_two, cot)
    half, early = lax.optimization_barrier((kept + over_core(away).astype(f32), early))
    early_parts = lax.all_to_all(early.reshape(REPLICAS, EARLY, D), PLANE, 0, 0)
    dnormed_two = scatter_over_z(half)
    dmiddle_norm, mlp_gain_rows = norm_back(dnormed_two, middle, scale_two, gain_mlp)
    dmiddle = cot_own.astype(f32) + dmiddle_norm
    dbranch, early_own = gather_line(
        dmiddle.astype(bf16), jnp.sum(early_parts.astype(f32), axis=0).astype(bf16)
    )
    early_all = lax.all_gather(early_own, ("y", "c", "z"), axis=0, tiled=True)

    away, kept, late, query_gain, key_gain, attn_gain = attention_back(
        order,
        tables,
        gain_attn[None, :],
        first_weights,
        (pre, query_use, key_t, key_use, value_use, attended, log_total, normed),
        first_momentum,
        dbranch,
    )
    late_parts = lax.all_to_all(late.reshape(REPLICAS, LATE, D), PLANE, 0, 0)
    half, out_away, out_half, mlp_gain_rows, attn_gain, query_gain, key_gain = lax.optimization_barrier(
        (kept + over_core(away).astype(f32), out_away, out_half, mlp_gain_rows, attn_gain, query_gain, key_gain)
    )
    dnormed = scatter_over_z(half)
    branch_out = scatter_over_z(out_half + over_core(out_away).astype(f32))
    late_parts, dnormed, branch_out = lax.optimization_barrier((late_parts, dnormed, branch_out))
    late_own = jnp.sum(late_parts.astype(f32), axis=0).astype(bf16)

    output = middle + branch_out
    dinput_norm, _ = norm_back(dnormed, inputs, scale_one, gain_attn)
    input_grad = dmiddle + dinput_norm
    by_y = [late_own] + [lax.ppermute(late_own, "y", [(i, i ^ k) for i in range(4)]) for k in (3, 2, 1)]
    early_gram = vmem_call(
        gram_kernel, (((D, D), f32),), (((D, D), f32),), (early_all,), 6 * 2**30, limit=24, stored=1
    )[0]
    early_rows = lax.dynamic_index_in_dim(early_all.reshape(4, 8, EARLY, D), c * 4 + z, 1, False)
    early_rows = early_rows.reshape(REPLICAS, 3, 8, D)
    early_rows = pad_rows(lax.dynamic_index_in_dim(early_rows, jnp.minimum(y, 2), 1, False), PIECE)
    by_y, early_gram, early_rows = lax.optimization_barrier((by_y, early_gram, early_rows))
    late_line = jnp.concatenate(by_y, axis=0)

    x_plane = xh * 2 + xl
    late_rows = jnp.stack([by_y[1], by_y[2], by_y[3], by_y[0]], axis=0)
    late_rows = jnp.where(
        (x_plane == 0) | (x_plane == 3),
        late_rows.reshape(REPLICAS, PIECE, D),
        pad_rows(late_rows[:, :32].reshape(REPLICAS, 8, D), PIECE),
    )
    own_rows = jnp.where(y == 3, late_rows, early_rows).reshape(REPLICAS * PIECE, D)
    is_late = (y == 3).astype(jnp.int32).reshape(1)
    results = jnp.concatenate([output.astype(bf16), input_grad.astype(bf16)], axis=0)
    (late_line, late_other), (own_rows, late_own, results) = gather_line(late_line, (own_rows, late_own, results))
    sums = vmem_call(
        home_rows_kernel,
        (((EARLY + LATE + 16, D), bf16),),
        (),
        (early_own, late_own, attn_gain, mlp_gain_rows, query_gain, key_gain),
        10**6,
        bytes_accessed=2**20,
        limit=8,
    )[0]
    line_gram = vmem_call(line_gram_kernel, (((D, D), f32),), (), (is_late, late_line), 2 * 2**30, 1, limit=16)[0]
    sums = trade(sums, home)
    line_gram, late_other, sums = lax.optimization_barrier((line_gram, late_other, sums))
    home_all = lax.all_gather(sums, ("xl", "y", "c"), axis=0)
    results = trade(results, home)
    orth = newton_schulz(is_late, early_gram, line_gram, own_rows, late_other)

    mine = (jnp.arange(2) == c)[:, None, None, None]
    sent = jnp.where(mine, orth.reshape(1, REPLICAS, PIECE, D), 0).reshape(2 * REPLICAS, PIECE, D)
    pieces = lax.all_to_all(sent, ("xh", "xl", "y", "c"), 0, 0)

    output = results[:BLOCK]
    input_grad = jnp.where(home, input_grad, results[BLOCK : 2 * BLOCK].astype(f32))
    gain_all = home_all[:, EARLY + LATE :].astype(f32)
    gain_sum = jnp.sum(gain_all[:, :3] + gain_all[:, 8:11], axis=0)
    for axis, step, size in (("z", 1, 4), ("z", 2, 4), ("xh", 1, 2)):
        gain_sum = gain_sum + lax.ppermute(gain_sum, axis, [(i, i ^ step) for i in range(size)])
    gain_grad = gain_sum.reshape(3 * D)[: 2 * D + 2 * HD]
    new_first = adam_first * gain_first + (1.0 - adam_first) * gain_grad
    new_second = adam_second * gain_second + (1.0 - adam_second) * gain_grad * gain_grad
    step_first = new_first / (1.0 - adam_first**STEP)
    step_second = new_second / (1.0 - adam_second**STEP)
    new_gains = gains - gain_rate * step_first / (jnp.sqrt(step_second) + adam_epsilon)
    new_moments = vmem_call(
        momentum_kernel,
        tuple((m.shape, f32) for m in moments),
        ((home_all.shape, bf16),),
        (home_all,),
        10**6,
        0,
        14 * 2**20,
        fetched=1,
    )
    pieces, new_moments, new_gains = lax.optimization_barrier((pieces, new_moments, new_gains))
    new_weights = vmem_call(
        weight_kernel,
        tuple((part.shape, f32) for part in own_parts),
        (),
        (xh.astype(jnp.int32).reshape(1), pieces, *own_parts),
        10**6,
        1,
        4 * 2**20,
    )
    new_weights = [w if i in SPLIT_FIRST else w.T for i, w in enumerate(new_weights)]
    return (output, input_grad, new_first, new_second, new_gains, *new_moments, *new_weights)


def solution(mesh):
    fine = Mesh(mesh.devices.reshape(2, 4, 2, 4, 2), ("xh", "z", "xl", "y", "c"))
    shard = ("xh", "z")
    replica = ("xl", "y", "c")
    rows = P(replica + shard, None)
    split = tuple(P(shard, None) if i in SPLIT_FIRST else P(None, shard) for i in range(7))
    pieces = tuple(
        P(shard + replica, None) if i in SPLIT_FIRST else P(None, shard + replica) for i in range(7)
    )
    in_specs = (rows, rows, P(replica, None), P(), P(), P()) + split + split
    out_specs = (rows, rows, P(), P(), P()) + split + pieces
    return jax.shard_map(shards, mesh=fine, in_specs=in_specs, out_specs=out_specs, check_vma=False)
```

```python
import math

import jax
import jax.numpy as jnp
from jax import lax
from jax.experimental import pallas as pl
from jax.experimental.pallas import tpu as pltpu
from jax.sharding import Mesh, PartitionSpec as P

D = 1024
H = 16
KV = 8
HD = 128
FF = 3072
NS_ITERS = 5
STEP = 10

norm_epsilon = 1e-06
rotary_base = 1000000.0
momentum_decay = 0.95
poly_first = 3.4445
poly_second = -4.775
poly_third = 2.0315
orth_epsilon = 1e-07
update_rate = 0.5
weight_shrink = 0.002
adam_first = 0.9
adam_second = 0.999
adam_epsilon = 1e-08
gain_rate = 0.8

f32 = jnp.float32
bf16 = jnp.bfloat16

PLANE = ("xh", "xl", "y")
REPLICAS = 16
BLOCK = 128
TOKENS = 8 * BLOCK
EARLY = 96
LATE = 64
PIECE = 16
FIRST_PACK = ((0, 256), (256, 128), (384, 128), (512, 256))
SECOND_PACK = ((0, 384), (384, 384), (768, 384))
PACK_PLACES = tuple((False, *at) for at in FIRST_PACK) + tuple((True, *SECOND_PACK[i]) for i in (1, 2, 0))
SPLIT_FIRST = (3, 6)
FULL_SHAPES = ((D, H * HD), (D, KV * HD), (D, KV * HD), (H * HD, D), (D, FF), (D, FF), (FF, D))
SPREADS = (
    D ** (-0.5),
    D ** (-0.5),
    D ** (-0.5),
    max(H * HD // 256, 4) ** (-0.5),
    D ** (-0.5),
    D ** (-0.5),
    FF ** (-0.5),
)
RATES = tuple(update_rate * s * math.sqrt(max(f)) for s, f in zip(SPREADS, FULL_SHAPES))


def dot(a, b):
    return jnp.dot(a, b, preferred_element_type=f32)


def dot_t(a, b):
    return lax.dot_general(a, b, (((1,), (1,)), ((), ())), preferred_element_type=f32)


def t_dot(a, b):
    return lax.dot_general(a, b, (((0,), (0,)), ((), ())), preferred_element_type=f32)


def vmem_call(kernel, outs, scratch, operands, flops, scalars=0, bytes_accessed=8 * 2**20, limit=16, fetched=0, stored=0):
    vmem, smem, anywhere = (pl.BlockSpec(memory_space=m) for m in (pltpu.VMEM, pltpu.SMEM, pl.ANY))
    scratch_shapes = [pltpu.VMEM(shape, dtype) for shape, dtype in scratch]
    if fetched + stored:
        scratch_shapes.append(pltpu.SemaphoreType.DMA((fetched + stored,)))
    return pl.pallas_call(
        kernel,
        out_shape=tuple(jax.ShapeDtypeStruct(shape, dtype) for shape, dtype in outs),
        in_specs=[smem] * scalars + [vmem] * (len(operands) - scalars - fetched) + [anywhere] * fetched,
        out_specs=(vmem,) * (len(outs) - stored) + (anywhere,) * stored,
        scratch_shapes=scratch_shapes,
        compiler_params=pltpu.CompilerParams(vmem_limit_bytes=limit * 2**20),
        cost_estimate=pl.CostEstimate(flops=flops, bytes_accessed=bytes_accessed, transcendentals=0),
    )(*operands)


def fetch(sources, targets, sems, first=0):
    copies = [
        pltpu.make_async_copy(source, target, sems.at[first + i])
        for i, (source, target) in enumerate(zip(sources, targets))
    ]
    for copy in copies:
        copy.start()
    return copies


def wait(copies):
    for copy in copies:
        copy.wait()


def trade(x, home):
    other = lax.ppermute(x, ("xh", "c"), [(1, 2), (2, 1)])
    return jnp.where(home, x, other)


def trade_copied(x, home):
    other = lax.ppermute(x, ("xh", "c"), [(0, 2), (3, 1)])
    return jnp.where(home, x, other)


def over_z(x, k):
    return lax.ppermute(x, "z", [(i, i ^ k) for i in range(4)])


def over_core(x):
    return lax.ppermute(x, "c", [(0, 1), (1, 0)])


def gather_line(block, beside=()):
    near, far, across = (over_z(block, k) for k in (1, 3, 2))
    line = jnp.concatenate([block, near, across, far], axis=0)
    line, beside = lax.optimization_barrier((line, beside))
    return (line, over_core(line)), beside


def scatter_over_z(half):
    sent = half.astype(bf16)
    parts = [over_z(sent[k * BLOCK : (k + 1) * BLOCK], k) for k in (1, 3, 2)]
    return half[:BLOCK] + sum(part.astype(f32) for part in parts)


def rms_scale(values):
    return lax.rsqrt(jnp.mean(values * values, axis=-1, keepdims=True) + norm_epsilon)


def rotary_tables(position, head_width):
    half_width = head_width // 2
    freq_steps = jnp.arange(half_width, dtype=f32)
    inverse = rotary_base ** (-2.0 * freq_steps / head_width)
    angles = inverse[:, None] * position.astype(f32)[None, :]
    return (jnp.cos(angles), jnp.sin(angles))


def stream_layout(lengths_row, stream_rows):
    ends_at = jnp.cumsum(lengths_row)
    places = jnp.arange(stream_rows, dtype=jnp.int32)
    passed = (places[:, None] >= ends_at[None, :]).astype(jnp.int32)
    start = jnp.sum(passed * lengths_row[None, :], axis=1)
    return (start, places - start)


def norm_back(upstream, values, scale, gain):
    weighted = upstream * gain
    inner = jnp.mean(weighted * values, axis=-1, keepdims=True)
    grad_values = scale * (weighted - values * scale * scale * inner)
    return (grad_values, upstream * values * scale)


def pack_kernel(scale_ref, *refs):
    sources, (first_ref, second_ref), targets, sems = refs[:7], refs[7:9], refs[9:16], refs[16]
    copies = fetch(sources, targets, sems)
    scale = scale_ref[0]
    for i, (is_second, at, count) in enumerate(PACK_PLACES):
        copies[i].wait()
        values = targets[i][...] * scale
        out_ref = second_ref if is_second else first_ref
        out_ref[at : at + count, :] = (values if i in SPLIT_FIRST else values.T).astype(bf16)


def pack(matrices, scale):
    return vmem_call(
        pack_kernel,
        (((768, D), bf16), ((1152, D), bf16)),
        tuple((m.shape, f32) for m in matrices),
        (jnp.asarray(scale, f32).reshape(1), *matrices),
        10**6,
        1,
        12 * 2**20,
        20,
        7,
    )


def pack_weights_kernel(place_ref, *refs):
    sources, (first_ref, second_ref), own_refs = refs[:7], refs[7:9], refs[9:16]
    targets, turned, sems = refs[16:23], refs[23], refs[24]
    copies = fetch(sources, targets, sems)
    place = place_ref[0]
    for i, (is_second, at, count) in enumerate(PACK_PLACES):
        copies[i].wait()
        values = targets[i]
        if i not in SPLIT_FIRST:
            turned[:count, :] = values[...].T
            values = turned
        out_ref = second_ref if is_second else first_ref
        out_ref[at : at + count, :] = values[:count, :].astype(bf16)
        per = count // REPLICAS
        own_refs[i][...] = values[pl.ds(pl.multiple_of(place * per, 8), per), :] * (1.0 - weight_shrink)


def pack_weights(matrices, place):
    own = tuple(((count // REPLICAS, D), f32) for _, _, count in PACK_PLACES)
    first, second, *own = vmem_call(
        pack_weights_kernel,
        (((768, D), bf16), ((1152, D), bf16), *own),
        (*((m.shape, f32) for m in matrices), ((384, D), f32)),
        (place.astype(jnp.int32).reshape(1), *matrices),
        10**6,
        1,
        12 * 2**20,
        20,
        7,
    )
    return first, second, own


def turn(values, cosine, sine):
    front, back = values[: HD // 2], values[HD // 2 :]
    return jnp.concatenate([front * cosine - back * sine, back * cosine + front * sine], axis=0)


def column_scale(values):
    return lax.rsqrt(jnp.mean(values * values, axis=0, keepdims=True) + norm_epsilon)


def block_mask(start_ref, at, count, keys):
    key = lax.broadcasted_iota(jnp.int32, (keys, count), 0)
    token = at + lax.broadcasted_iota(jnp.int32, (keys, count), 1)
    allowed = (key >= start_ref[:, at : at + count]) & (key <= token)
    return jnp.concatenate([allowed, allowed], axis=1)


def both_heads(ref, at, count):
    return jnp.concatenate([ref[:HD, at : at + count], ref[HD : 2 * HD, at : at + count]], axis=1)


def as_column(ref):
    eye = lax.broadcasted_iota(jnp.int32, (HD, HD), 0) == lax.broadcasted_iota(jnp.int32, (HD, HD), 1)
    return jnp.sum(jnp.where(eye, ref[...], 0.0), axis=1, keepdims=True)


def in_order(order_ref, block):
    return pl.ds(pl.multiple_of(order_ref[block] * BLOCK, BLOCK), BLOCK)


def attention_kernel(order_ref, cosine_ref, sine_ref, start_ref, gain_query_ref, gain_key_ref, weight_ref, *refs):
    lines = refs[:2]
    query_ref, key_t_ref, key_ref, value_ref, log_ref, away_ref, kept_ref, pre_ref, attended_ref, normed = refs[2:12]
    value_t, attn = refs[12:]
    for i in range(8):
        normed[in_order(order_ref, i), :] = lines[i // 4][i % 4 * BLOCK : (i % 4 + 1) * BLOCK, :]
    pre_ref[...] = dot_t(weight_ref[: 4 * HD, :], normed[...])
    cosine, sine = cosine_ref[...], sine_ref[...]
    for head in range(3):
        values = pre_ref[head * HD : (head + 1) * HD, :]
        gain = as_column(gain_query_ref if head < 2 else gain_key_ref)
        turned_low = turn(values * column_scale(values) * gain, cosine, sine).astype(bf16)
        if head < 2:
            query_ref[head * HD : (head + 1) * HD, :] = turned_low
        else:
            key_t_ref[...] = turned_low
            key_ref[...] = turned_low.T
    low = pre_ref[3 * HD :, :].astype(bf16)
    value_t[...] = low
    value_ref[...] = low.T
    count = 2 * BLOCK
    for at in range(0, TOKENS, count):
        keys = at + count
        scores = dot(key_ref[:keys, :], both_heads(query_ref, at, count)) * HD ** (-0.5)
        masked = jnp.where(block_mask(start_ref, at, count, keys), scores, -1e30)
        peak = jnp.max(masked, axis=0, keepdims=True)
        raised = jnp.exp(masked - peak)
        total = jnp.sum(raised, axis=0, keepdims=True)
        probs = (raised * (1.0 / total)).astype(bf16)
        attended = dot(value_t[:, :keys], probs)
        log_total = peak + jnp.log(total)
        for head in range(2):
            span = slice(head * count, (head + 1) * count)
            attended_ref[head * HD : (head + 1) * HD, at:keys] = attended[:, span]
            log_ref[head : head + 1, at:keys] = log_total[:, span]
    for i in range(8):
        attn[:, i * BLOCK : (i + 1) * BLOCK] = attended_ref[:, in_order(order_ref, i)].astype(bf16)
    away_ref[...] = t_dot(attn[:, TOKENS // 2 :], weight_ref[4 * HD :, :]).astype(bf16)
    kept_ref[...] = t_dot(attn[:, : TOKENS // 2], weight_ref[4 * HD :, :])


def attention(order, tables, weight, lines):
    outs = (
        ((2 * HD, TOKENS), bf16),
        ((HD, TOKENS), bf16),
        ((TOKENS, HD), bf16),
        ((TOKENS, HD), bf16),
        ((2, TOKENS), f32),
        ((TOKENS // 2, D), bf16),
        ((TOKENS // 2, D), f32),
        ((4 * HD, TOKENS), f32),
        ((2 * HD, TOKENS), f32),
        ((TOKENS, D), bf16),
    )
    scratch = (((HD, TOKENS), bf16), ((2 * HD, TOKENS), bf16))
    operands = (order, *tables, weight, *lines)
    return vmem_call(attention_kernel, outs, scratch, operands, 3 * 10**9, 1)


def norm_back_columns(upstream, values, gain):
    scale = column_scale(values)
    weighted = upstream * gain
    inner = jnp.mean(weighted * values, axis=0, keepdims=True)
    grad = scale * (weighted - values * (scale * scale * inner))
    return grad, jnp.sum(upstream * values * scale, axis=1, keepdims=True)


def attention_back_kernel(order_ref, cosine_ref, sine_ref, start_ref, gain_query_ref, gain_key_ref,
                          query_ref, key_t_ref, key_ref, value_ref, log_ref, gain_attn_ref, weight_ref, *refs):
    lines, (attended_hbm, pre_hbm, normed_hbm, momentum_hbm) = refs[:2], refs[2:6]
    away_ref, kept_ref, late_ref, query_gain_ref, key_gain_ref, attn_gain_ref = refs[6:12]
    dquery, dkey, dvalue, dattn_ref, dpre, dpre_blocks, dbranch = refs[12:19]
    attended_ref, pre_ref, normed, momentum_ref, sems = refs[19:]
    copies = fetch(
        (attended_hbm, pre_hbm, normed_hbm, momentum_hbm), (attended_ref, pre_ref, normed, momentum_ref), sems
    )
    for i in range(8):
        dbranch[in_order(order_ref, i), :] = lines[i // 4][i % 4 * BLOCK : (i % 4 + 1) * BLOCK, :]
    dattn_ref[...] = dot_t(weight_ref[4 * HD :, :], dbranch[...]).astype(bf16)
    copies[0].wait()
    dkey[...] = jnp.zeros_like(dkey)
    dvalue[...] = jnp.zeros_like(dvalue)
    count = 2 * BLOCK
    for at in range(0, TOKENS, count):
        keys = at + count
        query = both_heads(query_ref, at, count)
        dattn = both_heads(dattn_ref, at, count)
        row_dot = jnp.sum(dattn.astype(f32) * both_heads(attended_ref, at, count), axis=0, keepdims=True)
        log_total = jnp.concatenate([log_ref[:1, at:keys], log_ref[1:, at:keys]], axis=1)
        scores = dot(key_ref[:keys, :], query) * HD ** (-0.5)
        allowed = block_mask(start_ref, at, count, keys)
        probs = jnp.where(allowed, jnp.exp(scores - log_total), 0.0)
        dprobs = dot(value_ref[:keys, :], dattn)
        dscores = (probs * (dprobs - row_dot)).astype(bf16)
        grad = dot(key_t_ref[:, :keys], dscores)
        for head in range(2):
            dquery[head * HD : (head + 1) * HD, at:keys] = grad[:, head * count : (head + 1) * count]
        dkey[:, :keys] += dot_t(query, dscores)
        dvalue[:, :keys] += dot_t(dattn, probs.astype(bf16))
    wait(copies[1:])
    cosine, sine = cosine_ref[...], sine_ref[...]
    query_gain = jnp.zeros_like(query_gain_ref)
    for head in range(3):
        span = slice(head * HD, (head + 1) * HD)
        upstream = (dquery[span, :] if head < 2 else dkey[...]) * HD ** (-0.5)
        gain = as_column(gain_query_ref if head < 2 else gain_key_ref)
        grad, gain_part = norm_back_columns(turn(upstream, cosine, -sine), pre_ref[span, :], gain)
        dpre[span, :] = grad.astype(bf16)
        if head < 2:
            query_gain = query_gain + gain_part
        else:
            key_gain_ref[...] = gain_part
    query_gain_ref[...] = query_gain
    dpre[3 * HD :, :] = dvalue[...].astype(bf16)
    for i in range(8):
        dpre_blocks[:, i * BLOCK : (i + 1) * BLOCK] = dpre[:, in_order(order_ref, i)]
    away_ref[...] = t_dot(dpre_blocks[:, TOKENS // 2 :], weight_ref[: 4 * HD, :]).astype(bf16)
    kept_ref[...] = t_dot(dpre_blocks[:, : TOKENS // 2], weight_ref[: 4 * HD, :])
    grads = dot(dpre[...], normed[...])
    weighted = weight_ref[: 4 * HD, :].astype(f32) * grads
    attn_gain_ref[...] = jnp.sum(weighted, axis=0, keepdims=True) / gain_attn_ref[...]
    grads = grads + momentum_ref[: 4 * HD, :].astype(f32)
    late_ref[:256, :] = grads[:256].astype(bf16)
    late_ref[256:768, :] = jnp.zeros((512, D), bf16)
    for i in range(4):
        late_ref[256 + 64 * i : 288 + 64 * i, :] = grads[256 + 32 * i : 288 + 32 * i].astype(bf16)
        late_ref[512 + 64 * i : 544 + 64 * i, :] = grads[384 + 32 * i : 416 + 32 * i].astype(bf16)
    out_grad = dot(attended_ref[...].astype(bf16), dbranch[...])
    late_ref[768:, :] = (out_grad + momentum_ref[4 * HD :, :].astype(f32)).astype(bf16)


def attention_back(order, tables, gain_attn, weight, kept, momentum, dbranch):
    pre, query, key_t, key, value, attended, log_total, normed = kept
    outs = (
        ((TOKENS // 2, D), bf16),
        ((TOKENS // 2, D), f32),
        ((REPLICAS * LATE, D), bf16),
        ((HD, 1), f32),
        ((HD, 1), f32),
        ((1, D), f32),
    )
    scratch = (
        ((2 * HD, TOKENS), f32),
        ((HD, TOKENS), f32),
        ((HD, TOKENS), f32),
        ((2 * HD, TOKENS), bf16),
        ((4 * HD, TOKENS), bf16),
        ((4 * HD, TOKENS), bf16),
        ((TOKENS, D), bf16),
        (attended.shape, f32),
        (pre.shape, f32),
        (normed.shape, bf16),
        (momentum.shape, bf16),
    )
    operands = (
        *(order, *tables, query, key_t, key, value, log_total, gain_attn, weight),
        *(*dbranch, attended, pre, normed, momentum),
    )
    return vmem_call(attention_back_kernel, outs, scratch, operands, 6 * 10**9, 1, limit=20, fetched=4)


def feed_forward_kernel(home_ref, line_ref, other_ref, cot_line_ref, cot_other_ref, own_hbm, traded_hbm,
                        hidden_ref, grads_ref, away_ref, kept_ref, out_away_ref, out_kept_ref, normed, cot,
                        weight_ref, sems):
    @pl.when(home_ref[0] == 1)
    def _():
        pltpu.make_async_copy(own_hbm, weight_ref, sems.at[0]).start()

    @pl.when(home_ref[0] == 0)
    def _():
        pltpu.make_async_copy(traded_hbm, weight_ref, sems.at[0]).start()

    normed[: TOKENS // 2, :] = line_ref[...]
    normed[TOKENS // 2 :, :] = other_ref[...]
    cot[: TOKENS // 2, :] = cot_line_ref[...]
    cot[TOKENS // 2 :, :] = cot_other_ref[...]
    pltpu.make_async_copy(own_hbm, weight_ref, sems.at[0]).wait()
    width = SECOND_PACK[0][1]
    for part, out_ref, result_ref in ((1, away_ref, out_away_ref), (0, kept_ref, out_kept_ref)):
        span = slice(part * TOKENS // 2, (part + 1) * TOKENS // 2)
        both = dot_t(normed[span, :], weight_ref[width:, :])
        dhidden = dot_t(cot[span, :], weight_ref[:width, :])
        gate, upward = both[:, :width], both[:, width:]
        sigmoid_gate = jax.nn.sigmoid(gate)
        activated = gate * sigmoid_gate
        hidden_ref[span, :] = (activated * upward).astype(bf16)
        dgate = dhidden * upward * sigmoid_gate * (1.0 + gate * (1.0 - sigmoid_gate))
        grads_ref[span, :width] = dgate.astype(bf16)
        grads_ref[span, width:] = (dhidden * activated).astype(bf16)
        out_ref[...] = dot(grads_ref[span, :], weight_ref[width:, :]).astype(out_ref.dtype)
        result_ref[...] = dot(hidden_ref[span, :], weight_ref[:width, :]).astype(result_ref.dtype)


def feed_forward(home, normed, cot, own_weight, traded_weight):
    half = (TOKENS // 2, D)
    outs = (
        ((TOKENS, 384), bf16),
        ((TOKENS, 768), bf16),
        (half, bf16),
        (half, f32),
        (half, bf16),
        (half, f32),
        ((TOKENS, D), bf16),
        ((TOKENS, D), bf16),
    )
    operands = (home.astype(jnp.int32).reshape(1), *normed, *cot, own_weight, traded_weight)
    scratch = ((own_weight.shape, bf16),)
    return vmem_call(feed_forward_kernel, outs, scratch, operands, 5 * 10**9, 1, fetched=2)


def early_kernel(hidden_ref, grads_ref, momentum_ref, normed, cot, out_ref):
    out_ref[:768, :] = (t_dot(grads_ref[...], normed[...]) + momentum_ref[384:, :].astype(f32)).astype(bf16)
    out_ref[768:1152, :] = (t_dot(hidden_ref[...], cot[...]) + momentum_ref[:384, :].astype(f32)).astype(bf16)
    out_ref[1152:, :] = jnp.zeros((384, D), bf16)


def early_gradients(*operands):
    return vmem_call(early_kernel, (((REPLICAS * EARLY, D), bf16),), (), operands, 3 * 10**9)[0]


def gram_kernel(rows_ref, out_hbm, gram, sems):
    gram[...] = t_dot(rows_ref[...], rows_ref[...])
    wait(fetch((gram,), (out_hbm,), sems))


def line_gram_kernel(late_ref, line_ref, out_ref):
    @pl.when(late_ref[0] == 1)
    def _():
        out_ref[...] = t_dot(line_ref[...], line_ref[...])


def newton_schulz_kernel(late_ref, rows_ref, line_gram_ref, other_ref, early_hbm,
                         out_ref, full, low, rest, once, rows, sems):
    @pl.when(late_ref[0] == 0)
    def _():
        wait(fetch((early_hbm,), (full,), sems))

    @pl.when(late_ref[0] == 1)
    def _():
        full[...] = line_gram_ref[...] + t_dot(other_ref[...], other_ref[...])

    eye = lax.broadcasted_iota(jnp.int32, (128, 128), 0) == lax.broadcasted_iota(jnp.int32, (128, 128), 1)
    diagonal = jnp.zeros((128, 128), f32)
    for i in range(D // 128):
        span = slice(i * 128, (i + 1) * 128)
        diagonal = diagonal + jnp.where(eye, full[span, span], 0.0)
    total = jnp.sum(diagonal, axis=(0, 1), keepdims=True) + orth_epsilon
    inverse = lax.rsqrt(total)
    scaled = full[...] * (inverse * inverse)
    full[...] = scaled
    low[...] = scaled.astype(bf16)
    rows[...] = rows_ref[...].astype(f32) * inverse
    for iteration in range(NS_ITERS):
        rest[...] = (poly_second * full[...] + poly_third * dot(low[...], low[...])).astype(bf16)
        rows[...] = poly_first * rows[...] + dot(rows[...].astype(bf16), rest[...])
        if iteration + 1 < NS_ITERS:
            value = poly_first * full[...] + dot(rest[...], low[...])
            full[...] = value
            once[...] = value.astype(bf16)
            value = poly_first * full[...] + dot(rest[...], once[...])
            full[...] = value
            low[...] = value.astype(bf16)
    out_ref[...] = rows[...].astype(bf16)


def newton_schulz(is_late, early_gram, line_gram, rows, late_rows):
    count = rows.shape[0]
    scratch = (
        ((D, D), f32),
        ((D, D), bf16),
        ((D, D), bf16),
        ((D, D), bf16),
        ((count, D), f32),
    )
    operands = (is_late, rows, line_gram, late_rows, early_gram)
    flops = 15 * 2 * D**3 + 10 * count * D * D
    return vmem_call(newton_schulz_kernel, (((count, D), bf16),), scratch, operands, flops, 1, limit=20, fetched=1)[0]


def home_rows_kernel(early_ref, late_ref, attn_ref, mlp_ref, query_ref, key_ref, out_ref):
    out_ref[:EARLY, :] = early_ref[...]
    out_ref[EARLY : EARLY + LATE, :] = late_ref[...]
    eye = lax.broadcasted_iota(jnp.int32, (HD, HD), 0) == lax.broadcasted_iota(jnp.int32, (HD, HD), 1)
    heads = [jnp.sum(jnp.where(eye, ref[...], 0.0), axis=0, keepdims=True) for ref in (query_ref, key_ref)]
    rows = jnp.concatenate(
        [
            attn_ref[...],
            jnp.sum(mlp_ref[...], axis=0, keepdims=True),
            jnp.concatenate([*heads, jnp.zeros((1, D - 2 * HD), f32)], axis=1),
            jnp.zeros((5, D), f32),
        ],
        axis=0,
    )
    high = rows.astype(bf16).astype(f32)
    out_ref[EARLY + LATE :, :] = jnp.concatenate([high, rows - high], axis=0).astype(bf16)


def momentum_kernel(all_hbm, q, k, v, o, g, u, d, all_ref, sems):
    wait(fetch((all_hbm,), (all_ref,), sems))

    def rows(column, at, count):
        entries = [(column % 2 * 4 + y) * 2 + column // 2 for y in range(4)]
        return jnp.concatenate([all_ref[entry, at : at + count, :] for entry in entries], axis=0).astype(f32)

    q[...] = rows(0, EARLY, 64).T
    k[...] = rows(1, EARLY, 32).T
    v[...] = rows(2, EARLY, 32).T
    o[...] = rows(3, EARLY, 64)
    g[...] = rows(0, 0, EARLY).T
    u[...] = rows(1, 0, EARLY).T
    d[...] = rows(2, 0, EARLY)


def weight_kernel(half_ref, pieces_ref, *refs):
    kept, outs = refs[:7], refs[7:]
    half = half_ref[0]

    def rows(column, ys, count):
        return jnp.concatenate(
            [pieces_ref[column * 8 + y * 2 + half][:count, :] for y in ys], axis=0
        ).astype(f32)

    late, early = (3,), (0, 1, 2)
    updates = (
        rows(0, late, 16),
        rows(1, late, 8),
        rows(2, late, 8),
        rows(3, late, 16),
        rows(0, early, 8),
        rows(1, early, 8),
        rows(2, early, 8),
    )
    for i in range(7):
        outs[i][...] = kept[i][...] - RATES[i] * updates[i]


def pad_rows(rows, count):
    return jnp.pad(rows, ((0, 0), (0, count - rows.shape[1]), (0, 0)))


def shards(tokens, cotangent, lengths, gains, gain_first, gain_second, *matrices):
    weights, moments = matrices[:7], matrices[7:]
    xh, z, xl, y, c = (lax.axis_index(a) for a in ("xh", "z", "xl", "y", "c"))
    home = xh == c
    gain_attn = gains[:D]
    gain_mlp = gains[D : 2 * D]
    gain_query = gains[2 * D : 2 * D + HD]
    gain_key = gains[2 * D + HD :]
    order = jnp.stack([(c ^ (i // 4)) * 4 + (z ^ (i % 4)) for i in range(8)]).astype(jnp.int32)

    codes = jnp.concatenate([lengths[0] // 32, lengths[0] % 32]).astype(bf16)
    codes = jnp.pad(codes[None], ((0, 15), (0, D - codes.shape[0])))
    first_weights, second_weights, own_parts = pack_weights(weights, xl * 8 + y * 2 + c)
    arrived = trade(jnp.concatenate([tokens, cotangent, codes], axis=0), home)
    arrived, first_weights, moments = lax.optimization_barrier((arrived, first_weights, moments))
    inputs = arrived[:BLOCK].astype(f32)
    scale_one = rms_scale(inputs)
    own_normed = (inputs * scale_one * gain_attn).astype(bf16)
    cot_own = arrived[BLOCK : 2 * BLOCK]
    codes = arrived[2 * BLOCK, :12].astype(jnp.int32)
    start, position = stream_layout(codes[:6] * 32 + codes[6:], TOKENS)
    first_weights = trade_copied(first_weights, home)
    tables = (*rotary_tables(position, HD), start[None, :], gain_query[None, :], gain_key[None, :])
    momenta = pack(moments, jnp.where(home, momentum_decay / 8, 0.0))
    both = jnp.concatenate([own_normed, cot_own], axis=0)
    near, far, across = (over_z(both, k) for k in (1, 3, 2))
    parts = (both, near, across, far)
    line = jnp.concatenate([part[:BLOCK] for part in parts], axis=0)
    cot_line = jnp.concatenate([part[BLOCK:] for part in parts], axis=0)
    line, cot_line, first_weights, tables, second_weights, momenta = lax.optimization_barrier(
        (line, cot_line, first_weights, tables, second_weights, momenta)
    )
    first_momentum, second_momentum = momenta

    traded_weights = lax.ppermute(second_weights, ("xh", "c"), [(0, 2), (3, 1)])
    query_use, key_t, key_use, value_use, log_total, away, kept, pre, attended, normed = attention(
        order, tables, first_weights, (line, over_core(line))
    )
    cot = (cot_line, over_core(cot_line))
    half = kept + over_core(away).astype(f32)
    middle = inputs + scatter_over_z(half)

    scale_two = rms_scale(middle)
    normed_two, _ = gather_line((middle * scale_two * gain_mlp).astype(bf16))
    hidden, grads, away, kept, out_away, out_half, normed_two, cot = feed_forward(
        home, normed_two, cot, second_weights, traded_weights
    )
    early = early_gradients(hidden, grads, second_momentum, normed_two, cot)
    half, early = lax.optimization_barrier((kept + over_core(away).astype(f32), early))
    early_parts = lax.all_to_all(early.reshape(REPLICAS, EARLY, D), PLANE, 0, 0)
    dnormed_two = scatter_over_z(half)
    dmiddle_norm, mlp_gain_rows = norm_back(dnormed_two, middle, scale_two, gain_mlp)
    dmiddle = cot_own.astype(f32) + dmiddle_norm
    dbranch, early_own = gather_line(
        dmiddle.astype(bf16), jnp.sum(early_parts.astype(f32), axis=0).astype(bf16)
    )
    early_all = lax.all_gather(early_own, ("y", "c", "z"), axis=0, tiled=True)

    away, kept, late, query_gain, key_gain, attn_gain = attention_back(
        order,
        tables,
        gain_attn[None, :],
        first_weights,
        (pre, query_use, key_t, key_use, value_use, attended, log_total, normed),
        first_momentum,
        dbranch,
    )
    late_parts = lax.all_to_all(late.reshape(REPLICAS, LATE, D), PLANE, 0, 0)
    half, out_away, out_half, mlp_gain_rows, attn_gain, query_gain, key_gain = lax.optimization_barrier(
        (kept + over_core(away).astype(f32), out_away, out_half, mlp_gain_rows, attn_gain, query_gain, key_gain)
    )
    dnormed = scatter_over_z(half)
    branch_out = scatter_over_z(out_half + over_core(out_away).astype(f32))
    late_parts, dnormed, branch_out = lax.optimization_barrier((late_parts, dnormed, branch_out))
    late_own = jnp.sum(late_parts.astype(f32), axis=0).astype(bf16)

    output = middle + branch_out
    dinput_norm, _ = norm_back(dnormed, inputs, scale_one, gain_attn)
    input_grad = dmiddle + dinput_norm
    by_y = [late_own] + [lax.ppermute(late_own, "y", [(i, i ^ k) for i in range(4)]) for k in (3, 2, 1)]
    early_gram = vmem_call(
        gram_kernel, (((D, D), f32),), (((D, D), f32),), (early_all,), 6 * 2**30, limit=24, stored=1
    )[0]
    early_rows = lax.dynamic_index_in_dim(early_all.reshape(4, 8, EARLY, D), c * 4 + z, 1, False)
    early_rows = early_rows.reshape(REPLICAS, 3, 8, D)
    early_rows = pad_rows(lax.dynamic_index_in_dim(early_rows, jnp.minimum(y, 2), 1, False), PIECE)
    by_y, early_gram, early_rows = lax.optimization_barrier((by_y, early_gram, early_rows))
    late_line = jnp.concatenate(by_y, axis=0)

    x_plane = xh * 2 + xl
    late_rows = jnp.stack([by_y[1], by_y[2], by_y[3], by_y[0]], axis=0)
    late_rows = jnp.where(
        (x_plane == 0) | (x_plane == 3),
        late_rows.reshape(REPLICAS, PIECE, D),
        pad_rows(late_rows[:, :32].reshape(REPLICAS, 8, D), PIECE),
    )
    own_rows = jnp.where(y == 3, late_rows, early_rows).reshape(REPLICAS * PIECE, D)
    is_late = (y == 3).astype(jnp.int32).reshape(1)
    results = jnp.concatenate([output.astype(bf16), input_grad.astype(bf16)], axis=0)
    (late_line, late_other), (own_rows, late_own, results) = gather_line(late_line, (own_rows, late_own, results))
    sums = vmem_call(
        home_rows_kernel,
        (((EARLY + LATE + 16, D), bf16),),
        (),
        (early_own, late_own, attn_gain, mlp_gain_rows, query_gain, key_gain),
        10**6,
        bytes_accessed=2**20,
        limit=8,
    )[0]
    line_gram = vmem_call(line_gram_kernel, (((D, D), f32),), (), (is_late, late_line), 2 * 2**30, 1, limit=16)[0]
    sums = trade(sums, home)
    line_gram, late_other, sums = lax.optimization_barrier((line_gram, late_other, sums))
    home_all = lax.all_gather(sums, ("xl", "y", "c"), axis=0)
    results = trade(results, home)
    orth = newton_schulz(is_late, early_gram, line_gram, own_rows, late_other)

    mine = (jnp.arange(2) == c)[:, None, None, None]
    sent = jnp.where(mine, orth.reshape(1, REPLICAS, PIECE, D), 0).reshape(2 * REPLICAS, PIECE, D)
    pieces = lax.all_to_all(sent, ("xh", "xl", "y", "c"), 0, 0)

    output = results[:BLOCK]
    input_grad = jnp.where(home, input_grad, results[BLOCK : 2 * BLOCK].astype(f32))
    gain_all = home_all[:, EARLY + LATE :].astype(f32)
    gain_sum = jnp.sum(gain_all[:, :3] + gain_all[:, 8:11], axis=0)
    for axis, step, size in (("z", 1, 4), ("z", 2, 4), ("xh", 1, 2)):
        gain_sum = gain_sum + lax.ppermute(gain_sum, axis, [(i, i ^ step) for i in range(size)])
    gain_grad = gain_sum.reshape(3 * D)[: 2 * D + 2 * HD]
    new_first = adam_first * gain_first + (1.0 - adam_first) * gain_grad
    new_second = adam_second * gain_second + (1.0 - adam_second) * gain_grad * gain_grad
    step_first = new_first / (1.0 - adam_first**STEP)
    step_second = new_second / (1.0 - adam_second**STEP)
    new_gains = gains - gain_rate * step_first / (jnp.sqrt(step_second) + adam_epsilon)
    new_moments = vmem_call(
        momentum_kernel,
        tuple((m.shape, f32) for m in moments),
        ((home_all.shape, bf16),),
        (home_all,),
        10**6,
        0,
        14 * 2**20,
        fetched=1,
    )
    pieces, new_moments, new_gains = lax.optimization_barrier((pieces, new_moments, new_gains))
    new_weights = vmem_call(
        weight_kernel,
        tuple((part.shape, f32) for part in own_parts),
        (),
        (xh.astype(jnp.int32).reshape(1), pieces, *own_parts),
        10**6,
        1,
        4 * 2**20,
    )
    new_weights = [w if i in SPLIT_FIRST else w.T for i, w in enumerate(new_weights)]
    return (output, input_grad, new_first, new_second, new_gains, *new_moments, *new_weights)


def solution(mesh):
    fine = Mesh(mesh.devices.reshape(2, 4, 2, 4, 2), ("xh", "z", "xl", "y", "c"))
    shard = ("xh", "z")
    replica = ("xl", "y", "c")
    rows = P(replica + shard, None)
    split = tuple(P(shard, None) if i in SPLIT_FIRST else P(None, shard) for i in range(7))
    pieces = tuple(
        P(shard + replica, None) if i in SPLIT_FIRST else P(None, shard + replica) for i in range(7)
    )
    in_specs = (rows, rows, P(replica, None), P(), P(), P()) + split + split
    out_specs = (rows, rows, P(), P(), P()) + split + pieces
    return jax.shard_map(shards, mesh=fine, in_specs=in_specs, out_specs=out_specs, check_vma=False)
```
